32 devices in a mesh: pipe: 2 (over y), patch: 8 (over z, x), hour: 2 (over core).
Axes of the slice: x: 2, y: 2, z: 4, core: 2. Of those that a mesh axis runs over, the one named last changes fastest.
Arguments:
- inputs: bfloat16 [2, 128, 32, 512], P(None, 'patch', 'hour'), may hold values from -6 to 6
- visibility: int32 [2, 2], replicated, may hold values from 0 to 1, all different within a row
- norm_gains: float32 [2, 3, 512], P('pipe'), may hold values from 0.1 to 1.9
- scales: float32 [2, 2, 8], P('pipe'), may hold values from 2 to 12
- mixer_in: bfloat16 [2, 2, 512, 1536], P('pipe'), may hold values from -0.25 to 0.25
- mixer_out: bfloat16 [2, 2, 512, 512], P('pipe'), may hold values from -0.25 to 0.25
- expand_weight: bfloat16 [2, 512, 2048], P('pipe'), may hold values from -0.25 to 0.25
- reduce_weight: bfloat16 [2, 2048, 512], P('pipe'), may hold values from -0.125 to 0.125
Outputs:
- outputs: bfloat16 [2, 128, 32, 512], P(None, 'patch', 'hour')
The draws below stay inside these ranges and needn't reach their ends.
Inputs may be any that keep to these rules, and one draw needn't show every extreme that they name: `visibility`: row b lists 2 different key blocks of 64 patches for query block b; every block is listed in some row.
All inputs are finite; a program needn't handle non-finite values.
Results may differ from the reference program's by a relative error of at most 0.023.
Values may be sent and summed in bfloat16 or wider, within the bound.
No kernel may reach another device: no remote copies, remote signals or barrier semaphores. Data moves between devices by JAX's collectives and lax.ppermute only.
A program may use at most 64 MiB of HBM per device.

```python
import math
import jax
import jax.numpy as jnp
from jax import lax

D = 512
HEADS = 8
HEAD_DIM = 64
FF = 2048
PB = 64
KV = 2
MICRO = 2
P_SIZE = 128
H = 32
NB = 2


def block_scale(key, dims, cuts, low, high):
    loudness = 1.0
    for position, blocks in cuts:
        steps = jax.random.uniform(jax.random.fold_in(jax.random.fold_in(key, 6), position), (blocks,), jnp.float32, low / len(cuts), high / len(cuts))
        loudness = loudness * jnp.repeat(jnp.exp(steps), dims[position] // blocks).reshape((-1,) + (1,) * (len(dims) - 1 - position))
    return loudness


def different_ones(key, rows, number_of, top, lift):
    sequence = jax.random.permutation(jax.random.fold_in(key, 1), number_of)
    boost = sequence
    for power in range(3):
        boost = boost * boost // number_of
    boost = boost * lift // number_of
    tickets = jax.random.randint(jax.random.fold_in(key, 2), (rows, number_of), 0, 4096) + boost
    sure = jax.random.permutation(jax.random.fold_in(key, 3), rows)[jnp.arange(number_of) % rows]
    tickets = jnp.where(jnp.arange(rows)[:, None] == sure[None, :], 1 << 14, tickets)
    priority = tickets * number_of + jnp.arange(number_of)
    return lax.top_k(priority.astype(jnp.int32), top)[1].astype(jnp.int32)


def bell_draw(stream_key, extent, deviation, limit, split=(), held_as=jnp.bfloat16):
    entries = jax.random.normal(stream_key, extent, jnp.float32) * deviation
    if len(split) > 0:
        entries = block_scale(stream_key, extent, split, -0.22, 0.18) * entries
    return jnp.clip(entries, min=-limit, max=limit).astype(held_as)


def setup_inputs(seed: int = 0) -> dict:
    key_list = jax.random.split(jax.random.key(seed), 9)
    inputs = bell_draw(key_list[0], (MICRO, P_SIZE, H, D), 1.0, 6.0, ((1, 8), (2, 2)))
    visibility = different_ones(key_list[1], NB, NB, KV, 8192)
    norm_gains = jnp.clip(1.0 + 0.18 * jax.random.normal(key_list[2], (2, 3, D), jnp.float32), 0.1, 1.9)
    scales = jnp.clip(jnp.exp(math.log(12.0) - 1.7917595 * jax.random.uniform(key_list[3], (2, 2, HEADS), jnp.float32) ** block_scale(key_list[3], (2, 2, HEADS), ((0, 2),), -0.2, 0.2)), 2.0, 12.0)
    mixer_in = bell_draw(key_list[4], (2, 2, D, 3 * D), D ** -0.5, 0.25, ((0, 2),))
    mixer_out = bell_draw(key_list[5], (2, 2, D, D), D ** -0.5, 0.25, ((0, 2),))
    expand_weight = bell_draw(key_list[6], (2, D, FF), D ** -0.5, 0.25, ((0, 2),))
    reduce_weight = bell_draw(key_list[7], (2, FF, D), FF ** -0.5, 0.125, ((0, 2),))
    return dict(inputs=inputs, visibility=visibility, norm_gains=norm_gains, scales=scales, mixer_in=mixer_in, mixer_out=mixer_out, expand_weight=expand_weight, reduce_weight=reduce_weight)


def rms_norm(values, gain):
    values = values.astype(jnp.float32)
    factor = lax.rsqrt(lax.optimization_barrier(jnp.mean(values * values, axis=-1, keepdims=True)) + 1e-05)
    return (values * factor * gain).astype(jnp.bfloat16)

def head_norm(values):
    factor = lax.rsqrt(lax.optimization_barrier(jnp.mean(values * values, axis=-1, keepdims=True)) + 1e-06)
    return (values * factor).astype(jnp.bfloat16)

def split_heads(projected, lead_shape):
    width = projected.shape[-1] // 3
    shape = lead_shape + (HEADS, HEAD_DIM)
    queries = head_norm(projected[:, :width].reshape(shape))
    keys_all = head_norm(projected[:, width:2 * width].reshape(shape))
    values = projected[:, 2 * width:].astype(jnp.bfloat16).reshape(shape)
    return (queries, keys_all, values)

def softmax_weights(scores, scale):
    scaled = scores * (scale / HEAD_DIM)[:, None, None]
    powers = jnp.exp(scaled)
    return (powers / lax.optimization_barrier(jnp.sum(powers, axis=-1, keepdims=True))).astype(jnp.bfloat16)

def time_group(group, scale):
    queries, keys_all, values = group
    scores = jnp.einsum('pqnd,pknd->pnqk', queries.astype(jnp.float32), keys_all.astype(jnp.float32))
    weights = softmax_weights(scores, scale)
    mixed = jnp.einsum('pnqk,pknd->pqnd', weights.astype(jnp.float32), values.astype(jnp.float32))
    return mixed.astype(jnp.bfloat16)

def time_mix(tokens, gain, weight_in, weight_out, scale):
    count_p, count_h, width = tokens.shape
    normed = rms_norm(tokens, gain).reshape(-1, width)
    projected = jnp.dot(normed, weight_in, preferred_element_type=jnp.float32)
    parts = split_heads(projected, (count_p, count_h))
    grouped = tuple((item.reshape(count_p // 8, 8, count_h, HEADS, HEAD_DIM) for item in parts))
    attended = lax.map(lambda group: time_group(group, scale), grouped).reshape(-1, width)
    update = jnp.dot(attended, weight_out, preferred_element_type=jnp.float32)
    return (tokens.astype(jnp.float32) + update.reshape(tokens.shape)).astype(jnp.bfloat16)

def patch_hour(group, visibility, scale):
    queries, keys_all, values = group
    count = queries.shape[0]
    blocks = count // PB
    query_blocks = queries.reshape(blocks, PB, HEADS, HEAD_DIM)
    key_blocks = jnp.take(keys_all.reshape(blocks, PB, HEADS, HEAD_DIM), visibility, axis=0).reshape(blocks, KV * PB, HEADS, HEAD_DIM)
    value_blocks = jnp.take(values.reshape(blocks, PB, HEADS, HEAD_DIM), visibility, axis=0).reshape(blocks, KV * PB, HEADS, HEAD_DIM)
    scores = jnp.einsum('bqnd,bknd->bnqk', query_blocks.astype(jnp.float32), key_blocks.astype(jnp.float32))
    weights = softmax_weights(scores, scale)
    mixed = jnp.einsum('bnqk,bknd->bqnd', weights.astype(jnp.float32), value_blocks.astype(jnp.float32))
    return mixed.astype(jnp.bfloat16).reshape(count, HEADS, HEAD_DIM)

def patch_mix(tokens, visibility, gain, weight_in, weight_out, scale):
    count_p, count_h, width = tokens.shape
    normed = rms_norm(tokens, gain).reshape(-1, width)
    projected = jnp.dot(normed, weight_in, preferred_element_type=jnp.float32)
    parts = split_heads(projected, (count_p, count_h))
    moved = tuple((jnp.moveaxis(item, 1, 0) for item in parts))
    attended = lax.map(lambda group: patch_hour(group, visibility, scale), moved)
    attended = jnp.moveaxis(attended, 0, 1).reshape(-1, width)
    update = jnp.dot(attended, weight_out, preferred_element_type=jnp.float32)
    return (tokens.astype(jnp.float32) + update.reshape(tokens.shape)).astype(jnp.bfloat16)

def feed_forward(tokens, gain, weight_up, weight_down):
    width = tokens.shape[-1]
    normed = rms_norm(tokens, gain).reshape(-1, width)
    hidden = jax.nn.gelu(jnp.dot(normed, weight_up, preferred_element_type=jnp.float32)).astype(jnp.bfloat16)
    update = jnp.dot(hidden, weight_down, preferred_element_type=jnp.float32)
    return (tokens.astype(jnp.float32) + update.reshape(tokens.shape)).astype(jnp.bfloat16)

def run_block(tokens, visibility, gains, scales, mixer_in, mixer_out, expand_weight, reduce_weight):
    tokens = time_mix(tokens, gains[0], mixer_in[0], mixer_out[0], scales[0])
    tokens = patch_mix(tokens, visibility, gains[1], mixer_in[1], mixer_out[1], scales[1])
    return feed_forward(tokens, gains[2], expand_weight, reduce_weight)

def reference(inputs, visibility, norm_gains, scales, mixer_in, mixer_out, expand_weight, reduce_weight):
    finished = []
    for number in range(MICRO):
        tokens = inputs[number]
        for section in range(2):
            tokens = run_block(tokens, visibility, norm_gains[section], scales[section], mixer_in[section], mixer_out[section], expand_weight[section], reduce_weight[section])
        finished.append(tokens)
    return jnp.stack(finished)
```

```python
import functools

import jax
import jax.numpy as jnp
from jax import lax
from jax.experimental import pallas as pl
from jax.experimental.pallas import tpu as pltpu
from jax.sharding import PartitionSpec as P

HEADS = 8
HEAD_DIM = 64
PB = 64
LOG2E = 1.4426950408889634


def row_norm(x, gain):
    factor = lax.rsqrt(jnp.mean(x * x, axis=-1, keepdims=True) + 1e-05)
    return (x * factor * gain).astype(jnp.bfloat16)


def matmul(a, b):
    return jnp.dot(a, b, preferred_element_type=jnp.float32)


def same_head():
    rows = lax.broadcasted_iota(jnp.int32, (256, 256), 0) // HEAD_DIM
    cols = lax.broadcasted_iota(jnp.int32, (256, 256), 1) // HEAD_DIM
    return jnp.where(rows == cols, 1.0, 0.0).astype(jnp.bfloat16)


def head_factor(values, group):
    squares = (values * values).astype(jnp.bfloat16)
    halves = [
        matmul(squares[:, start : start + 256], group) for start in range(0, values.shape[1], 256)
    ]
    sums = jnp.concatenate(halves, axis=1)
    return lax.rsqrt(sums * (1.0 / HEAD_DIM) + 1e-06)


def attention_update(x, gain, scale_of, w_in, w_out, mask):
    width = x.shape[1]
    normed = row_norm(x, gain)
    group = same_head()
    head = lax.broadcasted_iota(jnp.int32, (1, width), 1) // HEAD_DIM
    scale = jnp.zeros((1, width), jnp.float32)
    for n in range(HEADS):
        scale = jnp.where(head == n, scale_of(n) * (LOG2E / HEAD_DIM), scale)
    q = matmul(normed, w_in[:, :width])
    k = matmul(normed, w_in[:, width : 2 * width])
    v = matmul(normed, w_in[:, 2 * width :]).astype(jnp.bfloat16)
    q = (q * head_factor(q, group) * scale).astype(jnp.bfloat16)
    k = (k * head_factor(k, group)).astype(jnp.bfloat16)
    rows = x.shape[0]
    pair = 2 * HEAD_DIM
    low = lax.broadcasted_iota(jnp.int32, (rows, pair), 1) < HEAD_DIM
    low = jnp.where(low, 1.0, 0.0).astype(jnp.bfloat16)
    high = (1.0 - low.astype(jnp.float32)).astype(jnp.bfloat16)
    parts = []
    for start in range(0, width, pair):
        q2, k2, v2 = (t[:, start : start + pair] for t in (q, k, v))
        powers = []
        for side in (low, high):
            scores = lax.dot_general(
                q2 * side, k2, (((1,), (1,)), ((), ())), preferred_element_type=jnp.float32
            )
            powers.append(jnp.exp2(scores).astype(jnp.bfloat16) * mask)
        powers = jnp.concatenate(powers, axis=1)
        upper = jnp.concatenate([v2 * low, low], axis=1)
        lower = jnp.concatenate([v2 * high, high], axis=1)
        sums = matmul(powers, jnp.concatenate([upper, lower], axis=0))
        parts.append((sums[:, :pair] / sums[:, pair:]).astype(jnp.bfloat16))
    return matmul(jnp.concatenate(parts, axis=1), w_out[...])


def rounded(x):
    return x.astype(jnp.bfloat16).astype(jnp.float32)


def time_kernel(sizes, from_inputs, x_ref, gain_ref, scale_ref, w_in_ref, w_out_ref, y_ref):
    patch_count, hour_count, pl_, hl = sizes
    rows = x_ref.shape[0]
    x = x_ref[...]
    if from_inputs:
        to = lax.broadcasted_iota(jnp.int32, (rows, rows), 0)
        source = lax.broadcasted_iota(jnp.int32, (rows, rows), 1)
        late = to % hl
        patch = (to // hl) % pl_
        half = (to // (hl * pl_)) % hour_count
        shard = to // (hl * pl_ * hour_count)
        wanted = ((half * pl_ + patch) * patch_count + shard) * hl + late
        x = matmul(jnp.where(wanted == source, 1.0, 0.0).astype(jnp.bfloat16), x)
    x = x.astype(jnp.float32)
    one = (lax.broadcasted_iota(jnp.int32, (rows, rows), 0) // hl) % pl_
    two = (lax.broadcasted_iota(jnp.int32, (rows, rows), 1) // hl) % pl_
    mask = jnp.where(one == two, 1.0, 0.0).astype(jnp.bfloat16)
    update = attention_update(
        x,
        gain_ref[0, 0:1, :],
        lambda n: scale_ref[0, 0, n],
        w_in_ref,
        w_out_ref,
        mask,
    )
    y_ref[...] = (x + update).astype(jnp.bfloat16)


def patch_kernel(
    sizes, x_ref, seen_ref, gain_ref, scale_ref, w_in_ref, w_out_ref, up_ref, down_ref, y_ref
):
    hl = sizes[3]
    rows = x_ref.shape[0]
    x = x_ref[...].astype(jnp.float32)
    query = lax.broadcasted_iota(jnp.int32, (rows, rows), 0)
    key = lax.broadcasted_iota(jnp.int32, (rows, rows), 1)
    query_block = query // (hl * PB)
    key_block = key // (hl * PB)
    seen = None
    for kv in range(seen_ref.shape[1]):
        chosen = jnp.full((rows, rows), seen_ref[0, kv], jnp.int32)
        for b in range(1, seen_ref.shape[0]):
            chosen = jnp.where(query_block == b, seen_ref[b, kv], chosen)
        hit = jnp.where(chosen == key_block, 1.0, 0.0)
        seen = hit if seen is None else jnp.maximum(seen, hit)
    mask = jnp.where(query % hl == key % hl, seen, 0.0).astype(jnp.bfloat16)
    update = attention_update(
        x,
        gain_ref[0, 1:2, :],
        lambda n: scale_ref[0, 1, n],
        w_in_ref,
        w_out_ref,
        mask,
    )
    x = rounded(x + update)
    normed = row_norm(x, gain_ref[0, 2:3, :])
    total = x
    step = 512
    for start in range(0, up_ref.shape[1], step):
        u = matmul(normed, up_ref[:, start : start + step])
        bent = jnp.tanh(u * (0.7978845608028654 + 0.035677408136300125 * (u * u)))
        hidden = (0.5 * u * (1.0 + bent)).astype(jnp.bfloat16)
        total = total + matmul(hidden, down_ref[start : start + step, :])
    y_ref[...] = total.astype(jnp.bfloat16)


def final_kernel(sizes, pipe_ref, a_ref, b_ref, y_ref):
    patch_count, hour_count, pl_, hl = sizes
    rows = a_ref.shape[1]
    patches = pl_ * hour_count
    to = lax.broadcasted_iota(jnp.int32, (rows, rows), 0)
    source = lax.broadcasted_iota(jnp.int32, (rows, rows), 1)
    late = to % hl
    shard = (to // hl) % patch_count
    patch = to // (hl * patch_count)
    wanted = (shard * patches + patch) * hl + late
    order = jnp.where(wanted == source, 1.0, 0.0).astype(jnp.bfloat16)
    own = pipe_ref[0] == 1
    for m in range(a_ref.shape[0]):
        x = jnp.where(own, a_ref[m], b_ref[m])
        y_ref[m] = matmul(order, x).astype(jnp.bfloat16)


VMEM = pl.BlockSpec(memory_space=pltpu.VMEM)
SMEM = pl.BlockSpec(memory_space=pltpu.SMEM)


def part(shape, index):
    return pl.BlockSpec((None, None) + shape, lambda i: (0, index, 0, 0))


def call_time(sizes, from_inputs, x, gains, scales, w_in, w_out):
    width = x.shape[1]
    return pl.pallas_call(
        functools.partial(time_kernel, sizes, from_inputs),
        out_shape=jax.ShapeDtypeStruct(x.shape, jnp.bfloat16),
        in_specs=[VMEM, VMEM, SMEM, part((width, 3 * width), 0), part((width, width), 0)],
        out_specs=VMEM,
        grid=(1,),
        compiler_params=pltpu.CompilerParams(vmem_limit_bytes=24 << 20),
        name="time_attention",
    )(x, gains, scales, w_in, w_out)


def call_patch(sizes, x, seen, gains, scales, w_in, w_out, w_up, w_down):
    width = x.shape[1]
    return pl.pallas_call(
        functools.partial(patch_kernel, sizes),
        out_shape=jax.ShapeDtypeStruct(x.shape, jnp.bfloat16),
        in_specs=[VMEM, SMEM, VMEM, SMEM, part((width, 3 * width), 1), part((width, width), 1)]
        + [pl.BlockSpec((None,) + w.shape[1:], lambda i: (0, 0, 0)) for w in (w_up, w_down)],
        out_specs=VMEM,
        grid=(1,),
        compiler_params=pltpu.CompilerParams(vmem_limit_bytes=24 << 20),
        name="patch_attention_and_ffn",
    )(x, seen, gains, scales, w_in, w_out, w_up, w_down)


def call_final(sizes, pipe, a, b):
    return pl.pallas_call(
        functools.partial(final_kernel, sizes),
        out_shape=jax.ShapeDtypeStruct(a.shape, jnp.bfloat16),
        in_specs=[SMEM, VMEM, VMEM],
        out_specs=VMEM,
        grid=(1,),
        compiler_params=pltpu.CompilerParams(vmem_limit_bytes=24 << 20),
        name="final_order",
    )(pipe, a, b)


def exchange(x, axes, count):
    rows, width = x.shape
    x = x.reshape(count, rows // count, width)
    return lax.all_to_all(x, axes, split_axis=0, concat_axis=0, tiled=True).reshape(rows, width)


def local(inputs, seen, gains, scales, w_in, w_out, w_up, w_down):
    patch_count = lax.axis_size("patch")
    hour_count = lax.axis_size("hour")
    pipes = lax.axis_size("pipe")
    micro, patches, hours, width = inputs.shape
    rows = patches * hours
    sizes = (patch_count, hour_count, patches // hour_count, hours // patch_count)
    both = ("patch", "hour")
    count = patch_count * hour_count
    onward = [(s, (s + 1) % pipes) for s in range(pipes)]
    tokens = [exchange(inputs[m].reshape(rows, width), "hour", hour_count) for m in range(micro)]
    for stage in range(pipes):
        last = stage == pipes - 1
        mixed = [call_time(sizes, stage == 0, t, gains, scales, w_in, w_out) for t in tokens]
        tokens = [exchange(t, both, count) for t in mixed]
        done = [call_patch(sizes, t, seen, gains, scales, w_in, w_out, w_up, w_down) for t in tokens]
        if not last:
            done = [lax.ppermute(t, "pipe", onward) for t in done]
            tokens = [exchange(t, both, count) for t in done]
    own = [exchange(t, "patch", patch_count) for t in done]
    other = [lax.ppermute(t, "pipe", onward) for t in own]
    pipe = lax.axis_index("pipe").reshape(1)
    out = call_final(sizes, pipe, jnp.stack(own), jnp.stack(other))
    return out.reshape(inputs.shape)


def solution(mesh):
    placed = (
        P(None, "patch", "hour", None),
        P(),
        P("pipe", None, None),
        P("pipe", None, None),
        P("pipe", None, None, None),
        P("pipe", None, None, None),
        P("pipe", None, None),
        P("pipe", None, None),
    )
    return jax.shard_map(
        local, mesh=mesh, in_specs=placed, out_specs=P(None, "patch", "hour", None), check_vma=False
    )
```

```python
import functools

import jax
import jax.numpy as jnp
from jax import lax
from jax.experimental import pallas as pl
from jax.experimental.pallas import tpu as pltpu
from jax.sharding import PartitionSpec as P

HEADS = 8
HEAD_DIM = 64
PB = 64
LOG2E = 1.4426950408889634


def row_norm(x, gain):
    factor = lax.rsqrt(jnp.mean(x * x, axis=-1, keepdims=True) + 1e-05)
    return (x * factor * gain).astype(jnp.bfloat16)


def matmul(a, b):
    return jnp.dot(a, b, preferred_element_type=jnp.float32)


def same_head():
    rows = lax.broadcasted_iota(jnp.int32, (256, 256), 0) // HEAD_DIM
    cols = lax.broadcasted_iota(jnp.int32, (256, 256), 1) // HEAD_DIM
    return jnp.where(rows == cols, 1.0, 0.0).astype(jnp.bfloat16)


def head_factor(values, group):
    squares = (values * values).astype(jnp.bfloat16)
    halves = [
        matmul(squares[:, start : start + 256], group) for start in range(0, values.shape[1], 256)
    ]
    sums = jnp.concatenate(halves, axis=1)
    return lax.rsqrt(sums * (1.0 / HEAD_DIM) + 1e-06)


def attention_update(x, more, gain, scale_of, w_in, w_out, mask):
    width = x.shape[1]
    normed = row_norm(x, gain)
    seen = jnp.concatenate([normed] + [row_norm(t, gain) for t in more], axis=0)
    group = same_head()
    head = lax.broadcasted_iota(jnp.int32, (1, width), 1) // HEAD_DIM
    scale = jnp.zeros((1, width), jnp.float32)
    for n in range(HEADS):
        scale = jnp.where(head == n, scale_of(n) * (LOG2E / HEAD_DIM), scale)
    q = matmul(normed, w_in[:, :width])
    k = matmul(seen, w_in[:, width : 2 * width])
    v = matmul(seen, w_in[:, 2 * width :]).astype(jnp.bfloat16)
    q = (q * head_factor(q, group) * scale).astype(jnp.bfloat16)
    k = (k * head_factor(k, group)).astype(jnp.bfloat16)
    pair = 2 * HEAD_DIM
    first = lax.broadcasted_iota(jnp.int32, (1, pair), 1) < HEAD_DIM
    low = jnp.where(first, 1.0, 0.0).astype(jnp.bfloat16)
    high = jnp.where(first, 0.0, 1.0).astype(jnp.bfloat16)
    low_all = jnp.broadcast_to(low, (k.shape[0], pair))
    high_all = jnp.broadcast_to(high, (k.shape[0], pair))
    parts = []
    for start in range(0, width, pair):
        q2, k2, v2 = (t[:, start : start + pair] for t in (q, k, v))
        powers = []
        for side in (low, high):
            scores = lax.dot_general(
                q2 * side, k2, (((1,), (1,)), ((), ())), preferred_element_type=jnp.float32
            )
            powers.append(jnp.exp2(scores).astype(jnp.bfloat16) * mask)
        powers = jnp.concatenate(powers, axis=1)
        upper = jnp.concatenate([v2 * low, low_all], axis=1)
        lower = jnp.concatenate([v2 * high, high_all], axis=1)
        sums = matmul(powers, jnp.concatenate([upper, lower], axis=0))
        parts.append((sums[:, :pair] / sums[:, pair:]).astype(jnp.bfloat16))
    return matmul(jnp.concatenate(parts, axis=1), w_out[...])


def rounded(x):
    return x.astype(jnp.bfloat16).astype(jnp.float32)


def digits(shape, dimension, *bases):
    index = lax.broadcasted_iota(jnp.int32, shape, dimension)
    out = []
    for base in bases:
        out.append(index % base)
        index = index // base
    return out + [index]


def time_kernel(sizes, from_inputs, place_ref, *refs):
    shards, peers, patches, hl = sizes
    x_refs, (gain_ref, scale_ref, w_in_ref, w_out_ref), y_refs = (
        refs[:peers],
        refs[peers : peers + 4],
        refs[peers + 4 :],
    )
    rows, _ = x_refs[0].shape
    xs = [x_ref[...] for x_ref in x_refs]
    if from_inputs:
        late, patch, offset = digits((rows, rows), 0, hl, patches)
        source = lax.broadcasted_iota(jnp.int32, (rows, rows), 1)
        wanted = (patch * shards + (offset ^ place_ref[1])) * hl + late
        order = jnp.where(wanted == source, 1.0, 0.0).astype(jnp.bfloat16)
        xs = [matmul(order, x) for x in xs]
    xs = [x.astype(jnp.float32) for x in xs]
    mine = digits((rows, rows * peers), 0, hl, patches)[1]
    theirs = digits((rows, rows * peers), 1, hl, patches)[1]
    mask = jnp.where(mine == theirs, 1.0, 0.0).astype(jnp.bfloat16)
    update = attention_update(
        xs[0],
        xs[1:],
        gain_ref[0, 0:1, :],
        lambda n: scale_ref[0, 0, n],
        w_in_ref.at[0, 0],
        w_out_ref.at[0, 0],
        mask,
    )
    y = (xs[0] + update).astype(jnp.bfloat16)
    size = rows // shards
    for k in range(shards):
        y_refs[k][...] = y[k * size : (k + 1) * size]


def patch_kernel(sizes, place_ref, seen_ref, *refs):
    shards, _, patches, hl = sizes
    x_refs, (gain_ref, scale_ref, w_in_ref, w_out_ref, up_ref, down_ref), y_refs = (
        refs[:shards],
        refs[shards : shards + 6],
        refs[shards + 6 :],
    )
    x = jnp.concatenate([x_ref[...] for x_ref in x_refs], axis=0).astype(jnp.float32)
    rows = x.shape[0]

    def block_and_hour(dimension):
        late, patch, offset = digits((rows, rows), dimension, hl, patches)
        return ((offset ^ place_ref[1]) * patches + patch) // PB, late

    query_block, query_hour = block_and_hour(0)
    key_block, key_hour = block_and_hour(1)
    seen = None
    for kv in range(seen_ref.shape[1]):
        chosen = jnp.full((rows, rows), seen_ref[0, kv], jnp.int32)
        for b in range(1, seen_ref.shape[0]):
            chosen = jnp.where(query_block == b, seen_ref[b, kv], chosen)
        hit = jnp.where(chosen == key_block, 1.0, 0.0)
        seen = hit if seen is None else jnp.maximum(seen, hit)
    mask = jnp.where(query_hour == key_hour, seen, 0.0).astype(jnp.bfloat16)
    update = attention_update(
        x,
        [],
        gain_ref[0, 1:2, :],
        lambda n: scale_ref[0, 1, n],
        w_in_ref.at[0, 1],
        w_out_ref.at[0, 1],
        mask,
    )
    x = rounded(x + update)
    normed = row_norm(x, gain_ref[0, 2:3, :])
    total = x
    step = 512
    for start in range(0, up_ref.shape[2], step):
        u = matmul(normed, up_ref[0, :, start : start + step])
        bent = jnp.tanh(u * (0.7978845608028654 + 0.035677408136300125 * (u * u)))
        hidden = (0.5 * u * (1.0 + bent)).astype(jnp.bfloat16)
        total = total + matmul(hidden, down_ref[0, start : start + step, :])
    y = total.astype(jnp.bfloat16)
    size = rows // shards
    for k in range(shards):
        y_refs[k][...] = y[k * size : (k + 1) * size]


def final_kernel(sizes, micro, place_ref, *refs):
    shards, _, patches, hl = sizes
    y_ref = refs[-1]
    rows = shards * patches * hl
    late, shard, patch = digits((rows, rows), 0, hl, shards)
    source = lax.broadcasted_iota(jnp.int32, (rows, rows), 1)
    wanted = ((shard ^ place_ref[1]) * patches + patch) * hl + late
    order = jnp.where(wanted == source, 1.0, 0.0).astype(jnp.bfloat16)
    mine = place_ref[0] == place_ref[2]
    for m in range(micro):
        own = refs[2 * m * shards : (2 * m + 1) * shards]
        sent = refs[(2 * m + 1) * shards : (2 * m + 2) * shards]
        x = [jnp.where(mine, a[...], b[...]) for a, b in zip(own, sent)]
        y_ref[m] = matmul(order, jnp.concatenate(x, axis=0)).astype(jnp.bfloat16)


VMEM = pl.BlockSpec(memory_space=pltpu.VMEM)
SMEM = pl.BlockSpec(memory_space=pltpu.SMEM)
PARAMS = pltpu.CompilerParams(vmem_limit_bytes=32 << 20)


def blocks_of(shards, rows, width):
    return [jax.ShapeDtypeStruct((rows // shards, width), jnp.bfloat16)] * shards


def call_time(sizes, from_inputs, place, xs, gains, scales, w_in, w_out):
    rows, width = xs[0].shape
    return pl.pallas_call(
        functools.partial(time_kernel, sizes, from_inputs),
        out_shape=blocks_of(sizes[0], rows, width),
        in_specs=[SMEM] + [VMEM] * len(xs) + [VMEM, SMEM, VMEM, VMEM],
        out_specs=[VMEM] * sizes[0],
        compiler_params=PARAMS,
        cost_estimate=pl.CostEstimate(
            flops=4 << 30, bytes_accessed=1 << 20, transcendentals=1 << 20
        ),
        name="time_attention",
    )(place, *xs, gains, scales, w_in, w_out)


def call_patch(sizes, place, seen, xs, gains, scales, w_in, w_out, w_up, w_down):
    rows, width = xs[0].shape
    return pl.pallas_call(
        functools.partial(patch_kernel, sizes),
        out_shape=blocks_of(sizes[0], rows * sizes[0], width),
        in_specs=[SMEM, SMEM] + [VMEM] * len(xs) + [VMEM, SMEM] + [VMEM] * 4,
        out_specs=[VMEM] * sizes[0],
        compiler_params=PARAMS,
        cost_estimate=pl.CostEstimate(
            flops=5 << 30, bytes_accessed=1 << 20, transcendentals=1 << 20
        ),
        name="patch_attention_and_ffn",
    )(place, seen, *xs, gains, scales, w_in, w_out, w_up, w_down)


def call_final(sizes, place, shape, parts):
    micro, rows, width = shape
    return pl.pallas_call(
        functools.partial(final_kernel, sizes, micro),
        out_shape=jax.ShapeDtypeStruct((micro, rows, width), jnp.bfloat16),
        in_specs=[SMEM] + [VMEM] * len(parts),
        out_specs=VMEM,
        compiler_params=PARAMS,
        name="final_order",
    )(place, *parts)


def flipped(x, axis, k):
    return lax.ppermute(x, axis, [(s, s ^ k) for s in range(lax.axis_size(axis))])


def handed_on(x, stage, target, k):
    shards = lax.axis_size("patch")
    pairs = [(stage * shards + s, target * shards + (s ^ k)) for s in range(shards)]
    return lax.ppermute(x, ("pipe", "patch"), pairs)


def local(inputs, seen, gains, scales, w_in, w_out, w_up, w_down):
    shards = lax.axis_size("patch")
    peers = lax.axis_size("hour")
    pipes = lax.axis_size("pipe")
    micro, patches, hours, width = inputs.shape
    rows = patches * hours
    sizes = (shards, peers, patches, hours // shards)
    place = jnp.stack([lax.axis_index("pipe"), lax.axis_index("patch"), jnp.int32(pipes - 1)])
    tokens = [inputs[m].reshape(rows, width) for m in range(micro)]
    for stage in range(pipes):
        gathered = [[t] + [flipped(t, "hour", j) for j in range(1, peers)] for t in tokens]
        mixed = [call_time(sizes, stage == 0, place, t, gains, scales, w_in, w_out) for t in gathered]
        spread = [
            [t[0]] + [flipped(t[k], "patch", k) for k in range(1, shards)] for t in mixed
        ]
        done = [
            call_patch(sizes, place, seen, t, gains, scales, w_in, w_out, w_up, w_down)
            for t in spread
        ]
        if stage < pipes - 1:
            tokens = [
                jnp.concatenate([handed_on(t[k], stage, stage + 1, k) for k in range(shards)])
                for t in done
            ]
    parts = []
    for t in done:
        parts += [t[0]] + [flipped(t[k], "patch", k) for k in range(1, shards)]
        for k in range(shards):
            sent = t[k]
            for target in range(pipes - 1):
                sent = handed_on(t[k], pipes - 1, target, k)
            parts.append(sent)
    return call_final(sizes, place, (micro, rows, width), parts).reshape(inputs.shape)


def solution(mesh):
    placed = (
        P(None, "patch", "hour", None),
        P(),
        P("pipe", None, None),
        P("pipe", None, None),
        P("pipe", None, None, None),
        P("pipe", None, None, None),
        P("pipe", None, None),
        P("pipe", None, None),
    )
    return jax.shard_map(
        local, mesh=mesh, in_specs=placed, out_specs=P(None, "patch", "hour", None), check_vma=False
    )
```

```python
import functools

import jax
import jax.numpy as jnp
from jax import lax
from jax.experimental import pallas as pl
from jax.experimental.pallas import tpu as pltpu
from jax.sharding import PartitionSpec as P

HEADS = 8
HEAD_DIM = 64
PB = 64
LOG2E = 1.4426950408889634


def row_norm(x, gain):
    factor = lax.rsqrt(jnp.mean(x * x, axis=-1, keepdims=True) + 1e-05)
    return (x * factor * gain).astype(jnp.bfloat16)


def matmul(a, b):
    return jnp.dot(a, b, preferred_element_type=jnp.float32)


def same_head():
    rows = lax.broadcasted_iota(jnp.int32, (256, 256), 0) // HEAD_DIM
    cols = lax.broadcasted_iota(jnp.int32, (256, 256), 1) // HEAD_DIM
    return jnp.where(rows == cols, 1.0, 0.0).astype(jnp.bfloat16)


def head_factor(values, group):
    squares = (values * values).astype(jnp.bfloat16)
    halves = [
        matmul(squares[:, start : start + 256], group) for start in range(0, values.shape[1], 256)
    ]
    sums = jnp.concatenate(halves, axis=1)
    return lax.rsqrt(sums * (1.0 / HEAD_DIM) + 1e-06)


def attention_update(x, more, gain, scale_of, w_in, w_out, mask):
    width = x.shape[1]
    normed = row_norm(x, gain)
    seen = jnp.concatenate([normed] + [row_norm(t, gain) for t in more], axis=0)
    group = same_head()
    head = lax.broadcasted_iota(jnp.int32, (1, width), 1) // HEAD_DIM
    scale = jnp.zeros((1, width), jnp.float32)
    for n in range(HEADS):
        scale = jnp.where(head == n, scale_of(n) * (LOG2E / HEAD_DIM), scale)
    q = matmul(normed, w_in[:, :width])
    k = matmul(seen, w_in[:, width : 2 * width])
    v = matmul(seen, w_in[:, 2 * width :]).astype(jnp.bfloat16)
    q = (q * head_factor(q, group) * scale).astype(jnp.bfloat16)
    k = (k * head_factor(k, group)).astype(jnp.bfloat16)
    pair = 2 * HEAD_DIM
    first = lax.broadcasted_iota(jnp.int32, (1, pair), 1) < HEAD_DIM
    low = jnp.where(first, 1.0, 0.0).astype(jnp.bfloat16)
    high = jnp.where(first, 0.0, 1.0).astype(jnp.bfloat16)
    low_all = jnp.broadcast_to(low, (k.shape[0], pair))
    high_all = jnp.broadcast_to(high, (k.shape[0], pair))
    parts = []
    for start in range(0, width, pair):
        q2, k2, v2 = (t[:, start : start + pair] for t in (q, k, v))
        powers = []
        for side in (low, high):
            scores = lax.dot_general(
                q2 * side, k2, (((1,), (1,)), ((), ())), preferred_element_type=jnp.float32
            )
            powers.append(jnp.exp2(scores).astype(jnp.bfloat16) * mask)
        powers = jnp.concatenate(powers, axis=1)
        upper = jnp.concatenate([v2 * low, low_all], axis=1)
        lower = jnp.concatenate([v2 * high, high_all], axis=1)
        sums = matmul(powers, jnp.concatenate([upper, lower], axis=0))
        parts.append((sums[:, :pair] / sums[:, pair:]).astype(jnp.bfloat16))
    return matmul(jnp.concatenate(parts, axis=1), w_out[...])


def rounded(x):
    return x.astype(jnp.bfloat16).astype(jnp.float32)


def digits(shape, dimension, *bases):
    index = lax.broadcasted_iota(jnp.int32, shape, dimension)
    out = []
    for base in bases:
        out.append(index % base)
        index = index // base
    return out + [index]


def time_kernel(sizes, stage, micro, place_ref, *refs):
    slow, peers, patches, hl = sizes
    x_refs, (gain_ref, scale_ref, w_in_ref, w_out_ref), y_refs = (
        refs[:peers],
        refs[peers : peers + 4],
        refs[peers + 4 :],
    )

    @pl.when(place_ref[0] == stage)
    def _():
        if micro is None:
            xs = [x_ref[...] for x_ref in x_refs]
            rows = xs[0].shape[0]
        else:
            rows = x_refs[0].shape[1]
            late, patch, offset = digits((rows, rows), 0, hl, patches)
            source = lax.broadcasted_iota(jnp.int32, (rows, rows), 1)
            wanted = (patch * slow + (offset ^ place_ref[1])) * hl + late
            order = jnp.where(wanted == source, 1.0, 0.0).astype(jnp.bfloat16)
            xs = [matmul(order, x_ref[micro]) for x_ref in x_refs]
        xs = [x.astype(jnp.float32) for x in xs]
        mine = digits((rows, rows * peers), 0, hl, patches)[1]
        theirs = digits((rows, rows * peers), 1, hl, patches)[1]
        mask = jnp.where(mine == theirs, 1.0, 0.0).astype(jnp.bfloat16)
        update = attention_update(
            xs[0],
            xs[1:],
            gain_ref[0, 0:1, :],
            lambda n: scale_ref[0, 0, n],
            w_in_ref.at[0, 0],
            w_out_ref.at[0, 0],
            mask,
        )
        y = (xs[0] + update).astype(jnp.bfloat16)
        size = rows // slow
        for k in range(slow):
            y_refs[k][...] = y[k * size : (k + 1) * size]


def patch_kernel(sizes, stage, place_ref, seen_ref, *refs):
    slow, _, patches, hl = sizes
    fast = len(refs) - 6 - slow
    x_refs, (gain_ref, scale_ref, w_in_ref, w_out_ref, up_ref, down_ref), y_refs = (
        refs[:fast],
        refs[fast : fast + 6],
        refs[fast + 6 :],
    )

    @pl.when(place_ref[0] == stage)
    def _():
        xs = [x_ref[...].astype(jnp.float32) for x_ref in x_refs]
        x = xs[0]
        rows = x.shape[0]
        shape = (rows, rows * fast)

        def block_and_hour(dimension):
            late, patch, offset, other = digits(shape, dimension, hl, patches, slow)
            shard = (offset ^ place_ref[1]) * fast + (other ^ place_ref[2])
            return (shard * patches + patch) // PB, late

        query_block, query_hour = block_and_hour(0)
        key_block, key_hour = block_and_hour(1)
        seen = None
        for kv in range(seen_ref.shape[1]):
            chosen = jnp.full(shape, seen_ref[0, kv], jnp.int32)
            for b in range(1, seen_ref.shape[0]):
                chosen = jnp.where(query_block == b, seen_ref[b, kv], chosen)
            hit = jnp.where(chosen == key_block, 1.0, 0.0)
            seen = hit if seen is None else jnp.maximum(seen, hit)
        mask = jnp.where(query_hour == key_hour, seen, 0.0).astype(jnp.bfloat16)
        update = attention_update(
            x,
            xs[1:],
            gain_ref[0, 1:2, :],
            lambda n: scale_ref[0, 1, n],
            w_in_ref.at[0, 1],
            w_out_ref.at[0, 1],
            mask,
        )
        x = rounded(x + update)
        normed = row_norm(x, gain_ref[0, 2:3, :])
        total = x
        step = 512
        for start in range(0, up_ref.shape[2], step):
            u = matmul(normed, up_ref[0, :, start : start + step])
            bent = jnp.tanh(u * (0.7978845608028654 + 0.035677408136300125 * (u * u)))
            hidden = (0.5 * u * (1.0 + bent)).astype(jnp.bfloat16)
            total = total + matmul(hidden, down_ref[0, start : start + step, :])
        y = total.astype(jnp.bfloat16)
        size = rows // slow
        for k in range(slow):
            y_refs[k][...] = y[k * size : (k + 1) * size]


def final_kernel(sizes, micro, last, place_ref, *refs):
    slow, _, patches, hl = sizes
    y_ref = refs[-1]
    rows = slow * patches * hl
    late, shard, patch = digits((rows, rows), 0, hl, slow)
    source = lax.broadcasted_iota(jnp.int32, (rows, rows), 1)
    wanted = ((shard ^ place_ref[1]) * patches + patch) * hl + late
    order = jnp.where(wanted == source, 1.0, 0.0).astype(jnp.bfloat16)

    def write(skip):
        for m in range(micro):
            start = (2 * m + skip) * slow
            x = jnp.concatenate([ref[...] for ref in refs[start : start + slow]], axis=0)
            y_ref[m] = matmul(order, x).astype(jnp.bfloat16)

    @pl.when(place_ref[0] == last)
    def _():
        write(0)

    @pl.when(place_ref[0] != last)
    def _():
        write(1)


VMEM = pl.BlockSpec(memory_space=pltpu.VMEM)
SMEM = pl.BlockSpec(memory_space=pltpu.SMEM)
PARAMS = pltpu.CompilerParams(vmem_limit_bytes=32 << 20)
COST = pl.CostEstimate(flops=5 << 30, bytes_accessed=1 << 20, transcendentals=1 << 20)


def blocks_of(count, rows, width):
    return [jax.ShapeDtypeStruct((rows // count, width), jnp.bfloat16)] * count


def call_time(sizes, stage, micro, place, xs, gains, scales, w_in, w_out):
    rows, width = xs[0].shape[-2:]
    return pl.pallas_call(
        functools.partial(time_kernel, sizes, stage, micro),
        out_shape=blocks_of(sizes[0], rows, width),
        in_specs=[SMEM] + [VMEM] * len(xs) + [VMEM, SMEM, VMEM, VMEM],
        out_specs=[VMEM] * sizes[0],
        compiler_params=PARAMS,
        cost_estimate=COST,
        name="time_attention",
    )(place, *xs, gains, scales, w_in, w_out)


def call_patch(sizes, stage, place, seen, xs, gains, scales, w_in, w_out, w_up, w_down):
    rows, width = xs[0].shape
    return pl.pallas_call(
        functools.partial(patch_kernel, sizes, stage),
        out_shape=blocks_of(sizes[0], rows, width),
        in_specs=[SMEM, SMEM] + [VMEM] * len(xs) + [VMEM, SMEM] + [VMEM] * 4,
        out_specs=[VMEM] * sizes[0],
        compiler_params=PARAMS,
        cost_estimate=COST,
        name="patch_attention_and_ffn",
    )(place, seen, *xs, gains, scales, w_in, w_out, w_up, w_down)


def call_final(sizes, last, place, shape, parts):
    micro, rows, width = shape
    return pl.pallas_call(
        functools.partial(final_kernel, sizes, micro, last),
        out_shape=jax.ShapeDtypeStruct((micro, rows, width), jnp.bfloat16),
        in_specs=[SMEM] + [VMEM] * len(parts),
        out_specs=VMEM,
        compiler_params=PARAMS,
        name="final_order",
    )(place, *parts)


def sent(x, axis, offset, stage, target):
    count = lax.axis_size(axis)
    pairs = [(stage * count + s, target * count + (s ^ offset)) for s in range(count)]
    return lax.ppermute(x, ("pipe", axis), pairs)


def local(inputs, seen, gains, scales, w_in, w_out, w_up, w_down):
    shards = lax.axis_size("patch")
    peers = lax.axis_size("hour")
    pipes = lax.axis_size("pipe")
    micro, patches, hours, width = inputs.shape
    rows = patches * hours
    fast = 2
    slow = shards // fast
    sizes = (slow, peers, patches, hours // slow)
    last = pipes - 1
    shard = lax.axis_index("patch")
    place = jnp.stack([lax.axis_index("pipe"), shard // fast, shard % fast])

    def to_slow(blocks, stage, target, first):
        return [sent(blocks[k], "patch", k * fast, stage, target) for k in range(first, slow)]

    def with_others(x, axis, count, stage):
        return [x] + [sent(x, axis, k, stage, stage) for k in range(1, count)]

    whole = with_others(inputs.reshape(micro, rows, width), "hour", peers, 0)
    tokens = [whole] * micro
    for stage in range(pipes):
        mixed = [
            call_time(sizes, stage, None if stage else m, place, t, gains, scales, w_in, w_out)
            for m, t in enumerate(tokens)
        ]
        spread = [jnp.concatenate([t[0]] + to_slow(t, stage, stage, 1)) for t in mixed]
        seen_rows = [with_others(t, "patch", fast, stage) for t in spread]
        done = [
            call_patch(sizes, stage, place, seen, t, gains, scales, w_in, w_out, w_up, w_down)
            for t in seen_rows
        ]
        if stage < last:
            arrived = [jnp.concatenate(to_slow(t, stage, stage + 1, 0)) for t in done]
            tokens = [with_others(t, "hour", peers, stage + 1) for t in arrived]
    parts = []
    for t in done:
        parts += [t[0]] + to_slow(t, last, last, 1)
        away = t
        for target in range(last):
            away = to_slow(t, last, target, 0)
        parts += away
    out = call_final(sizes, last, place, (micro, rows, width), parts)
    return out.reshape(inputs.shape)


def solution(mesh):
    placed = (
        P(None, "patch", "hour", None),
        P(),
        P("pipe", None, None),
        P("pipe", None, None),
        P("pipe", None, None, None),
        P("pipe", None, None, None),
        P("pipe", None, None),
        P("pipe", None, None),
    )
    return jax.shard_map(
        local, mesh=mesh, in_specs=placed, out_specs=P(None, "patch", "hour", None), check_vma=False
    )
```

```python
import functools

import jax
import jax.numpy as jnp
from jax import lax
from jax.experimental import pallas as pl
from jax.experimental.pallas import tpu as pltpu
from jax.sharding import PartitionSpec as P

HEADS = 8
HEAD_DIM = 64
PB = 64
LOG2E = 1.4426950408889634


def row_norm(x, gain):
    factor = lax.rsqrt(jnp.mean(x * x, axis=-1, keepdims=True) + 1e-05)
    return (x * factor * gain).astype(jnp.bfloat16)


def matmul(a, b):
    return jnp.dot(a, b, preferred_element_type=jnp.float32)


def same_head():
    rows = lax.broadcasted_iota(jnp.int32, (256, 256), 0) // HEAD_DIM
    cols = lax.broadcasted_iota(jnp.int32, (256, 256), 1) // HEAD_DIM
    return jnp.where(rows == cols, 1.0, 0.0).astype(jnp.bfloat16)


def head_factor(values, group):
    squares = (values * values).astype(jnp.bfloat16)
    halves = [
        matmul(squares[:, start : start + 256], group) for start in range(0, values.shape[1], 256)
    ]
    sums = jnp.concatenate(halves, axis=1)
    return lax.rsqrt(sums * (1.0 / HEAD_DIM) + 1e-06)


def attention_update(x, more, gain, scale_of, w_in, w_out, mask):
    width = x.shape[1]
    normed = row_norm(x, gain)
    seen = jnp.concatenate([normed] + [row_norm(t, gain) for t in more], axis=0)
    group = same_head()
    head = lax.broadcasted_iota(jnp.int32, (1, width), 1) // HEAD_DIM
    scale = jnp.zeros((1, width), jnp.float32)
    for n in range(HEADS):
        scale = jnp.where(head == n, scale_of(n) * (LOG2E / HEAD_DIM), scale)
    q = matmul(normed, w_in[:, :width])
    k = matmul(seen, w_in[:, width : 2 * width])
    v = matmul(seen, w_in[:, 2 * width :]).astype(jnp.bfloat16)
    q = (q * head_factor(q, group) * scale).astype(jnp.bfloat16)
    k = (k * head_factor(k, group)).astype(jnp.bfloat16)
    pair = 2 * HEAD_DIM
    first = lax.broadcasted_iota(jnp.int32, (1, pair), 1) < HEAD_DIM
    low = jnp.where(first, 1.0, 0.0).astype(jnp.bfloat16)
    high = jnp.where(first, 0.0, 1.0).astype(jnp.bfloat16)
    low_all = jnp.broadcast_to(low, (k.shape[0], pair))
    high_all = jnp.broadcast_to(high, (k.shape[0], pair))
    parts = []
    for start in range(0, width, pair):
        q2, k2, v2 = (t[:, start : start + pair] for t in (q, k, v))
        powers = []
        for side in (low, high):
            scores = lax.dot_general(
                q2 * side, k2, (((1,), (1,)), ((), ())), preferred_element_type=jnp.float32
            )
            powers.append(jnp.exp2(scores).astype(jnp.bfloat16) * mask)
        powers = jnp.concatenate(powers, axis=1)
        upper = jnp.concatenate([v2 * low, low_all], axis=1)
        lower = jnp.concatenate([v2 * high, high_all], axis=1)
        sums = matmul(powers, jnp.concatenate([upper, lower], axis=0))
        parts.append((sums[:, :pair] / sums[:, pair:]).astype(jnp.bfloat16))
    return matmul(jnp.concatenate(parts, axis=1), w_out[...])


def rounded(x):
    return x.astype(jnp.bfloat16).astype(jnp.float32)


def digits(shape, dimension, *bases):
    index = lax.broadcasted_iota(jnp.int32, shape, dimension)
    out = []
    for base in bases:
        out.append(index % base)
        index = index // base
    return out + [index]


def at_work(place_ref, step, micro):
    number = step - place_ref[0]
    return jnp.logical_and(number >= 0, number < micro)


def time_kernel(sizes, step, micro, place_ref, *refs):
    shards, peers, patches, hl = sizes
    given = peers if step < micro else 0
    came = peers if step > 0 else 0
    input_refs, refs = refs[:given], refs[given:]
    came_refs, refs = refs[:came], refs[came:]
    (gain_ref, scale_ref, w_in_ref, w_out_ref), refs = refs[:4], refs[4:]
    y_refs, refs = refs[:shards], refs[shards:]
    x_ref, refs = refs[0], refs[1:]
    rows = x_ref.shape[0] // peers

    @pl.when(at_work(place_ref, step, micro))
    def _():
        w_in, w_out = w_in_ref.at[0, 0], w_out_ref.at[0, 0]
        copies = []
        if refs:
            w_in_here, w_out_here, sems = refs
            copies = [
                pltpu.make_async_copy(w_in, w_in_here, sems.at[0]),
                pltpu.make_async_copy(w_out, w_out_here, sems.at[1]),
            ]
            for copy in copies:
                copy.start()
            w_in, w_out = w_in_here, w_out_here

        if given:

            @pl.when(place_ref[0] == 0)
            def _():
                late, patch, offset = digits((rows, rows), 0, hl, patches)
                source = lax.broadcasted_iota(jnp.int32, (rows, rows), 1)
                wanted = (patch * shards + (offset ^ place_ref[1])) * hl + late
                order = jnp.where(wanted == source, 1.0, 0.0).astype(jnp.bfloat16)
                for j, ref in enumerate(input_refs):
                    moved = matmul(order, ref[step]).astype(jnp.bfloat16)
                    x_ref[j * rows : (j + 1) * rows, :] = moved

        if came:

            @pl.when(place_ref[0] != 0)
            def _():
                for j, ref in enumerate(came_refs):
                    x_ref[j * rows : (j + 1) * rows, :] = ref[...]

        x = x_ref[...].astype(jnp.float32)
        mine = digits((rows, rows * peers), 0, hl, patches)[1]
        theirs = digits((rows, rows * peers), 1, hl, patches)[1]
        mask = jnp.where(mine == theirs, 1.0, 0.0).astype(jnp.bfloat16)
        for copy in copies:
            copy.wait()
        update = attention_update(
            x[:rows],
            [x[rows:]],
            gain_ref[0, 0:1, :],
            lambda n: scale_ref[0, 0, n],
            w_in,
            w_out,
            mask,
        )
        y = (x[:rows] + update).astype(jnp.bfloat16)
        size = rows // shards
        for k in range(shards):
            y_refs[k][...] = y[k * size : (k + 1) * size]


def patch_kernel(sizes, step, micro, place_ref, seen_ref, *refs):
    shards, _, patches, hl = sizes
    x_refs, (gain_ref, scale_ref, w_in_ref, w_out_ref, up_ref, down_ref), y_refs = (
        refs[:shards],
        refs[shards : shards + 6],
        refs[shards + 6 :],
    )

    @pl.when(at_work(place_ref, step, micro))
    def _():
        x = jnp.concatenate([x_ref[...] for x_ref in x_refs], axis=0).astype(jnp.float32)
        rows = x.shape[0]

        def block_and_hour(dimension):
            late, patch, offset = digits((rows, rows), dimension, hl, patches)
            return ((offset ^ place_ref[1]) * patches + patch) // PB, late

        query_block, query_hour = block_and_hour(0)
        key_block, key_hour = block_and_hour(1)
        seen = None
        for kv in range(seen_ref.shape[1]):
            chosen = jnp.full((rows, rows), seen_ref[0, kv], jnp.int32)
            for b in range(1, seen_ref.shape[0]):
                chosen = jnp.where(query_block == b, seen_ref[b, kv], chosen)
            hit = jnp.where(chosen == key_block, 1.0, 0.0)
            seen = hit if seen is None else jnp.maximum(seen, hit)
        mask = jnp.where(query_hour == key_hour, seen, 0.0).astype(jnp.bfloat16)
        update = attention_update(
            x,
            [],
            gain_ref[0, 1:2, :],
            lambda n: scale_ref[0, 1, n],
            w_in_ref.at[0, 1],
            w_out_ref.at[0, 1],
            mask,
        )
        x = rounded(x + update)
        normed = row_norm(x, gain_ref[0, 2:3, :])
        total = x
        width = 512
        for start in range(0, up_ref.shape[2], width):
            u = matmul(normed, up_ref[0, :, start : start + width])
            bent = jnp.tanh(u * (0.7978845608028654 + 0.035677408136300125 * (u * u)))
            hidden = (0.5 * u * (1.0 + bent)).astype(jnp.bfloat16)
            total = total + matmul(hidden, down_ref[0, start : start + width, :])
        y = total.astype(jnp.bfloat16)
        size = rows // shards
        for k in range(shards):
            y_refs[k][...] = y[k * size : (k + 1) * size]


def final_kernel(sizes, micro, place_ref, *refs):
    shards, _, patches, hl = sizes
    y_ref = refs[-1]
    rows = shards * patches * hl
    late, shard, patch = digits((rows, rows), 0, hl, shards)
    source = lax.broadcasted_iota(jnp.int32, (rows, rows), 1)
    wanted = ((shard ^ place_ref[1]) * patches + patch) * hl + late
    order = jnp.where(wanted == source, 1.0, 0.0).astype(jnp.bfloat16)
    for hops in range(len(refs) // micro):

        @pl.when(place_ref[0] == hops)
        def _():
            for m in range(micro):
                y_ref[m] = matmul(order, refs[hops * micro + m][...]).astype(jnp.bfloat16)


VMEM = pl.BlockSpec(memory_space=pltpu.VMEM)
SMEM = pl.BlockSpec(memory_space=pltpu.SMEM)
HBM = pl.BlockSpec(memory_space=pltpu.HBM)
PARAMS = pltpu.CompilerParams(vmem_limit_bytes=32 << 20)
FULL = pltpu.CompilerParams(vmem_limit_bytes=61 << 20)
COST = pl.CostEstimate(flops=5 << 30, bytes_accessed=1 << 20, transcendentals=1 << 20)


def blocks_of(count, rows, width):
    return [jax.ShapeDtypeStruct((rows // count, width), jnp.bfloat16)] * count


def call_time(sizes, step, micro, place, given, came, gains, scales, w_in, w_out):
    rows, width = given[0].shape[1:] if given else came[0].shape
    xs = list(given) + list(came)
    scratch = [pltpu.VMEM((rows * sizes[1], width), jnp.bfloat16)]
    weights = [VMEM, VMEM]
    if step == 0:
        weights = [HBM, HBM]
        scratch += [
            pltpu.VMEM((width, 3 * width), jnp.bfloat16),
            pltpu.VMEM((width, width), jnp.bfloat16),
            pltpu.SemaphoreType.DMA((2,)),
        ]
    return pl.pallas_call(
        functools.partial(time_kernel, sizes, step, micro),
        out_shape=blocks_of(sizes[0], rows, width),
        in_specs=[SMEM] + [VMEM] * len(xs) + [VMEM, SMEM] + weights,
        out_specs=[VMEM] * sizes[0],
        scratch_shapes=scratch,
        compiler_params=PARAMS if step else FULL,
        cost_estimate=COST,
        name="time_attention",
    )(place, *xs, gains, scales, w_in, w_out)


def call_patch(sizes, step, micro, place, seen, xs, gains, scales, w_in, w_out, w_up, w_down):
    rows, width = xs[0].shape
    return pl.pallas_call(
        functools.partial(patch_kernel, sizes, step, micro),
        out_shape=blocks_of(sizes[0], rows * sizes[0], width),
        in_specs=[SMEM, SMEM] + [VMEM] * len(xs) + [VMEM, SMEM] + [VMEM] * 4,
        out_specs=[VMEM] * sizes[0],
        compiler_params=PARAMS,
        cost_estimate=COST,
        name="patch_attention_and_ffn",
    )(place, seen, *xs, gains, scales, w_in, w_out, w_up, w_down)


def call_final(sizes, place, shape, parts):
    micro, rows, width = shape
    return pl.pallas_call(
        functools.partial(final_kernel, sizes, micro),
        out_shape=jax.ShapeDtypeStruct((micro, rows, width), jnp.bfloat16),
        in_specs=[SMEM] + [VMEM] * len(parts),
        out_specs=VMEM,
        compiler_params=PARAMS,
        name="final_order",
    )(place, *parts)


def flipped(x, axis, k):
    return lax.ppermute(x, axis, [(s, s ^ k) for s in range(lax.axis_size(axis))])


def handed_on(x, k):
    pipes, shards = lax.axis_size("pipe"), lax.axis_size("patch")
    pairs = [
        (stage * shards + s, (stage + 1) % pipes * shards + (s ^ k))
        for stage in range(pipes)
        for s in range(shards)
    ]
    return lax.ppermute(x, ("pipe", "patch"), pairs)


def local(inputs, seen, gains, scales, w_in, w_out, w_up, w_down):
    shards = lax.axis_size("patch")
    peers = lax.axis_size("hour")
    pipes = lax.axis_size("pipe")
    micro, patches, hours, width = inputs.shape
    rows = patches * hours
    sizes = (shards, peers, patches, hours // shards)
    place = jnp.stack([lax.axis_index("pipe"), lax.axis_index("patch")])

    def with_peers(x):
        return [x] + [flipped(x, "hour", j) for j in range(1, peers)]

    given = with_peers(inputs.reshape(micro, rows, width))
    came = []
    finished = []
    for step in range(micro + pipes - 1):
        if step > 0:
            came = with_peers(arrived)
        now = given if step < micro else []
        mixed = call_time(sizes, step, micro, place, now, came, gains, scales, w_in, w_out)
        spread = [mixed[0]] + [flipped(mixed[k], "patch", k) for k in range(1, shards)]
        done = call_patch(
            sizes, step, micro, place, seen, spread, gains, scales, w_in, w_out, w_up, w_down
        )
        arrived = jnp.concatenate([handed_on(done[k], k) for k in range(shards)])
        if step >= pipes - 1:
            finished.append(arrived)
    parts = list(finished)
    for _ in range(1, pipes):
        finished = [
            lax.ppermute(x, "pipe", [(s, (s + 1) % pipes) for s in range(pipes)]) for x in finished
        ]
        parts += finished
    return call_final(sizes, place, (micro, rows, width), parts).reshape(inputs.shape)


def solution(mesh):
    placed = (
        P(None, "patch", "hour", None),
        P(),
        P("pipe", None, None),
        P("pipe", None, None),
        P("pipe", None, None, None),
        P("pipe", None, None, None),
        P("pipe", None, None),
        P("pipe", None, None),
    )
    return jax.shard_map(
        local, mesh=mesh, in_specs=placed, out_specs=P(None, "patch", "hour", None), check_vma=False
    )
```

```python
import functools

import jax
import jax.numpy as jnp
from jax import lax
from jax.experimental import pallas as pl
from jax.experimental.pallas import tpu as pltpu
from jax.sharding import PartitionSpec as P

HEADS = 8
HEAD_DIM = 64
PB = 64
LOG2E = 1.4426950408889634


def row_norm(x, gain):
    factor = lax.rsqrt(jnp.mean(x * x, axis=-1, keepdims=True) + 1e-05)
    return (x * factor * gain).astype(jnp.bfloat16)


def matmul(a, b):
    return jnp.dot(a, b, preferred_element_type=jnp.float32)


def same_head():
    rows = lax.broadcasted_iota(jnp.int32, (256, 256), 0) // HEAD_DIM
    cols = lax.broadcasted_iota(jnp.int32, (256, 256), 1) // HEAD_DIM
    return jnp.where(rows == cols, 1.0, 0.0).astype(jnp.bfloat16)


def head_factor(values, group):
    squares = (values * values).astype(jnp.bfloat16)
    halves = [
        matmul(squares[:, start : start + 256], group) for start in range(0, values.shape[1], 256)
    ]
    sums = jnp.concatenate(halves, axis=1)
    return lax.rsqrt(sums * (1.0 / HEAD_DIM) + 1e-06)


def attention_update(x, more, gain, scale_of, w_in, w_out, mask):
    width = x.shape[1]
    normed = row_norm(x, gain)
    seen = jnp.concatenate([normed] + [row_norm(t, gain) for t in more], axis=0)
    group = same_head()
    head = lax.broadcasted_iota(jnp.int32, (1, width), 1) // HEAD_DIM
    scale = jnp.zeros((1, width), jnp.float32)
    for n in range(HEADS):
        scale = jnp.where(head == n, scale_of(n) * (LOG2E / HEAD_DIM), scale)
    q = matmul(normed, w_in[:, :width])
    k = matmul(seen, w_in[:, width : 2 * width])
    v = matmul(seen, w_in[:, 2 * width :]).astype(jnp.bfloat16)
    q = (q * head_factor(q, group) * scale).astype(jnp.bfloat16)
    k = (k * head_factor(k, group)).astype(jnp.bfloat16)
    pair = 2 * HEAD_DIM
    first = lax.broadcasted_iota(jnp.int32, (1, pair), 1) < HEAD_DIM
    low = jnp.where(first, 1.0, 0.0).astype(jnp.bfloat16)
    high = jnp.where(first, 0.0, 1.0).astype(jnp.bfloat16)
    low_all = jnp.broadcast_to(low, (k.shape[0], pair))
    high_all = jnp.broadcast_to(high, (k.shape[0], pair))
    parts = []
    for start in range(0, width, pair):
        q2, k2, v2 = (t[:, start : start + pair] for t in (q, k, v))
        powers = []
        for side in (low, high):
            scores = lax.dot_general(
                q2 * side, k2, (((1,), (1,)), ((), ())), preferred_element_type=jnp.float32
            )
            powers.append(jnp.exp2(scores).astype(jnp.bfloat16) * mask)
        powers = jnp.concatenate(powers, axis=1)
        upper = jnp.concatenate([v2 * low, low_all], axis=1)
        lower = jnp.concatenate([v2 * high, high_all], axis=1)
        sums = matmul(powers, jnp.concatenate([upper, lower], axis=0))
        parts.append((sums[:, :pair] / sums[:, pair:]).astype(jnp.bfloat16))
    return matmul(jnp.concatenate(parts, axis=1), w_out[...])


def rounded(x):
    return x.astype(jnp.bfloat16).astype(jnp.float32)


def digits(shape, dimension, *bases):
    index = lax.broadcasted_iota(jnp.int32, shape, dimension)
    out = []
    for base in bases:
        out.append(index % base)
        index = index // base
    return out + [index]


def at_work(place_ref, step, micro):
    number = step - place_ref[0]
    return jnp.logical_and(number >= 0, number < micro)


def time_kernel(sizes, step, micro, place_ref, *refs):
    shards, peers, patches, hl = sizes
    given = peers if step < micro else 0
    came = peers if step > 0 else 0
    input_refs, refs = refs[:given], refs[given:]
    came_refs, refs = refs[:came], refs[came:]
    (gain_ref, scale_ref, w_in_ref, w_out_ref), refs = refs[:4], refs[4:]
    y_refs, refs = refs[:shards], refs[shards:]
    x_ref = refs[0]
    rows = x_ref.shape[0] // peers

    @pl.when(at_work(place_ref, step, micro))
    def _():
        if given:

            @pl.when(place_ref[0] == 0)
            def _():
                late, patch, offset = digits((rows, rows), 0, hl, patches)
                source = lax.broadcasted_iota(jnp.int32, (rows, rows), 1)
                wanted = (patch * shards + (offset ^ place_ref[1])) * hl + late
                order = jnp.where(wanted == source, 1.0, 0.0).astype(jnp.bfloat16)
                for j, ref in enumerate(input_refs):
                    moved = matmul(order, ref[step]).astype(jnp.bfloat16)
                    x_ref[j * rows : (j + 1) * rows, :] = moved

        if came:

            @pl.when(place_ref[0] != 0)
            def _():
                for j, ref in enumerate(came_refs):
                    x_ref[j * rows : (j + 1) * rows, :] = ref[...]

        x = x_ref[...].astype(jnp.float32)
        mine = digits((rows, rows * peers), 0, hl, patches)[1]
        theirs = digits((rows, rows * peers), 1, hl, patches)[1]
        mask = jnp.where(mine == theirs, 1.0, 0.0).astype(jnp.bfloat16)
        update = attention_update(
            x[:rows],
            [x[rows:]],
            gain_ref[0, 0:1, :],
            lambda n: scale_ref[0, 0, n],
            w_in_ref.at[0, 0],
            w_out_ref.at[0, 0],
            mask,
        )
        y = (x[:rows] + update).astype(jnp.bfloat16)
        size = rows // shards
        for k in range(shards):
            y_refs[k][...] = y[k * size : (k + 1) * size]


def patch_kernel(sizes, step, micro, place_ref, seen_ref, *refs):
    slow, _, patches, hl = sizes
    fast = len(refs) - 6 - slow
    x_refs, (gain_ref, scale_ref, w_in_ref, w_out_ref, up_ref, down_ref), y_refs = (
        refs[:fast],
        refs[fast : fast + 6],
        refs[fast + 6 :],
    )

    @pl.when(at_work(place_ref, step, micro))
    def _():
        xs = [x_ref[...].astype(jnp.float32) for x_ref in x_refs]
        x = xs[0]
        rows = x.shape[0]
        shape = (rows, rows * fast)

        def block_and_hour(dimension):
            late, patch, offset, other = digits(shape, dimension, hl, patches, slow)
            shard = (offset ^ place_ref[1]) * fast + (other ^ place_ref[2])
            return (shard * patches + patch) // PB, late

        query_block, query_hour = block_and_hour(0)
        key_block, key_hour = block_and_hour(1)
        seen = None
        for kv in range(seen_ref.shape[1]):
            chosen = jnp.full(shape, seen_ref[0, kv], jnp.int32)
            for b in range(1, seen_ref.shape[0]):
                chosen = jnp.where(query_block == b, seen_ref[b, kv], chosen)
            hit = jnp.where(chosen == key_block, 1.0, 0.0)
            seen = hit if seen is None else jnp.maximum(seen, hit)
        mask = jnp.where(query_hour == key_hour, seen, 0.0).astype(jnp.bfloat16)
        update = attention_update(
            x,
            xs[1:],
            gain_ref[0, 1:2, :],
            lambda n: scale_ref[0, 1, n],
            w_in_ref.at[0, 1],
            w_out_ref.at[0, 1],
            mask,
        )
        x = rounded(x + update)
        normed = row_norm(x, gain_ref[0, 2:3, :])
        total = x
        chunk = 512
        for start in range(0, up_ref.shape[2], chunk):
            u = matmul(normed, up_ref[0, :, start : start + chunk])
            bent = jnp.tanh(u * (0.7978845608028654 + 0.035677408136300125 * (u * u)))
            hidden = (0.5 * u * (1.0 + bent)).astype(jnp.bfloat16)
            total = total + matmul(hidden, down_ref[0, start : start + chunk, :])
        y = total.astype(jnp.bfloat16)
        size = rows // slow
        for k in range(slow):
            y_refs[k][...] = y[k * size : (k + 1) * size]


def final_kernel(sizes, micro, place_ref, *refs):
    shards, _, patches, hl = sizes
    y_ref = refs[-1]
    rows = shards * patches * hl
    late, shard, patch = digits((rows, rows), 0, hl, shards)
    source = lax.broadcasted_iota(jnp.int32, (rows, rows), 1)
    wanted = ((shard ^ place_ref[1]) * patches + patch) * hl + late
    order = jnp.where(wanted == source, 1.0, 0.0).astype(jnp.bfloat16)
    for hops in range(len(refs) // micro):

        @pl.when(place_ref[0] == hops)
        def _():
            for m in range(micro):
                y_ref[m] = matmul(order, refs[hops * micro + m][...]).astype(jnp.bfloat16)


VMEM = pl.BlockSpec(memory_space=pltpu.VMEM)
SMEM = pl.BlockSpec(memory_space=pltpu.SMEM)
PARAMS = pltpu.CompilerParams(vmem_limit_bytes=32 << 20)
COST = pl.CostEstimate(flops=5 << 30, bytes_accessed=1 << 20, transcendentals=1 << 20)


def blocks_of(count, rows, width):
    return [jax.ShapeDtypeStruct((rows // count, width), jnp.bfloat16)] * count


def call_time(sizes, step, micro, place, given, came, gains, scales, w_in, w_out):
    rows, width = given[0].shape[1:] if given else came[0].shape
    xs = list(given) + list(came)
    return pl.pallas_call(
        functools.partial(time_kernel, sizes, step, micro),
        out_shape=blocks_of(sizes[0], rows, width),
        in_specs=[SMEM] + [VMEM] * len(xs) + [VMEM, SMEM, VMEM, VMEM],
        out_specs=[VMEM] * sizes[0],
        scratch_shapes=[pltpu.VMEM((rows * sizes[1], width), jnp.bfloat16)],
        compiler_params=PARAMS,
        cost_estimate=COST,
        name="time_attention",
    )(place, *xs, gains, scales, w_in, w_out)


def call_patch(sizes, step, micro, place, seen, xs, gains, scales, w_in, w_out, w_up, w_down):
    rows, width = xs[0].shape
    return pl.pallas_call(
        functools.partial(patch_kernel, sizes, step, micro),
        out_shape=blocks_of(sizes[0], rows, width),
        in_specs=[SMEM, SMEM] + [VMEM] * len(xs) + [VMEM, SMEM] + [VMEM] * 4,
        out_specs=[VMEM] * sizes[0],
        compiler_params=PARAMS,
        cost_estimate=COST,
        name="patch_attention_and_ffn",
    )(place, seen, *xs, gains, scales, w_in, w_out, w_up, w_down)


def call_final(sizes, place, shape, parts):
    micro, rows, width = shape
    return pl.pallas_call(
        functools.partial(final_kernel, sizes, micro),
        out_shape=jax.ShapeDtypeStruct((micro, rows, width), jnp.bfloat16),
        in_specs=[SMEM] + [VMEM] * len(parts),
        out_specs=VMEM,
        compiler_params=PARAMS,
        name="final_order",
    )(place, *parts)


def flipped(x, axis, k):
    return lax.ppermute(x, axis, [(s, s ^ k) for s in range(lax.axis_size(axis))])


def handed_on(x, k):
    pipes, shards = lax.axis_size("pipe"), lax.axis_size("patch")
    pairs = [
        (stage * shards + s, (stage + 1) % pipes * shards + (s ^ k))
        for stage in range(pipes)
        for s in range(shards)
    ]
    return lax.ppermute(x, ("pipe", "patch"), pairs)


def local(inputs, seen, gains, scales, w_in, w_out, w_up, w_down):
    shards = lax.axis_size("patch")
    peers = lax.axis_size("hour")
    pipes = lax.axis_size("pipe")
    micro, patches, hours, width = inputs.shape
    rows = patches * hours
    fast = 2
    slow = shards // fast
    sizes = (slow, peers, patches, hours // slow)
    shard = lax.axis_index("patch")
    place = jnp.stack([lax.axis_index("pipe"), lax.div(shard, fast), lax.rem(shard, fast)])
    order = sorted(range(slow), key=lambda k: (k < slow // 2, k))

    def with_others(x, axis, count):
        return [x] + [flipped(x, axis, j) for j in range(1, count)]

    def along_slow(blocks, send, first):
        got = {k: send(blocks[k], k * fast) for k in order if k >= first}
        return jnp.concatenate([got.get(k, blocks[k]) for k in range(slow)])

    def onward(x):
        return lax.ppermute(x, "pipe", [(s, (s + 1) % pipes) for s in range(pipes)])

    given = with_others(inputs.reshape(micro, rows, width), "hour", peers)
    came = []
    finished = []
    back = []
    for step in range(micro + pipes - 1):
        if step > 0:
            came = with_others(arrived, "hour", peers)
        now = given if step < micro else []
        mixed = call_time(sizes, step, micro, place, now, came, gains, scales, w_in, w_out)
        own = along_slow(mixed, lambda x, k: flipped(x, "patch", k), 1)
        spread = with_others(own, "patch", fast)
        if back:
            spread, back = lax.optimization_barrier((spread, back))
            finished[-1][1:] = back
        done = call_patch(
            sizes, step, micro, place, seen, spread, gains, scales, w_in, w_out, w_up, w_down
        )
        arrived = along_slow(done, handed_on, 0)
        back = []
        if step >= pipes - 1:
            for _ in range(1, pipes):
                back.append(onward(back[-1] if back else arrived))
            finished.append([arrived] + back)
    parts = [copies[hops] for hops in range(pipes) for copies in finished]
    return call_final(sizes, place, (micro, rows, width), parts).reshape(inputs.shape)


def solution(mesh):
    placed = (
        P(None, "patch", "hour", None),
        P(),
        P("pipe", None, None),
        P("pipe", None, None),
        P("pipe", None, None, None),
        P("pipe", None, None, None),
        P("pipe", None, None),
        P("pipe", None, None),
    )
    return jax.shard_map(
        local, mesh=mesh, in_specs=placed, out_specs=P(None, "patch", "hour", None), check_vma=False
    )
```

```python
import functools

import jax
import jax.numpy as jnp
from jax import lax
from jax.experimental import pallas as pl
from jax.experimental.pallas import tpu as pltpu
from jax.sharding import PartitionSpec as P

HEADS = 8
HEAD_DIM = 64
PB = 64
LOG2E = 1.4426950408889634


def row_norm(x, gain):
    factor = lax.rsqrt(jnp.mean(x * x, axis=-1, keepdims=True) + 1e-05)
    return (x * factor * gain).astype(jnp.bfloat16)


def matmul(a, b):
    return jnp.dot(a, b, preferred_element_type=jnp.float32)


def same_head():
    rows = lax.broadcasted_iota(jnp.int32, (256, 256), 0) // HEAD_DIM
    cols = lax.broadcasted_iota(jnp.int32, (256, 256), 1) // HEAD_DIM
    return jnp.where(rows == cols, 1.0, 0.0).astype(jnp.bfloat16)


def head_factor(values, group):
    squares = (values * values).astype(jnp.bfloat16)
    halves = [
        matmul(squares[:, start : start + 256], group) for start in range(0, values.shape[1], 256)
    ]
    sums = jnp.concatenate(halves, axis=1)
    return lax.rsqrt(sums * (1.0 / HEAD_DIM) + 1e-06)


def attention_update(x, more, gain, scale_of, w_in, w_out, mask):
    width = x.shape[1]
    normed = row_norm(x, gain)
    seen = jnp.concatenate([normed] + [row_norm(t, gain) for t in more], axis=0)
    group = same_head()
    head = lax.broadcasted_iota(jnp.int32, (1, width), 1) // HEAD_DIM
    scale = jnp.zeros((1, width), jnp.float32)
    for n in range(HEADS):
        scale = jnp.where(head == n, scale_of(n) * (LOG2E / HEAD_DIM), scale)
    q = matmul(normed, w_in[:, :width])
    k = matmul(seen, w_in[:, width : 2 * width])
    v = matmul(seen, w_in[:, 2 * width :]).astype(jnp.bfloat16)
    q = (q * head_factor(q, group) * scale).astype(jnp.bfloat16)
    k = (k * head_factor(k, group)).astype(jnp.bfloat16)
    pair = 2 * HEAD_DIM
    first = lax.broadcasted_iota(jnp.int32, (1, pair), 1) < HEAD_DIM
    low = jnp.where(first, 1.0, 0.0).astype(jnp.bfloat16)
    high = jnp.where(first, 0.0, 1.0).astype(jnp.bfloat16)
    low_all = jnp.broadcast_to(low, (k.shape[0], pair))
    high_all = jnp.broadcast_to(high, (k.shape[0], pair))
    parts = []
    for start in range(0, width, pair):
        q2, k2, v2 = (t[:, start : start + pair] for t in (q, k, v))
        powers = []
        for side in (low, high):
            scores = lax.dot_general(
                q2 * side, k2, (((1,), (1,)), ((), ())), preferred_element_type=jnp.float32
            )
            powers.append(jnp.exp2(scores).astype(jnp.bfloat16) * mask)
        powers = jnp.concatenate(powers, axis=1)
        upper = jnp.concatenate([v2 * low, low_all], axis=1)
        lower = jnp.concatenate([v2 * high, high_all], axis=1)
        sums = matmul(powers, jnp.concatenate([upper, lower], axis=0))
        parts.append((sums[:, :pair] / sums[:, pair:]).astype(jnp.bfloat16))
    return matmul(jnp.concatenate(parts, axis=1), w_out[...])


def rounded(x):
    return x.astype(jnp.bfloat16).astype(jnp.float32)


def digits(shape, dimension, *bases):
    index = lax.broadcasted_iota(jnp.int32, shape, dimension)
    out = []
    for base in bases:
        out.append(index % base)
        index = index // base
    return out + [index]


def at_work(place_ref, step, micro):
    number = step - place_ref[0]
    return jnp.logical_and(number >= 0, number < micro)


def time_kernel(sizes, step, micro, place_ref, *refs):
    shards, peers, patches, hl = sizes
    given = peers if step < micro else 0
    came = peers * shards if step > 0 else 0
    input_refs, refs = refs[:given], refs[given:]
    came_refs, refs = refs[:came], refs[came:]
    (gain_ref, scale_ref, w_in_ref, w_out_ref), refs = refs[:4], refs[4:]
    y_refs, refs = refs[:shards], refs[shards:]
    x_ref = refs[0]
    rows = x_ref.shape[0] // peers

    @pl.when(at_work(place_ref, step, micro))
    def _():
        if given:

            @pl.when(place_ref[0] == 0)
            def _():
                late, patch, offset = digits((rows, rows), 0, hl, patches)
                source = lax.broadcasted_iota(jnp.int32, (rows, rows), 1)
                wanted = (patch * shards + (offset ^ place_ref[1])) * hl + late
                order = jnp.where(wanted == source, 1.0, 0.0).astype(jnp.bfloat16)
                for j, ref in enumerate(input_refs):
                    moved = matmul(order, ref[step]).astype(jnp.bfloat16)
                    x_ref[j * rows : (j + 1) * rows, :] = moved

        if came:

            @pl.when(place_ref[0] != 0)
            def _():
                for j, ref in enumerate(came_refs):
                    size = rows // shards
                    x_ref[j * size : (j + 1) * size, :] = ref[...]

        x = x_ref[...].astype(jnp.float32)
        mine = digits((rows, rows * peers), 0, hl, patches)[1]
        theirs = digits((rows, rows * peers), 1, hl, patches)[1]
        mask = jnp.where(mine == theirs, 1.0, 0.0).astype(jnp.bfloat16)
        update = attention_update(
            x[:rows],
            [x[rows:]],
            gain_ref[0, 0:1, :],
            lambda n: scale_ref[0, 0, n],
            w_in_ref.at[0, 0],
            w_out_ref.at[0, 0],
            mask,
        )
        y = (x[:rows] + update).astype(jnp.bfloat16)
        size = rows // shards
        for k in range(shards):
            y_refs[k][...] = y[k * size : (k + 1) * size]


def patch_kernel(sizes, step, micro, outs, place_ref, seen_ref, *refs):
    slow, _, patches, hl = sizes
    count = len(refs) - 6 - outs
    fast = count // slow
    x_refs, (gain_ref, scale_ref, w_in_ref, w_out_ref, up_ref, down_ref), y_refs = (
        refs[:count],
        refs[count : count + 6],
        refs[count + 6 :],
    )

    @pl.when(at_work(place_ref, step, micro))
    def _():
        xs = [
            jnp.concatenate([ref[...] for ref in x_refs[i : i + slow]], axis=0).astype(jnp.float32)
            for i in range(0, count, slow)
        ]
        x = xs[0]
        rows = x.shape[0]
        shape = (rows, rows * fast)

        def block_and_hour(dimension):
            late, patch, offset, other = digits(shape, dimension, hl, patches, slow)
            shard = (offset ^ place_ref[1]) * fast + (other ^ place_ref[2])
            return (shard * patches + patch) // PB, late

        query_block, query_hour = block_and_hour(0)
        key_block, key_hour = block_and_hour(1)
        seen = None
        for kv in range(seen_ref.shape[1]):
            chosen = jnp.full(shape, seen_ref[0, kv], jnp.int32)
            for b in range(1, seen_ref.shape[0]):
                chosen = jnp.where(query_block == b, seen_ref[b, kv], chosen)
            hit = jnp.where(chosen == key_block, 1.0, 0.0)
            seen = hit if seen is None else jnp.maximum(seen, hit)
        mask = jnp.where(query_hour == key_hour, seen, 0.0).astype(jnp.bfloat16)
        update = attention_update(
            x,
            xs[1:],
            gain_ref[0, 1:2, :],
            lambda n: scale_ref[0, 1, n],
            w_in_ref.at[0, 1],
            w_out_ref.at[0, 1],
            mask,
        )
        x = rounded(x + update)
        normed = row_norm(x, gain_ref[0, 2:3, :])
        total = x
        chunk = 512
        for start in range(0, up_ref.shape[2], chunk):
            u = matmul(normed, up_ref[0, :, start : start + chunk])
            bent = jnp.tanh(u * (0.7978845608028654 + 0.035677408136300125 * (u * u)))
            hidden = (0.5 * u * (1.0 + bent)).astype(jnp.bfloat16)
            total = total + matmul(hidden, down_ref[0, start : start + chunk, :])
        y = total.astype(jnp.bfloat16)
        size = rows // outs
        for k in range(outs):
            y_refs[k][...] = y[k * size : (k + 1) * size]


def pick_kernel(slow, last, place_ref, *refs):
    x_refs, y_refs = refs[:-slow], refs[-slow:]
    size = x_refs[0].shape[0] // slow
    for hops, x_ref in enumerate(x_refs):

        @pl.when(place_ref[0] == (last + hops) % len(x_refs))
        def _():
            for k, y_ref in enumerate(y_refs):
                y_ref[...] = x_ref[k * size : (k + 1) * size, :]


def final_kernel(sizes, early, place_ref, *refs):
    slow, _, patches, hl = sizes
    y_ref = refs[-1]
    block_refs = refs[-1 - slow : -1]
    rows = slow * patches * hl
    late, shard, patch = digits((rows, rows), 0, hl, slow)
    source = lax.broadcasted_iota(jnp.int32, (rows, rows), 1)
    wanted = ((shard ^ place_ref[1]) * patches + patch) * hl + late
    order = jnp.where(wanted == source, 1.0, 0.0).astype(jnp.bfloat16)
    if early:
        for stage in range((len(refs) - 1 - slow) // early):

            @pl.when(place_ref[0] == stage)
            def _():
                for m in range(early):
                    y_ref[m] = matmul(order, refs[stage * early + m][...]).astype(jnp.bfloat16)

    x = jnp.concatenate([ref[...] for ref in block_refs], axis=0)
    y_ref[early] = matmul(order, x).astype(jnp.bfloat16)


VMEM = pl.BlockSpec(memory_space=pltpu.VMEM)
SMEM = pl.BlockSpec(memory_space=pltpu.SMEM)
PARAMS = pltpu.CompilerParams(vmem_limit_bytes=32 << 20)
COST = pl.CostEstimate(flops=5 << 30, bytes_accessed=1 << 20, transcendentals=1 << 20)


def blocks_of(count, rows, width):
    return [jax.ShapeDtypeStruct((rows // count, width), jnp.bfloat16)] * count


def call_time(sizes, step, micro, place, given, came, gains, scales, w_in, w_out):
    rows, width = given[0].shape[1:] if given else (sizes[0] * came[0].shape[0], came[0].shape[1])
    xs = list(given) + list(came)
    return pl.pallas_call(
        functools.partial(time_kernel, sizes, step, micro),
        out_shape=blocks_of(sizes[0], rows, width),
        in_specs=[SMEM] + [VMEM] * len(xs) + [VMEM, SMEM, VMEM, VMEM],
        out_specs=[VMEM] * sizes[0],
        scratch_shapes=[pltpu.VMEM((rows * sizes[1], width), jnp.bfloat16)],
        compiler_params=PARAMS,
        cost_estimate=COST,
        name="time_attention",
    )(place, *xs, gains, scales, w_in, w_out)


def call_patch(sizes, step, micro, outs, place, seen, xs, gains, scales, w_in, w_out, w_up, w_down):
    rows, width = sizes[0] * xs[0].shape[0], xs[0].shape[1]
    return pl.pallas_call(
        functools.partial(patch_kernel, sizes, step, micro, outs),
        out_shape=blocks_of(outs, rows, width),
        in_specs=[SMEM, SMEM] + [VMEM] * len(xs) + [VMEM, SMEM] + [VMEM] * 4,
        out_specs=[VMEM] * outs,
        compiler_params=PARAMS,
        cost_estimate=COST,
        name="patch_attention_and_ffn",
    )(place, seen, *xs, gains, scales, w_in, w_out, w_up, w_down)


def call_pick(slow, last, place, xs):
    rows, width = xs[0].shape
    return pl.pallas_call(
        functools.partial(pick_kernel, slow, last),
        out_shape=blocks_of(slow, rows, width),
        in_specs=[SMEM] + [VMEM] * len(xs),
        out_specs=[VMEM] * slow,
        compiler_params=PARAMS,
        name="pick",
    )(place, *xs)


def call_final(sizes, place, shape, parts):
    micro, rows, width = shape
    return pl.pallas_call(
        functools.partial(final_kernel, sizes, micro - 1),
        out_shape=jax.ShapeDtypeStruct((micro, rows, width), jnp.bfloat16),
        in_specs=[SMEM] + [VMEM] * len(parts),
        out_specs=VMEM,
        compiler_params=PARAMS,
        name="final_order",
    )(place, *parts)


def flipped(x, axis, k):
    return lax.ppermute(x, axis, [(s, s ^ k) for s in range(lax.axis_size(axis))])


def handed_on(x, k):
    pipes, shards = lax.axis_size("pipe"), lax.axis_size("patch")
    pairs = [
        (stage * shards + s, (stage + 1) % pipes * shards + (s ^ k))
        for stage in range(pipes)
        for s in range(shards)
    ]
    return lax.ppermute(x, ("pipe", "patch"), pairs)


def local(inputs, seen, gains, scales, w_in, w_out, w_up, w_down):
    shards = lax.axis_size("patch")
    peers = lax.axis_size("hour")
    pipes = lax.axis_size("pipe")
    micro, patches, hours, width = inputs.shape
    rows = patches * hours
    fast = 2
    slow = shards // fast
    sizes = (slow, peers, patches, hours // slow)
    last = pipes - 1
    shard = lax.axis_index("patch")
    place = jnp.stack([lax.axis_index("pipe"), lax.div(shard, fast), lax.rem(shard, fast)])
    order = sorted(range(slow), key=lambda k: (k < slow // 2, k))

    def gathered(blocks, axis, count):
        out = list(blocks)
        for j in range(1, count):
            got = {k: flipped(blocks[k], axis, j) for k in reversed(order)}
            out += [got[k] for k in range(len(blocks))]
        return out

    def along_slow(blocks, send, first):
        got = {k: send(blocks[k], k * fast) for k in order if k >= first}
        return [got.get(k, blocks[k]) for k in range(slow)]

    def in_stage(x, k):
        return flipped(x, "patch", k)

    def onward(x):
        return lax.ppermute(x, "pipe", [(s, (s + 1) % pipes) for s in range(pipes)])

    x = inputs.reshape(micro, rows, width)
    given = [x] + [flipped(x, "hour", j) for j in range(1, peers)]
    came = []
    early = []
    back = []
    for step in range(micro + pipes - 1):
        now = given if step < micro else []
        mixed = call_time(sizes, step, micro, place, now, came, gains, scales, w_in, w_out)
        own = along_slow(mixed, in_stage, 1)
        spread = gathered(own, "patch", fast)
        if back:
            spread, back = lax.optimization_barrier((spread, back))
            early.append(back)
        at_end = step == micro + pipes - 2
        outs = 1 if at_end else slow
        done = call_patch(
            sizes, step, micro, outs, place, seen, spread, gains, scales, w_in, w_out, w_up, w_down
        )
        if not at_end:
            arrived = along_slow(done, handed_on, 0)
            came = gathered(arrived, "hour", peers)
            if step >= last:
                back = [jnp.concatenate(arrived)]
                for _ in range(1, pipes):
                    back.append(onward(back[-1]))
    done = list(done)
    for _ in range(1, pipes):
        done.append(onward(done[-1]))
    blocks = along_slow(call_pick(slow, last, place, done), in_stage, 1)
    parts = [copies[stage] for stage in range(pipes) for copies in early] if early else []
    out = call_final(sizes, place, (micro, rows, width), parts + blocks)
    return out.reshape(inputs.shape)


def solution(mesh):
    placed = (
        P(None, "patch", "hour", None),
        P(),
        P("pipe", None, None),
        P("pipe", None, None),
        P("pipe", None, None, None),
        P("pipe", None, None, None),
        P("pipe", None, None),
        P("pipe", None, None),
    )
    return jax.shard_map(
        local, mesh=mesh, in_specs=placed, out_specs=P(None, "patch", "hour", None), check_vma=False
    )
```

```python
import functools

import jax
import jax.numpy as jnp
from jax import lax
from jax.experimental import pallas as pl
from jax.experimental.pallas import tpu as pltpu
from jax.sharding import PartitionSpec as P

HEADS = 8
HEAD_DIM = 64
PB = 64
LOG2E = 1.4426950408889634


def row_norm(x, gain):
    factor = lax.rsqrt(jnp.mean(x * x, axis=-1, keepdims=True) + 1e-05)
    return (x * factor * gain).astype(jnp.bfloat16)


def matmul(a, b):
    return jnp.dot(a, b, preferred_element_type=jnp.float32)


def same_head():
    rows = lax.broadcasted_iota(jnp.int32, (256, 256), 0) // HEAD_DIM
    cols = lax.broadcasted_iota(jnp.int32, (256, 256), 1) // HEAD_DIM
    return jnp.where(rows == cols, 1.0, 0.0).astype(jnp.bfloat16)


def head_factor(values, group):
    squares = (values * values).astype(jnp.bfloat16)
    halves = [
        matmul(squares[:, start : start + 256], group) for start in range(0, values.shape[1], 256)
    ]
    sums = jnp.concatenate(halves, axis=1)
    return lax.rsqrt(sums * (1.0 / HEAD_DIM) + 1e-06)


def regrouped(x, groups, inner):
    outer = x.shape[0] // (groups * inner)
    starts = [(o * groups + g) * inner for g in range(groups) for o in range(outer)]
    return jnp.concatenate([x[start : start + inner] for start in starts], axis=0)


def attention_update(xs, groups, gain, scale_of, w_in, w_out, mask):
    rows, width = xs[0].shape
    normed = row_norm(xs[0], gain)
    seen = jnp.concatenate([normed] + [row_norm(t, gain) for t in xs[1:]], axis=0)
    same = same_head()
    head = lax.broadcasted_iota(jnp.int32, (1, width), 1) // HEAD_DIM
    scale = jnp.zeros((1, width), jnp.float32)
    for n in range(HEADS):
        scale = jnp.where(head == n, scale_of(n) * (LOG2E / HEAD_DIM), scale)
    q = matmul(normed, w_in[:, :width])
    k = matmul(seen, w_in[:, width : 2 * width])
    v = matmul(seen, w_in[:, 2 * width :]).astype(jnp.bfloat16)
    q = (q * head_factor(q, same) * scale).astype(jnp.bfloat16)
    k = (k * head_factor(k, same)).astype(jnp.bfloat16)
    pair = 2 * HEAD_DIM
    size = rows // groups
    first = lax.broadcasted_iota(jnp.int32, (1, pair), 1) < HEAD_DIM
    low = jnp.where(first, 1.0, 0.0).astype(jnp.bfloat16)
    high = jnp.where(first, 0.0, 1.0).astype(jnp.bfloat16)
    keys = size * len(xs)
    low_all = jnp.broadcast_to(low, (keys, pair))
    high_all = jnp.broadcast_to(high, (keys, pair))
    done = []
    for g in range(groups):
        q_g = q[g * size : (g + 1) * size]
        spans = [slice(i * rows + g * size, i * rows + (g + 1) * size) for i in range(len(xs))]
        k_g = jnp.concatenate([k[span] for span in spans], axis=0)
        v_g = jnp.concatenate([v[span] for span in spans], axis=0)
        parts = []
        for start in range(0, width, pair):
            q2, k2, v2 = (t[:, start : start + pair] for t in (q_g, k_g, v_g))
            powers = []
            for side in (low, high):
                scores = lax.dot_general(
                    q2 * side, k2, (((1,), (1,)), ((), ())), preferred_element_type=jnp.float32
                )
                powers.append(jnp.exp2(scores).astype(jnp.bfloat16) * mask)
            powers = jnp.concatenate(powers, axis=1)
            upper = jnp.concatenate([v2 * low, low_all], axis=1)
            lower = jnp.concatenate([v2 * high, high_all], axis=1)
            sums = matmul(powers, jnp.concatenate([upper, lower], axis=0))
            parts.append((sums[:, :pair] / sums[:, pair:]).astype(jnp.bfloat16))
        done.append(jnp.concatenate(parts, axis=1))
    return matmul(jnp.concatenate(done, axis=0), w_out[...])


def rounded(x):
    return x.astype(jnp.bfloat16).astype(jnp.float32)


def digits(shape, dimension, *bases):
    index = lax.broadcasted_iota(jnp.int32, shape, dimension)
    out = []
    for base in bases:
        out.append(index % base)
        index = index // base
    return out + [index]


def at_work(place_ref, step, micro):
    number = step - place_ref[0]
    return jnp.logical_and(number >= 0, number < micro)


def time_kernel(sizes, step, micro, place_ref, *refs):
    shards, peers, patches, hl = sizes
    given = peers if step < micro else 0
    came = peers * shards if step > 0 else 0
    input_refs, refs = refs[:given], refs[given:]
    came_refs, refs = refs[:came], refs[came:]
    (gain_ref, scale_ref, w_in_ref, w_out_ref), refs = refs[:4], refs[4:]
    y_refs, refs = refs[:shards], refs[shards:]
    x_ref = refs[0]
    rows = x_ref.shape[0] // peers

    @pl.when(at_work(place_ref, step, micro))
    def _():
        if given:

            @pl.when(place_ref[0] == 0)
            def _():
                patch, late, offset = digits((rows, rows), 0, patches, hl)
                source = lax.broadcasted_iota(jnp.int32, (rows, rows), 1)
                wanted = (patch * shards + (offset ^ place_ref[1])) * hl + late
                order = jnp.where(wanted == source, 1.0, 0.0).astype(jnp.bfloat16)
                for j, ref in enumerate(input_refs):
                    moved = matmul(order, ref[step]).astype(jnp.bfloat16)
                    x_ref[j * rows : (j + 1) * rows, :] = moved

        if came:

            @pl.when(place_ref[0] != 0)
            def _():
                for j, ref in enumerate(came_refs):
                    size = rows // shards
                    x_ref[j * size : (j + 1) * size, :] = ref[...]

        inner = min(patches, 8)
        groups = patches // inner
        xs = [
            regrouped(x_ref[j * rows : (j + 1) * rows, :].astype(jnp.float32), groups, inner)
            for j in range(peers)
        ]
        shape = (rows // groups, rows // groups * peers)
        mine = digits(shape, 0, inner)[0]
        theirs = digits(shape, 1, inner)[0]
        mask = jnp.where(mine == theirs, 1.0, 0.0).astype(jnp.bfloat16)
        update = attention_update(
            xs,
            groups,
            gain_ref[0, 0:1, :],
            lambda n: scale_ref[0, 0, n],
            w_in_ref.at[0, 0],
            w_out_ref.at[0, 0],
            mask,
        )
        y = regrouped(xs[0] + update, rows // (groups * inner), inner).astype(jnp.bfloat16)
        size = rows // shards
        for k in range(shards):
            y_refs[k][...] = y[k * size : (k + 1) * size]


def patch_kernel(sizes, step, micro, outs, place_ref, seen_ref, *refs):
    slow, _, patches, hl = sizes
    count = len(refs) - 6 - outs
    fast = count // slow
    x_refs, (gain_ref, scale_ref, w_in_ref, w_out_ref, up_ref, down_ref), y_refs = (
        refs[:count],
        refs[count : count + 6],
        refs[count + 6 :],
    )

    @pl.when(at_work(place_ref, step, micro))
    def _():
        xs = [
            jnp.concatenate([ref[...] for ref in x_refs[i : i + slow]], axis=0).astype(jnp.float32)
            for i in range(0, count, slow)
        ]
        rows = xs[0].shape[0]
        groups = 2 if hl % 2 == 0 else 1
        inner = hl // groups * patches
        xs = [regrouped(x, groups, inner) for x in xs]
        x = xs[0]
        shape = (rows // groups, rows // groups * fast)

        def block_and_hour(dimension):
            patch, late, offset, other = digits(shape, dimension, patches, hl // groups, slow)
            shard = (offset ^ place_ref[1]) * fast + (other ^ place_ref[2])
            return (shard * patches + patch) // PB, late

        query_block, query_hour = block_and_hour(0)
        key_block, key_hour = block_and_hour(1)
        seen = None
        for kv in range(seen_ref.shape[1]):
            chosen = jnp.full(shape, seen_ref[0, kv], jnp.int32)
            for b in range(1, seen_ref.shape[0]):
                chosen = jnp.where(query_block == b, seen_ref[b, kv], chosen)
            hit = jnp.where(chosen == key_block, 1.0, 0.0)
            seen = hit if seen is None else jnp.maximum(seen, hit)
        mask = jnp.where(query_hour == key_hour, seen, 0.0).astype(jnp.bfloat16)
        update = attention_update(
            xs,
            groups,
            gain_ref[0, 1:2, :],
            lambda n: scale_ref[0, 1, n],
            w_in_ref.at[0, 1],
            w_out_ref.at[0, 1],
            mask,
        )
        x = rounded(x + update)
        normed = row_norm(x, gain_ref[0, 2:3, :])
        total = x
        chunk = 512
        for start in range(0, up_ref.shape[2], chunk):
            u = matmul(normed, up_ref[0, :, start : start + chunk])
            bent = jnp.tanh(u * (0.7978845608028654 + 0.035677408136300125 * (u * u)))
            hidden = (0.5 * u * (1.0 + bent)).astype(jnp.bfloat16)
            total = total + matmul(hidden, down_ref[0, start : start + chunk, :])
        y = regrouped(total, slow, inner).astype(jnp.bfloat16)
        size = rows // outs
        for k in range(outs):
            y_refs[k][...] = y[k * size : (k + 1) * size]


def pick_kernel(slow, last, place_ref, *refs):
    x_refs, y_refs = refs[:-slow], refs[-slow:]
    size = x_refs[0].shape[0] // slow
    for hops, x_ref in enumerate(x_refs):

        @pl.when(place_ref[0] == (last + hops) % len(x_refs))
        def _():
            for k, y_ref in enumerate(y_refs):
                y_ref[...] = x_ref[k * size : (k + 1) * size, :]


def write_rows(sizes, place_ref, x, y_ref):
    slow, _, patches, hl = sizes
    rows = slow * patches * hl
    late, shard, patch = digits((rows, rows), 0, hl, slow)
    source = lax.broadcasted_iota(jnp.int32, (rows, rows), 1)
    wanted = ((shard ^ place_ref[1]) * hl + late) * patches + patch
    order = jnp.where(wanted == source, 1.0, 0.0).astype(jnp.bfloat16)
    y_ref[...] = matmul(order, x).astype(jnp.bfloat16)


def early_kernel(sizes, pipes, place_ref, *refs):
    x_refs, y_ref = refs[:pipes], refs[-1]
    for stage, x_ref in enumerate(x_refs):

        @pl.when(place_ref[0] == stage)
        def _():
            write_rows(sizes, place_ref, x_ref[...], y_ref)


def final_kernel(sizes, place_ref, *refs):
    x_refs, y_ref = refs[: sizes[0]], refs[-1]
    write_rows(sizes, place_ref, jnp.concatenate([ref[...] for ref in x_refs], axis=0), y_ref)


VMEM = pl.BlockSpec(memory_space=pltpu.VMEM)
SMEM = pl.BlockSpec(memory_space=pltpu.SMEM)
PARAMS = pltpu.CompilerParams(vmem_limit_bytes=32 << 20)
COST = pl.CostEstimate(flops=5 << 30, bytes_accessed=1 << 20, transcendentals=1 << 20)


def blocks_of(count, rows, width):
    return [jax.ShapeDtypeStruct((rows // count, width), jnp.bfloat16)] * count


def call_time(sizes, step, micro, place, given, came, gains, scales, w_in, w_out):
    rows, width = given[0].shape[1:] if given else (sizes[0] * came[0].shape[0], came[0].shape[1])
    xs = list(given) + list(came)
    return pl.pallas_call(
        functools.partial(time_kernel, sizes, step, micro),
        out_shape=blocks_of(sizes[0], rows, width),
        in_specs=[SMEM] + [VMEM] * len(xs) + [VMEM, SMEM, VMEM, VMEM],
        out_specs=[VMEM] * sizes[0],
        scratch_shapes=[pltpu.VMEM((rows * sizes[1], width), jnp.bfloat16)],
        compiler_params=PARAMS,
        cost_estimate=COST,
        name="time_attention",
    )(place, *xs, gains, scales, w_in, w_out)


def call_patch(sizes, step, micro, outs, place, seen, xs, gains, scales, w_in, w_out, w_up, w_down):
    rows, width = sizes[0] * xs[0].shape[0], xs[0].shape[1]
    return pl.pallas_call(
        functools.partial(patch_kernel, sizes, step, micro, outs),
        out_shape=blocks_of(outs, rows, width),
        in_specs=[SMEM, SMEM] + [VMEM] * len(xs) + [VMEM, SMEM] + [VMEM] * 4,
        out_specs=[VMEM] * outs,
        compiler_params=PARAMS,
        cost_estimate=COST,
        name="patch_attention_and_ffn",
    )(place, seen, *xs, gains, scales, w_in, w_out, w_up, w_down)


def call_pick(slow, last, place, xs):
    rows, width = xs[0].shape
    return pl.pallas_call(
        functools.partial(pick_kernel, slow, last),
        out_shape=blocks_of(slow, rows, width),
        in_specs=[SMEM] + [VMEM] * len(xs),
        out_specs=[VMEM] * slow,
        compiler_params=PARAMS,
        name="pick",
    )(place, *xs)


def call_write(kernel, sizes, place, shape, number, xs, out):
    given = [] if out is None else [out]
    return pl.pallas_call(
        kernel,
        out_shape=jax.ShapeDtypeStruct(shape, jnp.bfloat16),
        grid=(1,),
        in_specs=[SMEM] + [VMEM] * len(xs) + [pl.BlockSpec(memory_space=pl.ANY)] * len(given),
        out_specs=pl.BlockSpec((None,) + shape[1:], lambda i: (number, 0, 0)),
        input_output_aliases={1 + len(xs): 0} if given else {},
        compiler_params=PARAMS,
        name="final_order",
    )(place, *xs, *given)


def flipped(x, axis, k):
    return lax.ppermute(x, axis, [(s, s ^ k) for s in range(lax.axis_size(axis))])


def handed_on(x, k):
    pipes, shards = lax.axis_size("pipe"), lax.axis_size("patch")
    pairs = [
        (stage * shards + s, (stage + 1) % pipes * shards + (s ^ k))
        for stage in range(pipes)
        for s in range(shards)
    ]
    return lax.ppermute(x, ("pipe", "patch"), pairs)


def local(inputs, seen, gains, scales, w_in, w_out, w_up, w_down):
    shards = lax.axis_size("patch")
    peers = lax.axis_size("hour")
    pipes = lax.axis_size("pipe")
    micro, patches, hours, width = inputs.shape
    rows = patches * hours
    fast = 2
    slow = shards // fast
    sizes = (slow, peers, patches, hours // slow)
    last = pipes - 1
    shard = lax.axis_index("patch")
    place = jnp.stack([lax.axis_index("pipe"), lax.div(shard, fast), lax.rem(shard, fast)])
    order = sorted(range(slow), key=lambda k: (k < slow // 2, k))

    def gathered(blocks, axis, count):
        out = list(blocks)
        for j in range(1, count):
            got = {k: flipped(blocks[k], axis, j) for k in reversed(order)}
            out += [got[k] for k in range(len(blocks))]
        return out

    def along_slow(blocks, send, first):
        got = {k: send(blocks[k], k * fast) for k in order if k >= first}
        return [got.get(k, blocks[k]) for k in range(slow)]

    def in_stage(x, k):
        return flipped(x, "patch", k)

    def onward(x):
        return lax.ppermute(x, "pipe", [(s, (s + 1) % pipes) for s in range(pipes)])

    x = inputs.reshape(micro, rows, width)
    given = [x] + [flipped(x, "hour", j) for j in range(1, peers)]
    came = []
    out = None
    back = []
    for step in range(micro + pipes - 1):
        now = given if step < micro else []
        mixed = call_time(sizes, step, micro, place, now, came, gains, scales, w_in, w_out)
        own = along_slow(mixed, in_stage, 1)
        spread = gathered(own, "patch", fast)
        if back:
            spread, back = lax.optimization_barrier((spread, back))
            write = functools.partial(early_kernel, sizes, pipes)
            out = call_write(write, sizes, place, x.shape, step - pipes, back, out)
        at_end = step == micro + pipes - 2
        outs = 1 if at_end else slow
        done = call_patch(
            sizes, step, micro, outs, place, seen, spread, gains, scales, w_in, w_out, w_up, w_down
        )
        if not at_end:
            arrived = along_slow(done, handed_on, 0)
            came = gathered(arrived, "hour", peers)
            if step >= last:
                back = [jnp.concatenate(arrived)]
                for _ in range(1, pipes):
                    back.append(onward(back[-1]))
    done = list(done)
    for _ in range(1, pipes):
        done.append(onward(done[-1]))
    blocks = along_slow(call_pick(slow, last, place, done), in_stage, 1)
    write = functools.partial(final_kernel, sizes)
    out = call_write(write, sizes, place, x.shape, micro - 1, blocks, out)
    return out.reshape(inputs.shape)


def solution(mesh):
    placed = (
        P(None, "patch", "hour", None),
        P(),
        P("pipe", None, None),
        P("pipe", None, None),
        P("pipe", None, None, None),
        P("pipe", None, None, None),
        P("pipe", None, None),
        P("pipe", None, None),
    )
    return jax.shard_map(
        local, mesh=mesh, in_specs=placed, out_specs=P(None, "patch", "hour", None), check_vma=False
    )
```

```python
import functools

import jax
import jax.numpy as jnp
from jax import lax
from jax.experimental import pallas as pl
from jax.experimental.pallas import tpu as pltpu
from jax.sharding import PartitionSpec as P

HEADS = 8
HEAD_DIM = 64
PB = 64
LOG2E = 1.4426950408889634


def row_norm(x, gain):
    factor = lax.rsqrt(jnp.mean(x * x, axis=-1, keepdims=True) + 1e-05)
    return (x * factor * gain).astype(jnp.bfloat16)


def matmul(a, b):
    return jnp.dot(a, b, preferred_element_type=jnp.float32)


def same_head():
    rows = lax.broadcasted_iota(jnp.int32, (256, 256), 0) // HEAD_DIM
    cols = lax.broadcasted_iota(jnp.int32, (256, 256), 1) // HEAD_DIM
    return jnp.where(rows == cols, 1.0, 0.0).astype(jnp.bfloat16)


def head_factor(values, group):
    squares = (values * values).astype(jnp.bfloat16)
    halves = [
        matmul(squares[:, start : start + 256], group) for start in range(0, values.shape[1], 256)
    ]
    sums = jnp.concatenate(halves, axis=1)
    return lax.rsqrt(sums * (1.0 / HEAD_DIM) + 1e-06)


def regrouped(x, groups, inner):
    outer = x.shape[0] // (groups * inner)
    starts = [(o * groups + g) * inner for g in range(groups) for o in range(outer)]
    return jnp.concatenate([x[start : start + inner] for start in starts], axis=0)


def attention_update(xs, groups, gain, scale_of, w_in, w_out, mask):
    rows, width = xs[0].shape
    normed = row_norm(xs[0], gain)
    seen = jnp.concatenate([normed] + [row_norm(t, gain) for t in xs[1:]], axis=0)
    same = same_head()
    head = lax.broadcasted_iota(jnp.int32, (1, width), 1) // HEAD_DIM
    scale = jnp.zeros((1, width), jnp.float32)
    for n in range(HEADS):
        scale = jnp.where(head == n, scale_of(n) * (LOG2E / HEAD_DIM), scale)
    q = matmul(normed, w_in[:, :width])
    k = matmul(seen, w_in[:, width : 2 * width])
    v = matmul(seen, w_in[:, 2 * width :]).astype(jnp.bfloat16)
    q = (q * head_factor(q, same) * scale).astype(jnp.bfloat16)
    k = (k * head_factor(k, same)).astype(jnp.bfloat16)
    pair = 2 * HEAD_DIM
    size = rows // groups
    first = lax.broadcasted_iota(jnp.int32, (1, pair), 1) < HEAD_DIM
    low = jnp.where(first, 1.0, 0.0).astype(jnp.bfloat16)
    high = jnp.where(first, 0.0, 1.0).astype(jnp.bfloat16)
    keys = size * len(xs)
    low_all = jnp.broadcast_to(low, (keys, pair))
    high_all = jnp.broadcast_to(high, (keys, pair))
    done = []
    for g in range(groups):
        q_g = q[g * size : (g + 1) * size]
        spans = [slice(i * rows + g * size, i * rows + (g + 1) * size) for i in range(len(xs))]
        k_g = jnp.concatenate([k[span] for span in spans], axis=0)
        v_g = jnp.concatenate([v[span] for span in spans], axis=0)
        parts = []
        for start in range(0, width, pair):
            q2, k2, v2 = (t[:, start : start + pair] for t in (q_g, k_g, v_g))
            powers = []
            for side in (low, high):
                scores = lax.dot_general(
                    q2 * side, k2, (((1,), (1,)), ((), ())), preferred_element_type=jnp.float32
                )
                powers.append(jnp.exp2(scores).astype(jnp.bfloat16) * mask)
            powers = jnp.concatenate(powers, axis=1)
            upper = jnp.concatenate([v2 * low, low_all], axis=1)
            lower = jnp.concatenate([v2 * high, high_all], axis=1)
            sums = matmul(powers, jnp.concatenate([upper, lower], axis=0))
            parts.append((sums[:, :pair] / sums[:, pair:]).astype(jnp.bfloat16))
        done.append(jnp.concatenate(parts, axis=1))
    return matmul(jnp.concatenate(done, axis=0), w_out[...])


def rounded(x):
    return x.astype(jnp.bfloat16).astype(jnp.float32)


def digits(shape, dimension, *bases):
    index = lax.broadcasted_iota(jnp.int32, shape, dimension)
    out = []
    for base in bases:
        out.append(index % base)
        index = index // base
    return out + [index]


def far_first(slow):
    return sorted(range(slow), key=lambda k: (k < slow // 2, k))


def pieces_of(sequence):
    half = len(sequence) // 2
    return [sequence[:half], sequence[half:]]


def row_sets(refs, slow, pieces):
    sets = []
    for start in range(0, len(refs), len(pieces)):
        found = {}
        for ref, piece in zip(refs[start : start + len(pieces)], pieces):
            size = ref.shape[0] // len(piece)
            for place, k in enumerate(piece):
                found[k] = ref[place * size : (place + 1) * size, :]
        sets.append([found[k] for k in range(slow)])
    return sets


def at_work(place_ref, step, micro):
    number = step - place_ref[0]
    return jnp.logical_and(number >= 0, number < micro)


def order_kernel(sizes, place_ref, order_ref):
    slow, _, patches, hl = sizes
    shape = order_ref.shape
    patch, late, offset = digits(shape, 0, patches, hl)
    source = lax.broadcasted_iota(jnp.int32, shape, 1)
    wanted = (patch * slow + (offset ^ place_ref[1])) * hl + late
    order_ref[...] = jnp.where(wanted == source, 1.0, 0.0).astype(jnp.bfloat16)


def time_kernel(sizes, step, micro, place_ref, *refs):
    shards, peers, patches, hl = sizes
    given = peers if step < micro else 0
    order_refs, refs = refs[: min(given, 1)], refs[min(given, 1) :]
    pieces = pieces_of(far_first(shards))
    came = peers * len(pieces) if step > 0 else 0
    input_refs, refs = refs[:given], refs[given:]
    came_refs, refs = refs[:came], refs[came:]
    (gain_ref, scale_ref, w_in_ref, w_out_ref), refs = refs[:4], refs[4:]
    y_refs, refs = refs[:shards], refs[shards:]
    x_ref = refs[0]
    rows = x_ref.shape[0] // peers

    @pl.when(at_work(place_ref, step, micro))
    def _():
        if given:

            @pl.when(place_ref[0] == 0)
            def _():
                order = order_refs[0][...]
                for j, ref in enumerate(input_refs):
                    moved = matmul(order, ref[step]).astype(jnp.bfloat16)
                    x_ref[j * rows : (j + 1) * rows, :] = moved

        if came:

            @pl.when(place_ref[0] != 0)
            def _():
                for j, blocks in enumerate(row_sets(came_refs, shards, pieces)):
                    x_ref[j * rows : (j + 1) * rows, :] = jnp.concatenate(blocks, axis=0)

        inner = min(patches, 8)
        groups = patches // inner
        xs = [
            regrouped(x_ref[j * rows : (j + 1) * rows, :].astype(jnp.float32), groups, inner)
            for j in range(peers)
        ]
        shape = (rows // groups, rows // groups * peers)
        mine = digits(shape, 0, inner)[0]
        theirs = digits(shape, 1, inner)[0]
        mask = jnp.where(mine == theirs, 1.0, 0.0).astype(jnp.bfloat16)
        update = attention_update(
            xs,
            groups,
            gain_ref[0, 0:1, :],
            lambda n: scale_ref[0, 0, n],
            w_in_ref.at[0, 0],
            w_out_ref.at[0, 0],
            mask,
        )
        y = regrouped(xs[0] + update, rows // (groups * inner), inner).astype(jnp.bfloat16)
        size = rows // shards
        for k in range(shards):
            y_refs[k][...] = y[k * size : (k + 1) * size]


def patch_kernel(sizes, step, micro, outs, place_ref, seen_ref, *refs):
    slow, _, patches, hl = sizes
    count = len(refs) - 6 - outs
    pieces = pieces_of([0] + [k for k in far_first(slow) if k])
    fast = count // len(pieces)
    x_refs, (gain_ref, scale_ref, w_in_ref, w_out_ref, up_ref, down_ref), y_refs = (
        refs[:count],
        refs[count : count + 6],
        refs[count + 6 :],
    )

    @pl.when(at_work(place_ref, step, micro))
    def _():
        xs = [
            jnp.concatenate(blocks, axis=0).astype(jnp.float32)
            for blocks in row_sets(x_refs, slow, pieces)
        ]
        rows = xs[0].shape[0]
        groups = 2 if hl % 2 == 0 else 1
        inner = hl // groups * patches
        xs = [regrouped(x, groups, inner) for x in xs]
        x = xs[0]
        shape = (rows // groups, rows // groups * fast)

        def block_and_hour(dimension):
            patch, late, offset, other = digits(shape, dimension, patches, hl // groups, slow)
            shard = (offset ^ place_ref[1]) * fast + (other ^ place_ref[2])
            return (shard * patches + patch) // PB, late

        query_block, query_hour = block_and_hour(0)
        key_block, key_hour = block_and_hour(1)
        seen = None
        for kv in range(seen_ref.shape[1]):
            chosen = jnp.full(shape, seen_ref[0, kv], jnp.int32)
            for b in range(1, seen_ref.shape[0]):
                chosen = jnp.where(query_block == b, seen_ref[b, kv], chosen)
            hit = jnp.where(chosen == key_block, 1.0, 0.0)
            seen = hit if seen is None else jnp.maximum(seen, hit)
        mask = jnp.where(query_hour == key_hour, seen, 0.0).astype(jnp.bfloat16)
        update = attention_update(
            xs,
            groups,
            gain_ref[0, 1:2, :],
            lambda n: scale_ref[0, 1, n],
            w_in_ref.at[0, 1],
            w_out_ref.at[0, 1],
            mask,
        )
        x = rounded(x + update)
        normed = row_norm(x, gain_ref[0, 2:3, :])
        total = x
        chunk = 512
        for start in range(0, up_ref.shape[2], chunk):
            u = matmul(normed, up_ref[0, :, start : start + chunk])
            bent = jnp.tanh(u * (0.7978845608028654 + 0.035677408136300125 * (u * u)))
            hidden = (0.5 * u * (1.0 + bent)).astype(jnp.bfloat16)
            total = total + matmul(hidden, down_ref[0, start : start + chunk, :])
        y = regrouped(total, slow, inner).astype(jnp.bfloat16)
        size = rows // outs
        for k in range(outs):
            y_refs[k][...] = y[k * size : (k + 1) * size]


def pick_kernel(slow, last, place_ref, *refs):
    x_refs, y_refs = refs[:-slow], refs[-slow:]
    size = x_refs[0].shape[0] // slow
    for hops, x_ref in enumerate(x_refs):

        @pl.when(place_ref[0] == (last + hops) % len(x_refs))
        def _():
            for k, y_ref in enumerate(y_refs):
                y_ref[...] = x_ref[k * size : (k + 1) * size, :]


def write_rows(sizes, place_ref, x, y_ref):
    slow, _, patches, hl = sizes
    rows = slow * patches * hl
    late, shard, patch = digits((rows, rows), 0, hl, slow)
    source = lax.broadcasted_iota(jnp.int32, (rows, rows), 1)
    wanted = ((shard ^ place_ref[1]) * hl + late) * patches + patch
    order = jnp.where(wanted == source, 1.0, 0.0).astype(jnp.bfloat16)
    y_ref[...] = matmul(order, x).astype(jnp.bfloat16)


def early_kernel(sizes, pipes, place_ref, *refs):
    x_refs, y_ref = refs[:pipes], refs[-1]
    for stage, x_ref in enumerate(x_refs):

        @pl.when(place_ref[0] == stage)
        def _():
            write_rows(sizes, place_ref, x_ref[...], y_ref)


def final_kernel(sizes, place_ref, *refs):
    x_refs, y_ref = refs[: sizes[0]], refs[-1]
    write_rows(sizes, place_ref, jnp.concatenate([ref[...] for ref in x_refs], axis=0), y_ref)


VMEM = pl.BlockSpec(memory_space=pltpu.VMEM)
SMEM = pl.BlockSpec(memory_space=pltpu.SMEM)
PARAMS = pltpu.CompilerParams(vmem_limit_bytes=32 << 20)
COST = pl.CostEstimate(flops=5 << 30, bytes_accessed=1 << 20, transcendentals=1 << 20)


def blocks_of(count, rows, width):
    return [jax.ShapeDtypeStruct((rows // count, width), jnp.bfloat16)] * count


def call_order(sizes, place, rows):
    return pl.pallas_call(
        functools.partial(order_kernel, sizes),
        out_shape=jax.ShapeDtypeStruct((rows, rows), jnp.bfloat16),
        in_specs=[SMEM],
        out_specs=VMEM,
        compiler_params=PARAMS,
        cost_estimate=COST,
        name="input_order",
    )(place)


def call_time(sizes, step, micro, shape, place, order, given, came, gains, scales, w_in, w_out):
    rows, width = shape
    xs = ([order] if given else []) + list(given) + list(came)
    return pl.pallas_call(
        functools.partial(time_kernel, sizes, step, micro),
        out_shape=blocks_of(sizes[0], rows, width),
        in_specs=[SMEM] + [VMEM] * len(xs) + [VMEM, SMEM, VMEM, VMEM],
        out_specs=[VMEM] * sizes[0],
        scratch_shapes=[pltpu.VMEM((rows * sizes[1], width), jnp.bfloat16)],
        compiler_params=PARAMS,
        cost_estimate=COST,
        name="time_attention",
    )(place, *xs, gains, scales, w_in, w_out)


def call_patch(sizes, step, micro, shape, outs, place, seen, xs, gains, scales, w_in, w_out, w_up, w_down):
    rows, width = shape
    return pl.pallas_call(
        functools.partial(patch_kernel, sizes, step, micro, outs),
        out_shape=blocks_of(outs, rows, width),
        in_specs=[SMEM, SMEM] + [VMEM] * len(xs) + [VMEM, SMEM] + [VMEM] * 4,
        out_specs=[VMEM] * outs,
        compiler_params=PARAMS,
        cost_estimate=COST,
        name="patch_attention_and_ffn",
    )(place, seen, *xs, gains, scales, w_in, w_out, w_up, w_down)


def call_pick(slow, last, place, xs):
    rows, width = xs[0].shape
    return pl.pallas_call(
        functools.partial(pick_kernel, slow, last),
        out_shape=blocks_of(slow, rows, width),
        in_specs=[SMEM] + [VMEM] * len(xs),
        out_specs=[VMEM] * slow,
        compiler_params=PARAMS,
        name="pick",
    )(place, *xs)


def call_write(kernel, sizes, place, shape, number, xs, out):
    given = [] if out is None else [out]
    return pl.pallas_call(
        kernel,
        out_shape=jax.ShapeDtypeStruct(shape, jnp.bfloat16),
        grid=(1,),
        in_specs=[SMEM] + [VMEM] * len(xs) + [pl.BlockSpec(memory_space=pl.ANY)] * len(given),
        out_specs=pl.BlockSpec((None,) + shape[1:], lambda i: (number, 0, 0)),
        input_output_aliases={1 + len(xs): 0} if given else {},
        compiler_params=PARAMS,
        name="final_order",
    )(place, *xs, *given)


def flipped(x, axis, k):
    return lax.ppermute(x, axis, [(s, s ^ k) for s in range(lax.axis_size(axis))])


def handed_on(x, k):
    pipes, shards = lax.axis_size("pipe"), lax.axis_size("patch")
    pairs = [
        (stage * shards + s, (stage + 1) % pipes * shards + (s ^ k))
        for stage in range(pipes)
        for s in range(shards)
    ]
    return lax.ppermute(x, ("pipe", "patch"), pairs)


def local(inputs, seen, gains, scales, w_in, w_out, w_up, w_down):
    shards = lax.axis_size("patch")
    peers = lax.axis_size("hour")
    pipes = lax.axis_size("pipe")
    micro, patches, hours, width = inputs.shape
    rows = patches * hours
    fast = 2
    slow = shards // fast
    sizes = (slow, peers, patches, hours // slow)
    last = pipes - 1
    shard = lax.axis_index("patch")
    place = jnp.stack([lax.axis_index("pipe"), lax.div(shard, fast), lax.rem(shard, fast)])
    far = far_first(slow)
    order = call_order(sizes, place, rows)

    def gathered(blocks, axis, count, sequence):
        own = [jnp.concatenate([blocks[k] for k in piece]) for piece in pieces_of(sequence)]
        out = list(own)
        for j in range(1, count):
            out += [flipped(piece, axis, j) for piece in own]
        return out

    def along_slow(blocks, send, first):
        got = {k: send(blocks[k], k * fast) for k in far if k >= first}
        return [got.get(k, blocks[k]) for k in range(slow)]

    def in_stage(x, k):
        return flipped(x, "patch", k)

    def onward(x):
        return lax.ppermute(x, "pipe", [(s, (s + 1) % pipes) for s in range(pipes)])

    x = inputs.reshape(micro, rows, width)
    given = [x] + [flipped(x, "hour", j) for j in range(1, peers)]
    came = []
    out = None
    back = []
    for step in range(micro + pipes - 1):
        now = given if step < micro else []
        mixed = call_time(sizes, step, micro, x.shape[1:], place, order, now, came, gains, scales, w_in, w_out)
        own = along_slow(mixed, in_stage, 1)
        spread = gathered(own, "patch", fast, [0] + [k for k in far if k])
        if back:
            spread, back = lax.optimization_barrier((spread, back))
            write = functools.partial(early_kernel, sizes, pipes)
            out = call_write(write, sizes, place, x.shape, step - pipes, back, out)
        at_end = step == micro + pipes - 2
        outs = 1 if at_end else slow
        done = call_patch(
            sizes,
            step,
            micro,
            x.shape[1:],
            outs,
            place,
            seen,
            spread,
            gains,
            scales,
            w_in,
            w_out,
            w_up,
            w_down,
        )
        if not at_end:
            arrived = along_slow(done, handed_on, 0)
            came = gathered(arrived, "hour", peers, far)
            if step >= last:
                back = [jnp.concatenate(arrived)]
                for _ in range(1, pipes):
                    back.append(onward(back[-1]))
    done = list(done)
    for _ in range(1, pipes):
        done.append(onward(done[-1]))
    blocks = along_slow(call_pick(slow, last, place, done), in_stage, 1)
    write = functools.partial(final_kernel, sizes)
    out = call_write(write, sizes, place, x.shape, micro - 1, blocks, out)
    return out.reshape(inputs.shape)


def solution(mesh):
    placed = (
        P(None, "patch", "hour", None),
        P(),
        P("pipe", None, None),
        P("pipe", None, None),
        P("pipe", None, None, None),
        P("pipe", None, None, None),
        P("pipe", None, None),
        P("pipe", None, None),
    )
    return jax.shard_map(
        local, mesh=mesh, in_specs=placed, out_specs=P(None, "patch", "hour", None), check_vma=False
    )
```

```python
import functools

import jax
import jax.numpy as jnp
from jax import lax
from jax.experimental import pallas as pl
from jax.experimental.pallas import tpu as pltpu
from jax.sharding import PartitionSpec as P

HEADS = 8
HEAD_DIM = 64
PB = 64
LOG2E = 1.4426950408889634


def row_norm(x, gain):
    factor = lax.rsqrt(jnp.mean(x * x, axis=-1, keepdims=True) + 1e-05)
    return (x * factor * gain).astype(jnp.bfloat16)


def matmul(a, b):
    return jnp.dot(a, b, preferred_element_type=jnp.float32)


def same_head():
    rows = lax.broadcasted_iota(jnp.int32, (256, 256), 0) // HEAD_DIM
    cols = lax.broadcasted_iota(jnp.int32, (256, 256), 1) // HEAD_DIM
    return jnp.where(rows == cols, 1.0, 0.0).astype(jnp.bfloat16)


def head_factor(values, group):
    squares = (values * values).astype(jnp.bfloat16)
    halves = [
        matmul(squares[:, start : start + 256], group) for start in range(0, values.shape[1], 256)
    ]
    sums = jnp.concatenate(halves, axis=1)
    return lax.rsqrt(sums * (1.0 / HEAD_DIM) + 1e-06)


def regrouped(x, groups, inner):
    outer = x.shape[0] // (groups * inner)
    starts = [(o * groups + g) * inner for g in range(groups) for o in range(outer)]
    return jnp.concatenate([x[start : start + inner] for start in starts], axis=0)


def attention_update(xs, groups, gain, scale_of, w_in, w_out, mask):
    rows, width = xs[0].shape
    normed = row_norm(xs[0], gain)
    seen = jnp.concatenate([normed] + [row_norm(t, gain) for t in xs[1:]], axis=0)
    same = same_head()
    head = lax.broadcasted_iota(jnp.int32, (1, width), 1) // HEAD_DIM
    scale = jnp.zeros((1, width), jnp.float32)
    for n in range(HEADS):
        scale = jnp.where(head == n, scale_of(n) * (LOG2E / HEAD_DIM), scale)
    q = matmul(normed, w_in[:, :width])
    k = matmul(seen, w_in[:, width : 2 * width])
    v = matmul(seen, w_in[:, 2 * width :]).astype(jnp.bfloat16)
    q = (q * head_factor(q, same) * scale).astype(jnp.bfloat16)
    k = (k * head_factor(k, same)).astype(jnp.bfloat16)
    pair = 2 * HEAD_DIM
    size = rows // groups
    first = lax.broadcasted_iota(jnp.int32, (1, pair), 1) < HEAD_DIM
    low = jnp.where(first, 1.0, 0.0).astype(jnp.bfloat16)
    high = jnp.where(first, 0.0, 1.0).astype(jnp.bfloat16)
    keys = size * len(xs)
    low_all = jnp.broadcast_to(low, (keys, pair))
    high_all = jnp.broadcast_to(high, (keys, pair))
    done = []
    for g in range(groups):
        q_g = q[g * size : (g + 1) * size]
        spans = [slice(i * rows + g * size, i * rows + (g + 1) * size) for i in range(len(xs))]
        k_g = jnp.concatenate([k[span] for span in spans], axis=0)
        v_g = jnp.concatenate([v[span] for span in spans], axis=0)
        parts = []
        for start in range(0, width, pair):
            q2, k2, v2 = (t[:, start : start + pair] for t in (q_g, k_g, v_g))
            powers = []
            for side in (low, high):
                scores = lax.dot_general(
                    q2 * side, k2, (((1,), (1,)), ((), ())), preferred_element_type=jnp.float32
                )
                powers.append(jnp.exp2(scores).astype(jnp.bfloat16) * mask)
            powers = jnp.concatenate(powers, axis=1)
            upper = jnp.concatenate([v2 * low, low_all], axis=1)
            lower = jnp.concatenate([v2 * high, high_all], axis=1)
            sums = matmul(powers, jnp.concatenate([upper, lower], axis=0))
            parts.append((sums[:, :pair] / sums[:, pair:]).astype(jnp.bfloat16))
        done.append(jnp.concatenate(parts, axis=1))
    return matmul(jnp.concatenate(done, axis=0), w_out[...])


def rounded(x):
    return x.astype(jnp.bfloat16).astype(jnp.float32)


def digits(shape, dimension, *bases):
    index = lax.broadcasted_iota(jnp.int32, shape, dimension)
    out = []
    for base in bases:
        out.append(index % base)
        index = index // base
    return out + [index]


def far_first(slow):
    return sorted(range(slow), key=lambda k: (k < slow // 2, k))


def pieces_of(sequence):
    return [[k] for k in sequence]


def row_sets(refs, slow, pieces):
    sets = []
    for start in range(0, len(refs), len(pieces)):
        found = {}
        for ref, piece in zip(refs[start : start + len(pieces)], pieces):
            size = ref.shape[0] // len(piece)
            for place, k in enumerate(piece):
                found[k] = ref[place * size : (place + 1) * size, :]
        sets.append([found[k] for k in range(slow)])
    return sets


def at_work(place_ref, step, micro):
    number = step - place_ref[0]
    return jnp.logical_and(number >= 0, number < micro)


def order_kernel(sizes, place_ref, order_ref):
    slow, _, patches, hl = sizes
    shape = order_ref.shape
    patch, late, offset = digits(shape, 0, patches, hl)
    source = lax.broadcasted_iota(jnp.int32, shape, 1)
    wanted = (patch * slow + (offset ^ place_ref[1])) * hl + late
    order_ref[...] = jnp.where(wanted == source, 1.0, 0.0).astype(jnp.bfloat16)


def time_kernel(sizes, step, micro, place_ref, *refs):
    shards, peers, patches, hl = sizes
    given = peers if step < micro else 0
    order_refs, refs = refs[: min(given, 1)], refs[min(given, 1) :]
    pieces = pieces_of(far_first(shards))
    came = peers * len(pieces) if step > 0 else 0
    input_refs, refs = refs[:given], refs[given:]
    came_refs, refs = refs[:came], refs[came:]
    (gain_ref, scale_ref, w_in_ref, w_out_ref), refs = refs[:4], refs[4:]
    y_refs, refs = refs[:shards], refs[shards:]
    x_ref = refs[0]
    rows = x_ref.shape[0] // peers

    @pl.when(at_work(place_ref, step, micro))
    def _():
        if given:

            @pl.when(place_ref[0] == 0)
            def _():
                order = order_refs[0][...]
                for j, ref in enumerate(input_refs):
                    moved = matmul(order, ref[step]).astype(jnp.bfloat16)
                    x_ref[j * rows : (j + 1) * rows, :] = moved

        if came:

            @pl.when(place_ref[0] != 0)
            def _():
                for j, blocks in enumerate(row_sets(came_refs, shards, pieces)):
                    x_ref[j * rows : (j + 1) * rows, :] = jnp.concatenate(blocks, axis=0)

        inner = min(patches, 8)
        groups = patches // inner
        xs = [
            regrouped(x_ref[j * rows : (j + 1) * rows, :].astype(jnp.float32), groups, inner)
            for j in range(peers)
        ]
        shape = (rows // groups, rows // groups * peers)
        mine = digits(shape, 0, inner)[0]
        theirs = digits(shape, 1, inner)[0]
        mask = jnp.where(mine == theirs, 1.0, 0.0).astype(jnp.bfloat16)
        update = attention_update(
            xs,
            groups,
            gain_ref[0, 0:1, :],
            lambda n: scale_ref[0, 0, n],
            w_in_ref.at[0, 0],
            w_out_ref.at[0, 0],
            mask,
        )
        y = regrouped(xs[0] + update, rows // (groups * inner), inner).astype(jnp.bfloat16)
        size = rows // shards
        for k in range(shards):
            y_refs[k][...] = y[k * size : (k + 1) * size]


def patch_kernel(sizes, step, micro, place_ref, seen_ref, *refs):
    slow, _, patches, hl = sizes
    count = len(refs) - 6 - slow
    pieces = pieces_of([0] + [k for k in far_first(slow) if k])
    fast = count // len(pieces)
    x_refs, (gain_ref, scale_ref, w_in_ref, w_out_ref, up_ref, down_ref), y_refs = (
        refs[:count],
        refs[count : count + 6],
        refs[count + 6 :],
    )

    @pl.when(at_work(place_ref, step, micro))
    def _():
        xs = [
            jnp.concatenate(blocks, axis=0).astype(jnp.float32)
            for blocks in row_sets(x_refs, slow, pieces)
        ]
        rows = xs[0].shape[0]
        groups = 2 if hl % 2 == 0 else 1
        inner = hl // groups * patches
        xs = [regrouped(x, groups, inner) for x in xs]
        x = xs[0]
        shape = (rows // groups, rows // groups * fast)

        def block_and_hour(dimension):
            patch, late, offset, other = digits(shape, dimension, patches, hl // groups, slow)
            shard = (offset ^ place_ref[1]) * fast + (other ^ place_ref[2])
            return (shard * patches + patch) // PB, late

        query_block, query_hour = block_and_hour(0)
        key_block, key_hour = block_and_hour(1)
        seen = None
        for kv in range(seen_ref.shape[1]):
            chosen = jnp.full(shape, seen_ref[0, kv], jnp.int32)
            for b in range(1, seen_ref.shape[0]):
                chosen = jnp.where(query_block == b, seen_ref[b, kv], chosen)
            hit = jnp.where(chosen == key_block, 1.0, 0.0)
            seen = hit if seen is None else jnp.maximum(seen, hit)
        mask = jnp.where(query_hour == key_hour, seen, 0.0).astype(jnp.bfloat16)
        update = attention_update(
            xs,
            groups,
            gain_ref[0, 1:2, :],
            lambda n: scale_ref[0, 1, n],
            w_in_ref.at[0, 1],
            w_out_ref.at[0, 1],
            mask,
        )
        x = rounded(x + update)
        normed = row_norm(x, gain_ref[0, 2:3, :])
        total = x
        chunk = 512
        for start in range(0, up_ref.shape[2], chunk):
            u = matmul(normed, up_ref[0, :, start : start + chunk])
            bent = jnp.tanh(u * (0.7978845608028654 + 0.035677408136300125 * (u * u)))
            hidden = (0.5 * u * (1.0 + bent)).astype(jnp.bfloat16)
            total = total + matmul(hidden, down_ref[0, start : start + chunk, :])
        y = regrouped(total, slow, inner).astype(jnp.bfloat16)
        size = rows // slow
        for k in range(slow):
            y_refs[k][...] = y[k * size : (k + 1) * size]


def write_rows(sizes, place_ref, x, y_ref):
    slow, _, patches, hl = sizes
    rows = slow * patches * hl
    late, shard, patch = digits((rows, rows), 0, hl, slow)
    source = lax.broadcasted_iota(jnp.int32, (rows, rows), 1)
    wanted = ((shard ^ place_ref[1]) * hl + late) * patches + patch
    order = jnp.where(wanted == source, 1.0, 0.0).astype(jnp.bfloat16)
    y_ref[...] = matmul(order, x).astype(jnp.bfloat16)


def early_kernel(sizes, pipes, place_ref, *refs):
    x_refs, y_ref = refs[:pipes], refs[-1]
    for stage, x_ref in enumerate(x_refs):

        @pl.when(place_ref[0] == stage)
        def _():
            write_rows(sizes, place_ref, x_ref[...], y_ref)


def final_kernel(sizes, place_ref, *refs):
    x_refs, y_ref = refs[: sizes[0]], refs[-1]
    write_rows(sizes, place_ref, jnp.concatenate([ref[...] for ref in x_refs], axis=0), y_ref)


VMEM = pl.BlockSpec(memory_space=pltpu.VMEM)
SMEM = pl.BlockSpec(memory_space=pltpu.SMEM)
PARAMS = pltpu.CompilerParams(vmem_limit_bytes=32 << 20)
COST = pl.CostEstimate(flops=5 << 30, bytes_accessed=1 << 20, transcendentals=1 << 20)


def blocks_of(count, rows, width):
    return [jax.ShapeDtypeStruct((rows // count, width), jnp.bfloat16)] * count


def call_order(sizes, place, rows):
    return pl.pallas_call(
        functools.partial(order_kernel, sizes),
        out_shape=jax.ShapeDtypeStruct((rows, rows), jnp.bfloat16),
        in_specs=[SMEM],
        out_specs=VMEM,
        compiler_params=PARAMS,
        cost_estimate=COST,
        name="input_order",
    )(place)


def call_time(sizes, step, micro, shape, place, order, given, came, gains, scales, w_in, w_out):
    rows, width = shape
    xs = ([order] if given else []) + list(given) + list(came)
    return pl.pallas_call(
        functools.partial(time_kernel, sizes, step, micro),
        out_shape=blocks_of(sizes[0], rows, width),
        in_specs=[SMEM] + [VMEM] * len(xs) + [VMEM, SMEM, VMEM, VMEM],
        out_specs=[VMEM] * sizes[0],
        scratch_shapes=[pltpu.VMEM((rows * sizes[1], width), jnp.bfloat16)],
        compiler_params=PARAMS,
        cost_estimate=COST,
        name="time_attention",
    )(place, *xs, gains, scales, w_in, w_out)


def call_patch(sizes, step, micro, shape, place, seen, xs, gains, scales, w_in, w_out, w_up, w_down):
    rows, width = shape
    return pl.pallas_call(
        functools.partial(patch_kernel, sizes, step, micro),
        out_shape=blocks_of(sizes[0], rows, width),
        in_specs=[SMEM, SMEM] + [VMEM] * len(xs) + [VMEM, SMEM] + [VMEM] * 4,
        out_specs=[VMEM] * sizes[0],
        compiler_params=PARAMS,
        cost_estimate=COST,
        name="patch_attention_and_ffn",
    )(place, seen, *xs, gains, scales, w_in, w_out, w_up, w_down)


def call_write(kernel, sizes, place, shape, number, xs, out):
    given = [] if out is None else [out]
    return pl.pallas_call(
        kernel,
        out_shape=jax.ShapeDtypeStruct(shape, jnp.bfloat16),
        grid=(1,),
        in_specs=[SMEM] + [VMEM] * len(xs) + [pl.BlockSpec(memory_space=pl.ANY)] * len(given),
        out_specs=pl.BlockSpec((None,) + shape[1:], lambda i: (number, 0, 0)),
        input_output_aliases={1 + len(xs): 0} if given else {},
        compiler_params=PARAMS,
        name="final_order",
    )(place, *xs, *given)


def flipped(x, axis, k):
    return lax.ppermute(x, axis, [(s, s ^ k) for s in range(lax.axis_size(axis))])


def handed_on(x, k):
    pipes, shards = lax.axis_size("pipe"), lax.axis_size("patch")
    pairs = [
        (stage * shards + s, (stage + 1) % pipes * shards + (s ^ k))
        for stage in range(pipes)
        for s in range(shards)
    ]
    return lax.ppermute(x, ("pipe", "patch"), pairs)


def local(inputs, seen, gains, scales, w_in, w_out, w_up, w_down):
    shards = lax.axis_size("patch")
    peers = lax.axis_size("hour")
    pipes = lax.axis_size("pipe")
    micro, patches, hours, width = inputs.shape
    rows = patches * hours
    fast = 2
    slow = shards // fast
    sizes = (slow, peers, patches, hours // slow)
    last = pipes - 1
    shard = lax.axis_index("patch")
    place = jnp.stack([lax.axis_index("pipe"), lax.div(shard, fast), lax.rem(shard, fast)])
    far = far_first(slow)
    order = call_order(sizes, place, rows)

    def gathered(blocks, axis, count, sequence):
        own = [jnp.concatenate([blocks[k] for k in piece]) for piece in pieces_of(sequence)]
        out = list(own)
        for j in range(1, count):
            out += [flipped(piece, axis, j) for piece in own]
        return out

    def along_slow(blocks, send, first):
        got = {k: send(blocks[k], k * fast) for k in far if k >= first}
        return [got.get(k, blocks[k]) for k in range(slow)]

    def in_stage(x, k):
        return flipped(x, "patch", k)

    def onward(x):
        return lax.ppermute(x, "pipe", [(s, (s + 1) % pipes) for s in range(pipes)])

    x = inputs.reshape(micro, rows, width)
    given = [x] + [flipped(x, "hour", j) for j in range(1, peers)]
    came = []
    out = None
    back = []
    for step in range(micro + pipes - 1):
        now = given if step < micro else []
        mixed = call_time(sizes, step, micro, x.shape[1:], place, order, now, came, gains, scales, w_in, w_out)
        own = along_slow(mixed, in_stage, 1)
        spread = gathered(own, "patch", fast, [0] + [k for k in far if k])
        if back:
            spread, back = lax.optimization_barrier((spread, back))
            write = functools.partial(early_kernel, sizes, pipes)
            out = call_write(write, sizes, place, x.shape, step - pipes, back, out)
        at_end = step == micro + pipes - 2
        done = call_patch(
            sizes,
            step,
            micro,
            x.shape[1:],
            place,
            seen,
            spread,
            gains,
            scales,
            w_in,
            w_out,
            w_up,
            w_down,
        )
        if not at_end:
            arrived = along_slow(done, handed_on, 0)
            came = gathered(arrived, "hour", peers, far)
            if step >= last:
                back = [jnp.concatenate(arrived)]
                for _ in range(1, pipes):
                    back.append(onward(back[-1]))
    stage = lax.axis_index("pipe")
    blocks = {}
    for count, k in enumerate(far):
        own = done[k]
        if count >= slow // 2:
            own, blocks[far[0]] = lax.optimization_barrier((own, blocks[far[0]]))
        chosen = block = own
        for hop in range(pipes - 1):
            block = onward(block)
            chosen = jnp.where(stage == hop, block, chosen)
        blocks[k] = chosen
    blocks = {k: in_stage(blocks[k], k * fast) if k else blocks[k] for k in far}
    blocks = [blocks[k] for k in range(slow)]
    write = functools.partial(final_kernel, sizes)
    out = call_write(write, sizes, place, x.shape, micro - 1, blocks, out)
    return out.reshape(inputs.shape)


def solution(mesh):
    placed = (
        P(None, "patch", "hour", None),
        P(),
        P("pipe", None, None),
        P("pipe", None, None),
        P("pipe", None, None, None),
        P("pipe", None, None, None),
        P("pipe", None, None),
        P("pipe", None, None),
    )
    return jax.shard_map(
        local, mesh=mesh, in_specs=placed, out_specs=P(None, "patch", "hour", None), check_vma=False
    )
```

```python
import functools

import jax
import jax.numpy as jnp
from jax import lax
from jax.experimental import pallas as pl
from jax.experimental.pallas import tpu as pltpu
from jax.sharding import PartitionSpec as P

HEADS = 8
HEAD_DIM = 64
PB = 64
LOG2E = 1.4426950408889634


def row_norm(x, gain):
    factor = lax.rsqrt(jnp.mean(x * x, axis=-1, keepdims=True) + 1e-05)
    return (x * factor * gain).astype(jnp.bfloat16)


def matmul(a, b):
    return jnp.dot(a, b, preferred_element_type=jnp.float32)


def same_head():
    rows = lax.broadcasted_iota(jnp.int32, (256, 256), 0) // HEAD_DIM
    cols = lax.broadcasted_iota(jnp.int32, (256, 256), 1) // HEAD_DIM
    return jnp.where(rows == cols, 1.0, 0.0).astype(jnp.bfloat16)


def head_factor(values, group):
    squares = (values * values).astype(jnp.bfloat16)
    halves = [
        matmul(squares[:, start : start + 256], group) for start in range(0, values.shape[1], 256)
    ]
    sums = jnp.concatenate(halves, axis=1)
    return lax.rsqrt(sums * (1.0 / HEAD_DIM) + 1e-06)


def regrouped(x, groups, inner):
    outer = x.shape[0] // (groups * inner)
    starts = [(o * groups + g) * inner for g in range(groups) for o in range(outer)]
    return jnp.concatenate([x[start : start + inner] for start in starts], axis=0)


def queries(normed, scale_of, w_in):
    width = normed.shape[1]
    head = lax.broadcasted_iota(jnp.int32, (1, width), 1) // HEAD_DIM
    scale = jnp.zeros((1, width), jnp.float32)
    for n in range(HEADS):
        scale = jnp.where(head == n, scale_of(n) * (LOG2E / HEAD_DIM), scale)
    q = matmul(normed, w_in[:, :width])
    return (q * head_factor(q, same_head()) * scale).astype(jnp.bfloat16)


def keys_and_values(normed, w_in):
    width = normed.shape[1]
    k = matmul(normed, w_in[:, width : 2 * width])
    v = matmul(normed, w_in[:, 2 * width :]).astype(jnp.bfloat16)
    return (k * head_factor(k, same_head())).astype(jnp.bfloat16), v


def attention_sums(q, k, v, groups, mask):
    rows, width = q.shape
    pair = 2 * HEAD_DIM
    size = rows // groups
    sets = k.shape[0] // rows
    keys = size * sets
    first = lax.broadcasted_iota(jnp.int32, (1, pair), 1) < HEAD_DIM
    low = jnp.where(first, 1.0, 0.0).astype(jnp.bfloat16)
    high = jnp.where(first, 0.0, 1.0).astype(jnp.bfloat16)
    low_all = jnp.broadcast_to(low, (keys, pair))
    high_all = jnp.broadcast_to(high, (keys, pair))
    both = jnp.concatenate([mask, mask], axis=1)
    out = []
    for g in range(groups):
        q_g = q[g * size : (g + 1) * size]
        spans = [slice(i * rows + g * size, i * rows + (g + 1) * size) for i in range(sets)]
        k_g = jnp.concatenate([k[span] for span in spans], axis=0)
        v_g = jnp.concatenate([v[span] for span in spans], axis=0)
        parts = []
        for start in range(0, width, pair):
            q2, k2, v2 = (t[:, start : start + pair] for t in (q_g, k_g, v_g))
            scores = lax.dot_general(
                q2,
                jnp.concatenate([k2 * low, k2 * high], axis=0),
                (((1,), (1,)), ((), ())),
                preferred_element_type=jnp.float32,
            )
            powers = jnp.exp2(scores).astype(jnp.bfloat16) * both
            upper = jnp.concatenate([v2 * low, low_all], axis=1)
            lower = jnp.concatenate([v2 * high, high_all], axis=1)
            parts.append(matmul(powers, jnp.concatenate([upper, lower], axis=0)))
        out.append(parts)
    return out


def projected(sums, w_out):
    pair = 2 * HEAD_DIM
    rows = [
        jnp.concatenate([(t[:, :pair] / t[:, pair:]).astype(jnp.bfloat16) for t in parts], axis=1)
        for parts in sums
    ]
    return matmul(jnp.concatenate(rows, axis=0), w_out[...])


def rounded(x):
    return x.astype(jnp.bfloat16).astype(jnp.float32)


def digits(shape, dimension, *bases):
    index = lax.broadcasted_iota(jnp.int32, shape, dimension)
    out = []
    for base in bases:
        out.append(index % base)
        index = index // base
    return out + [index]


def far_first(slow):
    return sorted(range(slow), key=lambda k: (k < slow // 2, k))


def pieces_of(sequence):
    return [[k] for k in sequence]


def row_sets(refs, slow, pieces):
    sets = []
    for start in range(0, len(refs), len(pieces)):
        found = {}
        for ref, piece in zip(refs[start : start + len(pieces)], pieces):
            size = ref.shape[0] // len(piece)
            for place, k in enumerate(piece):
                found[k] = ref[place * size : (place + 1) * size, :]
        sets.append([found[k] for k in range(slow)])
    return sets


def at_work(place_ref, step, micro):
    number = step - place_ref[0]
    return jnp.logical_and(number >= 0, number < micro)


def order_kernel(sizes, place_ref, order_ref):
    slow, _, patches, hl = sizes
    shape = order_ref.shape
    patch, late, offset = digits(shape, 0, patches, hl)
    source = lax.broadcasted_iota(jnp.int32, shape, 1)
    wanted = (patch * slow + (offset ^ place_ref[1])) * hl + late
    order_ref[...] = jnp.where(wanted == source, 1.0, 0.0).astype(jnp.bfloat16)


def time_kernel(sizes, step, micro, place_ref, *refs):
    shards, peers, patches, hl = sizes
    given = peers if step < micro else 0
    order_refs, refs = refs[: min(given, 1)], refs[min(given, 1) :]
    pieces = pieces_of(far_first(shards))
    came = peers * len(pieces) if step > 0 else 0
    input_refs, refs = refs[:given], refs[given:]
    came_refs, refs = refs[:came], refs[came:]
    (gain_ref, scale_ref, w_in_ref, w_out_ref), refs = refs[:4], refs[4:]
    y_refs, refs = refs[:shards], refs[shards:]
    x_ref = refs[0]
    rows = x_ref.shape[0] // peers

    @pl.when(at_work(place_ref, step, micro))
    def _():
        if given:

            @pl.when(place_ref[0] == 0)
            def _():
                order = order_refs[0][...]
                for j, ref in enumerate(input_refs):
                    moved = matmul(order, ref[step]).astype(jnp.bfloat16)
                    x_ref[j * rows : (j + 1) * rows, :] = moved

        if came:

            @pl.when(place_ref[0] != 0)
            def _():
                for j, blocks in enumerate(row_sets(came_refs, shards, pieces)):
                    x_ref[j * rows : (j + 1) * rows, :] = jnp.concatenate(blocks, axis=0)

        inner = min(patches, 8)
        groups = patches // inner
        xs = [
            regrouped(x_ref[j * rows : (j + 1) * rows, :].astype(jnp.float32), groups, inner)
            for j in range(peers)
        ]
        shape = (rows // groups, rows // groups * peers)
        mine = digits(shape, 0, inner)[0]
        theirs = digits(shape, 1, inner)[0]
        mask = jnp.where(mine == theirs, 1.0, 0.0).astype(jnp.bfloat16)
        normed = [row_norm(x, gain_ref[0, 0:1, :]) for x in xs]
        w_in = w_in_ref.at[0, 0]
        q = queries(normed[0], lambda n: scale_ref[0, 0, n], w_in)
        k, v = keys_and_values(jnp.concatenate(normed, axis=0), w_in)
        update = projected(attention_sums(q, k, v, groups, mask), w_out_ref.at[0, 0])
        y = regrouped(xs[0] + update, rows // (groups * inner), inner).astype(jnp.bfloat16)
        size = rows // shards
        for k in range(shards):
            y_refs[k][...] = y[k * size : (k + 1) * size]


def hour_groups(sizes):
    _, _, patches, hl = sizes
    groups = 2 if hl % 2 == 0 else 1
    return groups, hl // groups * patches


def patch_mask(sizes, fast, others, place_ref, seen_ref):
    slow, _, patches, hl = sizes
    groups, inner = hour_groups(sizes)
    size = slow * inner
    shape = (size, size * len(others))

    def block_and_hour(dimension, first):
        patch, late, offset, other = digits(shape, dimension, patches, hl // groups, slow)
        shard = (offset ^ place_ref[1]) * fast + ((other + first) ^ place_ref[2])
        return (shard * patches + patch) // PB, late

    query_block, query_hour = block_and_hour(0, 0)
    key_block, key_hour = block_and_hour(1, others[0])
    seen = None
    for kv in range(seen_ref.shape[1]):
        chosen = jnp.full(shape, seen_ref[0, kv], jnp.int32)
        for b in range(1, seen_ref.shape[0]):
            chosen = jnp.where(query_block == b, seen_ref[b, kv], chosen)
        hit = jnp.where(chosen == key_block, 1.0, 0.0)
        seen = hit if seen is None else jnp.maximum(seen, hit)
    return jnp.where(query_hour == key_hour, seen, 0.0).astype(jnp.bfloat16)


def own_patch_kernel(sizes, fast, step, micro, place_ref, seen_ref, *refs):
    slow = sizes[0]
    x_refs, (gain_ref, scale_ref, w_in_ref), (q_ref, sums_ref) = (
        refs[:slow],
        refs[slow : slow + 3],
        refs[slow + 3 :],
    )

    @pl.when(at_work(place_ref, step, micro))
    def _():
        groups, inner = hour_groups(sizes)
        x = jnp.concatenate([ref[...] for ref in x_refs], axis=0).astype(jnp.float32)
        normed = row_norm(regrouped(x, groups, inner), gain_ref[0, 1:2, :])
        w_in = w_in_ref.at[0, 1]
        q = queries(normed, lambda n: scale_ref[0, 1, n], w_in)
        k, v = keys_and_values(normed, w_in)
        q_ref[...] = q
        mask = patch_mask(sizes, fast, [0], place_ref, seen_ref)
        sums = attention_sums(q, k, v, groups, mask)
        sums_ref[...] = jnp.concatenate([jnp.concatenate(t, axis=1) for t in sums], axis=0)


def patch_kernel(sizes, fast, step, micro, place_ref, seen_ref, *refs):
    slow = sizes[0]
    count = fast * slow
    x_refs, refs, y_refs = refs[:count], refs[count:-slow], refs[-slow:]
    q_ref, sums_ref, gain_ref, w_in_ref, w_out_ref, up_ref, down_ref = refs
    pieces = pieces_of([0] + [k for k in far_first(slow) if k])

    @pl.when(at_work(place_ref, step, micro))
    def _():
        groups, inner = hour_groups(sizes)
        xs = [
            regrouped(jnp.concatenate(blocks, axis=0).astype(jnp.float32), groups, inner)
            for blocks in row_sets(x_refs, slow, pieces)
        ]
        x = xs[0]
        rows, width = x.shape
        normed = jnp.concatenate([row_norm(t, gain_ref[0, 1:2, :]) for t in xs[1:]], axis=0)
        k, v = keys_and_values(normed, w_in_ref.at[0, 1])
        mask = patch_mask(sizes, fast, range(1, fast), place_ref, seen_ref)
        more = attention_sums(q_ref[...], k, v, groups, mask)
        size = rows // groups
        sums = [
            [
                t + sums_ref[g * size : (g + 1) * size, i * 256 : (i + 1) * 256]
                for i, t in enumerate(parts)
            ]
            for g, parts in enumerate(more)
        ]
        x = rounded(x + projected(sums, w_out_ref.at[0, 1]))
        normed = row_norm(x, gain_ref[0, 2:3, :])
        total = x
        chunk = 512
        for start in range(0, up_ref.shape[2], chunk):
            u = matmul(normed, up_ref[0, :, start : start + chunk])
            bent = jnp.tanh(u * (0.7978845608028654 + 0.035677408136300125 * (u * u)))
            hidden = (0.5 * u * (1.0 + bent)).astype(jnp.bfloat16)
            total = total + matmul(hidden, down_ref[0, start : start + chunk, :])
        y = regrouped(total, slow, inner).astype(jnp.bfloat16)
        size = rows // slow
        for k in range(slow):
            y_refs[k][...] = y[k * size : (k + 1) * size]


def write_rows(sizes, place_ref, x, y_ref):
    slow, _, patches, hl = sizes
    rows = slow * patches * hl
    late, shard, patch = digits((rows, rows), 0, hl, slow)
    source = lax.broadcasted_iota(jnp.int32, (rows, rows), 1)
    wanted = ((shard ^ place_ref[1]) * hl + late) * patches + patch
    order = jnp.where(wanted == source, 1.0, 0.0).astype(jnp.bfloat16)
    y_ref[...] = matmul(order, x).astype(jnp.bfloat16)


def early_kernel(sizes, pipes, place_ref, *refs):
    x_refs, y_ref = refs[:pipes], refs[-1]
    for stage, x_ref in enumerate(x_refs):

        @pl.when(place_ref[0] == stage)
        def _():
            write_rows(sizes, place_ref, x_ref[...], y_ref)


def final_kernel(sizes, place_ref, *refs):
    x_refs, y_ref = refs[: sizes[0]], refs[-1]
    write_rows(sizes, place_ref, jnp.concatenate([ref[...] for ref in x_refs], axis=0), y_ref)


VMEM = pl.BlockSpec(memory_space=pltpu.VMEM)
SMEM = pl.BlockSpec(memory_space=pltpu.SMEM)
PARAMS = pltpu.CompilerParams(vmem_limit_bytes=32 << 20)
COST = pl.CostEstimate(flops=5 << 30, bytes_accessed=1 << 20, transcendentals=1 << 20)


def blocks_of(count, rows, width):
    return [jax.ShapeDtypeStruct((rows // count, width), jnp.bfloat16)] * count


def call_order(sizes, place, rows):
    return pl.pallas_call(
        functools.partial(order_kernel, sizes),
        out_shape=jax.ShapeDtypeStruct((rows, rows), jnp.bfloat16),
        in_specs=[SMEM],
        out_specs=VMEM,
        compiler_params=PARAMS,
        cost_estimate=COST,
        name="input_order",
    )(place)


def call_time(sizes, step, micro, shape, place, order, given, came, gains, scales, w_in, w_out):
    rows, width = shape
    xs = ([order] if given else []) + list(given) + list(came)
    return pl.pallas_call(
        functools.partial(time_kernel, sizes, step, micro),
        out_shape=blocks_of(sizes[0], rows, width),
        in_specs=[SMEM] + [VMEM] * len(xs) + [VMEM, SMEM, VMEM, VMEM],
        out_specs=[VMEM] * sizes[0],
        scratch_shapes=[pltpu.VMEM((rows * sizes[1], width), jnp.bfloat16)],
        compiler_params=PARAMS,
        cost_estimate=COST,
        name="time_attention",
    )(place, *xs, gains, scales, w_in, w_out)


def call_own_patch(sizes, fast, step, micro, shape, place, seen, xs, gains, scales, w_in):
    rows, width = shape
    return pl.pallas_call(
        functools.partial(own_patch_kernel, sizes, fast, step, micro),
        out_shape=[
            jax.ShapeDtypeStruct((rows, width), jnp.bfloat16),
            jax.ShapeDtypeStruct((rows, 2 * width), jnp.float32),
        ],
        in_specs=[SMEM, SMEM] + [VMEM] * len(xs) + [VMEM, SMEM, VMEM],
        out_specs=[VMEM, VMEM],
        compiler_params=PARAMS,
        cost_estimate=COST,
        name="own_patch_attention",
    )(place, seen, *xs, gains, scales, w_in)


def call_patch(sizes, fast, step, micro, shape, place, seen, xs, weights):
    rows, width = shape
    return pl.pallas_call(
        functools.partial(patch_kernel, sizes, fast, step, micro),
        out_shape=blocks_of(sizes[0], rows, width),
        in_specs=[SMEM, SMEM] + [VMEM] * (len(xs) + len(weights)),
        out_specs=[VMEM] * sizes[0],
        compiler_params=PARAMS,
        cost_estimate=COST,
        name="patch_attention_and_ffn",
    )(place, seen, *xs, *weights)


def call_write(kernel, sizes, place, shape, number, xs, out):
    given = [] if out is None else [out]
    return pl.pallas_call(
        kernel,
        out_shape=jax.ShapeDtypeStruct(shape, jnp.bfloat16),
        grid=(1,),
        in_specs=[SMEM] + [VMEM] * len(xs) + [pl.BlockSpec(memory_space=pl.ANY)] * len(given),
        out_specs=pl.BlockSpec((None,) + shape[1:], lambda i: (number, 0, 0)),
        input_output_aliases={1 + len(xs): 0} if given else {},
        compiler_params=PARAMS,
        name="final_order",
    )(place, *xs, *given)


def flipped(x, axis, k):
    return lax.ppermute(x, axis, [(s, s ^ k) for s in range(lax.axis_size(axis))])


def handed_on(x, k):
    pipes, shards = lax.axis_size("pipe"), lax.axis_size("patch")
    pairs = [
        (stage * shards + s, (stage + 1) % pipes * shards + (s ^ k))
        for stage in range(pipes)
        for s in range(shards)
    ]
    return lax.ppermute(x, ("pipe", "patch"), pairs)


def local(inputs, seen, gains, scales, w_in, w_out, w_up, w_down):
    shards = lax.axis_size("patch")
    peers = lax.axis_size("hour")
    pipes = lax.axis_size("pipe")
    micro, patches, hours, width = inputs.shape
    rows = patches * hours
    fast = 2
    slow = shards // fast
    sizes = (slow, peers, patches, hours // slow)
    last = pipes - 1
    shard = lax.axis_index("patch")
    place = jnp.stack([lax.axis_index("pipe"), lax.div(shard, fast), lax.rem(shard, fast)])
    far = far_first(slow)
    order = call_order(sizes, place, rows)

    def gathered(blocks, axis, count, sequence):
        own = [jnp.concatenate([blocks[k] for k in piece]) for piece in pieces_of(sequence)]
        out = list(own)
        for j in range(1, count):
            out += [flipped(piece, axis, j) for piece in own]
        return out

    def along_slow(blocks, send, first):
        got = {k: send(blocks[k], k * fast) for k in far if k >= first}
        return [got.get(k, blocks[k]) for k in range(slow)]

    def in_stage(x, k):
        return flipped(x, "patch", k)

    def onward(x):
        return lax.ppermute(x, "pipe", [(s, (s + 1) % pipes) for s in range(pipes)])

    x = inputs.reshape(micro, rows, width)
    given = [x] + [flipped(x, "hour", j) for j in range(1, peers)]
    came = []
    out = None
    back = []
    for step in range(micro + pipes - 1):
        now = given if step < micro else []
        mixed = call_time(
            sizes, step, micro, x.shape[1:], place, order, now, came, gains, scales, w_in, w_out
        )
        own = along_slow(mixed, in_stage, 1)
        spread = gathered(own, "patch", fast, [0] + [k for k in far if k])
        begun = call_own_patch(
            sizes, fast, step, micro, x.shape[1:], place, seen, own, gains, scales, w_in
        )
        if back:
            write = functools.partial(early_kernel, sizes, pipes)
            out = call_write(write, sizes, place, x.shape, step - pipes, back, out)
            spread, out = lax.optimization_barrier((spread, out))
        at_end = step == micro + pipes - 2
        weights = [*begun, gains, w_in, w_out, w_up, w_down]
        done = call_patch(sizes, fast, step, micro, x.shape[1:], place, seen, spread, weights)
        if not at_end:
            arrived = along_slow(done, handed_on, 0)
            came = gathered(arrived, "hour", peers, far)
            if step >= last:
                back = [jnp.concatenate(arrived)]
                for _ in range(1, pipes):
                    back.append(onward(back[-1]))
    stage = lax.axis_index("pipe")
    blocks = {}
    for count, k in enumerate(far):
        own = done[k]
        if count >= slow // 2:
            own, blocks[far[0]] = lax.optimization_barrier((own, blocks[far[0]]))
        chosen = block = own
        for hop in range(pipes - 1):
            block = onward(block)
            chosen = jnp.where(stage == hop, block, chosen)
        blocks[k] = chosen
    blocks = {k: in_stage(blocks[k], k * fast) if k else blocks[k] for k in far}
    blocks = [blocks[k] for k in range(slow)]
    write = functools.partial(final_kernel, sizes)
    out = call_write(write, sizes, place, x.shape, micro - 1, blocks, out)
    return out.reshape(inputs.shape)


def solution(mesh):
    placed = (
        P(None, "patch", "hour", None),
        P(),
        P("pipe", None, None),
        P("pipe", None, None),
        P("pipe", None, None, None),
        P("pipe", None, None, None),
        P("pipe", None, None),
        P("pipe", None, None),
    )
    return jax.shard_map(
        local, mesh=mesh, in_specs=placed, out_specs=P(None, "patch", "hour", None), check_vma=False
    )
```

```python
import functools

import jax
import jax.numpy as jnp
from jax import lax
from jax.experimental import pallas as pl
from jax.experimental.pallas import tpu as pltpu
from jax.sharding import PartitionSpec as P

HEADS = 8
HEAD_DIM = 64
PB = 64
FAST = 2
LOG2E = 1.4426950408889634


def row_norm(x, gain):
    factor = lax.rsqrt(jnp.mean(x * x, axis=-1, keepdims=True) + 1e-05)
    return (x * factor * gain).astype(jnp.bfloat16)


def matmul(a, b):
    return jnp.dot(a, b, preferred_element_type=jnp.float32)


def same_head():
    rows = lax.broadcasted_iota(jnp.int32, (256, 256), 0) // HEAD_DIM
    cols = lax.broadcasted_iota(jnp.int32, (256, 256), 1) // HEAD_DIM
    return jnp.where(rows == cols, 1.0, 0.0).astype(jnp.bfloat16)


def head_factor(values, group):
    squares = (values * values).astype(jnp.bfloat16)
    halves = [
        matmul(squares[:, start : start + 256], group) for start in range(0, values.shape[1], 256)
    ]
    sums = jnp.concatenate(halves, axis=1)
    return lax.rsqrt(sums * (1.0 / HEAD_DIM) + 1e-06)


def regrouped(x, groups, inner):
    outer = x.shape[0] // (groups * inner)
    starts = [(o * groups + g) * inner for g in range(groups) for o in range(outer)]
    return jnp.concatenate([x[start : start + inner] for start in starts], axis=0)


def queries(normed, scale_of, w_in):
    width = normed.shape[1]
    head = lax.broadcasted_iota(jnp.int32, (1, width), 1) // HEAD_DIM
    scale = jnp.zeros((1, width), jnp.float32)
    for n in range(HEADS):
        scale = jnp.where(head == n, scale_of(n) * (LOG2E / HEAD_DIM), scale)
    q = matmul(normed, w_in[:, :width])
    return (q * head_factor(q, same_head()) * scale).astype(jnp.bfloat16)


def keys_and_values(normed, w_in):
    width = normed.shape[1]
    k = matmul(normed, w_in[:, width : 2 * width])
    v = matmul(normed, w_in[:, 2 * width :]).astype(jnp.bfloat16)
    return (k * head_factor(k, same_head())).astype(jnp.bfloat16), v


def attention_sums(q, k, v, groups, mask):
    rows, width = q.shape
    pair = 2 * HEAD_DIM
    size = rows // groups
    sets = k.shape[0] // rows
    keys = size * sets
    first = lax.broadcasted_iota(jnp.int32, (1, pair), 1) < HEAD_DIM
    low = jnp.where(first, 1.0, 0.0).astype(jnp.bfloat16)
    high = jnp.where(first, 0.0, 1.0).astype(jnp.bfloat16)
    low_all = jnp.broadcast_to(low, (keys, pair))
    high_all = jnp.broadcast_to(high, (keys, pair))
    both = jnp.concatenate([mask, mask], axis=1)
    out = []
    for g in range(groups):
        q_g = q[g * size : (g + 1) * size]
        spans = [slice(i * rows + g * size, i * rows + (g + 1) * size) for i in range(sets)]
        k_g = jnp.concatenate([k[span] for span in spans], axis=0)
        v_g = jnp.concatenate([v[span] for span in spans], axis=0)
        parts = []
        for start in range(0, width, pair):
            q2, k2, v2 = (t[:, start : start + pair] for t in (q_g, k_g, v_g))
            scores = lax.dot_general(
                q2,
                jnp.concatenate([k2 * low, k2 * high], axis=0),
                (((1,), (1,)), ((), ())),
                preferred_element_type=jnp.float32,
            )
            powers = jnp.exp2(scores).astype(jnp.bfloat16) * both
            upper = jnp.concatenate([v2 * low, low_all], axis=1)
            lower = jnp.concatenate([v2 * high, high_all], axis=1)
            parts.append(matmul(powers, jnp.concatenate([upper, lower], axis=0)))
        out.append(parts)
    return out


def projected(sums, w_out):
    pair = 2 * HEAD_DIM
    rows = [
        jnp.concatenate([(t[:, :pair] / t[:, pair:]).astype(jnp.bfloat16) for t in parts], axis=1)
        for parts in sums
    ]
    return matmul(jnp.concatenate(rows, axis=0), w_out[...])


def rounded(x):
    return x.astype(jnp.bfloat16).astype(jnp.float32)


def digits(shape, dimension, *bases):
    index = lax.broadcasted_iota(jnp.int32, shape, dimension)
    out = []
    for base in bases:
        out.append(index % base)
        index = index // base
    return out + [index]


def far_first(slow):
    return sorted(range(slow), key=lambda k: (k < slow // 2, k))


def pieces_of(sequence):
    return [[k] for k in sequence]


def row_sets(refs, slow, pieces):
    sets = []
    for start in range(0, len(refs), len(pieces)):
        found = {}
        for ref, piece in zip(refs[start : start + len(pieces)], pieces):
            size = ref.shape[0] // len(piece)
            for place, k in enumerate(piece):
                found[k] = ref[place * size : (place + 1) * size, :]
        sets.append([found[k] for k in range(slow)])
    return sets


def here():
    shard = lax.axis_index("patch")
    return lax.axis_index("pipe"), lax.div(shard, FAST), lax.rem(shard, FAST)


def at_work(stage, step, micro):
    number = step - stage
    return jnp.logical_and(number >= 0, number < micro)


def order_kernel(sizes, order_ref):
    slow, _, patches, hl = sizes
    shape = order_ref.shape
    patch, late, offset = digits(shape, 0, patches, hl)
    source = lax.broadcasted_iota(jnp.int32, shape, 1)
    wanted = (patch * slow + (offset ^ here()[1])) * hl + late
    order_ref[...] = jnp.where(wanted == source, 1.0, 0.0).astype(jnp.bfloat16)


def time_kernel(sizes, step, micro, *refs):
    shards, peers, patches, hl = sizes
    given = peers if step < micro else 0
    order_refs, refs = refs[: min(given, 1)], refs[min(given, 1) :]
    pieces = pieces_of(far_first(shards))
    came = peers * len(pieces) if step > 0 else 0
    input_refs, refs = refs[:given], refs[given:]
    came_refs, refs = refs[:came], refs[came:]
    (gain_ref, scale_ref, w_in_ref, w_out_ref), refs = refs[:4], refs[4:]
    y_refs, refs = refs[:shards], refs[shards:]
    x_ref = refs[0]
    rows = x_ref.shape[0] // peers
    stage = here()[0]

    @pl.when(at_work(stage, step, micro))
    def _():
        if given:

            @pl.when(stage == 0)
            def _():
                order = order_refs[0][...]
                for j, ref in enumerate(input_refs):
                    moved = matmul(order, ref[step]).astype(jnp.bfloat16)
                    x_ref[j * rows : (j + 1) * rows, :] = moved

        if came:

            @pl.when(stage != 0)
            def _():
                for j, blocks in enumerate(row_sets(came_refs, shards, pieces)):
                    x_ref[j * rows : (j + 1) * rows, :] = jnp.concatenate(blocks, axis=0)

        inner = min(patches, 8)
        groups = patches // inner
        xs = [
            regrouped(x_ref[j * rows : (j + 1) * rows, :].astype(jnp.float32), groups, inner)
            for j in range(peers)
        ]
        shape = (rows // groups, rows // groups * peers)
        mine = digits(shape, 0, inner)[0]
        theirs = digits(shape, 1, inner)[0]
        mask = jnp.where(mine == theirs, 1.0, 0.0).astype(jnp.bfloat16)
        normed = [row_norm(x, gain_ref[0]) for x in xs]
        w_in = w_in_ref.at[0, 0]
        q = queries(normed[0], lambda n: scale_ref[0, 0:1, n : n + 1], w_in)
        k, v = keys_and_values(jnp.concatenate(normed, axis=0), w_in)
        update = projected(attention_sums(q, k, v, groups, mask), w_out_ref.at[0, 0])
        y = regrouped(xs[0] + update, rows // (groups * inner), inner).astype(jnp.bfloat16)
        size = rows // shards
        for k in range(shards):
            y_refs[k][...] = y[k * size : (k + 1) * size]


def hour_groups(sizes):
    _, _, patches, hl = sizes
    groups = 2 if hl % 2 == 0 else 1
    return groups, hl // groups * patches


def patch_mask(sizes, fast, others, seen_ref):
    slow, _, patches, hl = sizes
    groups, inner = hour_groups(sizes)
    size = slow * inner
    shape = (size, size * len(others))
    _, my_slow, my_fast = here()

    def block_and_hour(dimension, first):
        patch, late, offset, other = digits(shape, dimension, patches, hl // groups, slow)
        shard = (offset ^ my_slow) * fast + ((other + first) ^ my_fast)
        return (shard * patches + patch) // PB, late

    query_block, query_hour = block_and_hour(0, 0)
    key_block, key_hour = block_and_hour(1, others[0])
    seen = None
    for kv in range(seen_ref.shape[1]):
        chosen = jnp.broadcast_to(seen_ref[0:1, kv : kv + 1], shape)
        for b in range(1, seen_ref.shape[0]):
            chosen = jnp.where(query_block == b, seen_ref[b : b + 1, kv : kv + 1], chosen)
        hit = jnp.where(chosen == key_block, 1.0, 0.0)
        seen = hit if seen is None else jnp.maximum(seen, hit)
    return jnp.where(query_hour == key_hour, seen, 0.0).astype(jnp.bfloat16)


def own_patch_kernel(sizes, fast, step, micro, seen_ref, *refs):
    slow = sizes[0]
    x_refs, (gain_ref, scale_ref, w_in_ref), (q_ref, sums_ref) = (
        refs[:slow],
        refs[slow : slow + 3],
        refs[slow + 3 :],
    )

    @pl.when(at_work(here()[0], step, micro))
    def _():
        groups, inner = hour_groups(sizes)
        x = jnp.concatenate([ref[...] for ref in x_refs], axis=0).astype(jnp.float32)
        normed = row_norm(regrouped(x, groups, inner), gain_ref[1])
        w_in = w_in_ref.at[0, 1]
        q = queries(normed, lambda n: scale_ref[0, 1:2, n : n + 1], w_in)
        k, v = keys_and_values(normed, w_in)
        q_ref[...] = q
        mask = patch_mask(sizes, fast, [0], seen_ref)
        sums = attention_sums(q, k, v, groups, mask)
        sums_ref[...] = jnp.concatenate([jnp.concatenate(t, axis=1) for t in sums], axis=0)


def patch_kernel(sizes, fast, step, micro, seen_ref, *refs):
    slow = sizes[0]
    count = fast * slow
    x_refs, refs, y_refs = refs[:count], refs[count:-slow], refs[-slow:]
    q_ref, sums_ref, gain_ref, w_in_ref, w_out_ref, up_ref, down_ref = refs
    pieces = pieces_of([0] + [k for k in far_first(slow) if k])

    @pl.when(at_work(here()[0], step, micro))
    def _():
        groups, inner = hour_groups(sizes)
        xs = [
            regrouped(jnp.concatenate(blocks, axis=0).astype(jnp.float32), groups, inner)
            for blocks in row_sets(x_refs, slow, pieces)
        ]
        x = xs[0]
        rows, width = x.shape
        normed = jnp.concatenate([row_norm(t, gain_ref[1]) for t in xs[1:]], axis=0)
        k, v = keys_and_values(normed, w_in_ref.at[0, 1])
        mask = patch_mask(sizes, fast, range(1, fast), seen_ref)
        more = attention_sums(q_ref[...], k, v, groups, mask)
        size = rows // groups
        sums = [
            [
                t + sums_ref[g * size : (g + 1) * size, i * 256 : (i + 1) * 256]
                for i, t in enumerate(parts)
            ]
            for g, parts in enumerate(more)
        ]
        x = rounded(x + projected(sums, w_out_ref.at[0, 1]))
        normed = row_norm(x, gain_ref[2])
        total = x
        chunk = 512
        for start in range(0, up_ref.shape[2], chunk):
            u = matmul(normed, up_ref[0, :, start : start + chunk])
            bent = jnp.tanh(u * (0.7978845608028654 + 0.035677408136300125 * (u * u)))
            hidden = (0.5 * u * (1.0 + bent)).astype(jnp.bfloat16)
            total = total + matmul(hidden, down_ref[0, start : start + chunk, :])
        y = regrouped(total, slow, inner).astype(jnp.bfloat16)
        size = rows // slow
        for k in range(slow):
            y_refs[k][...] = y[k * size : (k + 1) * size]


def write_rows(sizes, x, y_ref):
    slow, _, patches, hl = sizes
    rows = slow * patches * hl
    late, shard, patch = digits((rows, rows), 0, hl, slow)
    source = lax.broadcasted_iota(jnp.int32, (rows, rows), 1)
    wanted = ((shard ^ here()[1]) * hl + late) * patches + patch
    order = jnp.where(wanted == source, 1.0, 0.0).astype(jnp.bfloat16)
    y_ref[...] = matmul(order, x).astype(jnp.bfloat16)


def early_kernel(sizes, pipes, *refs):
    x_refs, y_ref = refs[:pipes], refs[-1]
    for stage, x_ref in enumerate(x_refs):

        @pl.when(here()[0] == stage)
        def _():
            write_rows(sizes, x_ref[...], y_ref)


def final_kernel(sizes, *refs):
    x_refs, y_ref = refs[: sizes[0]], refs[-1]
    write_rows(sizes, jnp.concatenate([ref[...] for ref in x_refs], axis=0), y_ref)


VMEM = pl.BlockSpec(memory_space=pltpu.VMEM)
PARAMS = pltpu.CompilerParams(vmem_limit_bytes=32 << 20)
COST = pl.CostEstimate(flops=5 << 30, bytes_accessed=1 << 20, transcendentals=1 << 20)


def blocks_of(count, rows, width):
    return [jax.ShapeDtypeStruct((rows // count, width), jnp.bfloat16)] * count


def call_order(sizes, rows):
    return pl.pallas_call(
        functools.partial(order_kernel, sizes),
        out_shape=jax.ShapeDtypeStruct((rows, rows), jnp.bfloat16),
        in_specs=[],
        out_specs=VMEM,
        compiler_params=PARAMS,
        cost_estimate=COST,
        name="input_order",
    )()


def call_time(sizes, step, micro, shape, order, given, came, gains, scales, w_in, w_out):
    rows, width = shape
    xs = ([order] if given else []) + list(given) + list(came)
    return pl.pallas_call(
        functools.partial(time_kernel, sizes, step, micro),
        out_shape=blocks_of(sizes[0], rows, width),
        in_specs=[VMEM] * (len(xs) + 4),
        out_specs=[VMEM] * sizes[0],
        scratch_shapes=[pltpu.VMEM((rows * sizes[1], width), jnp.bfloat16)],
        compiler_params=PARAMS,
        cost_estimate=COST,
        name="time_attention",
    )(*xs, gains, scales, w_in, w_out)


def call_own_patch(sizes, fast, step, micro, shape, seen, xs, gains, scales, w_in):
    rows, width = shape
    return pl.pallas_call(
        functools.partial(own_patch_kernel, sizes, fast, step, micro),
        out_shape=[
            jax.ShapeDtypeStruct((rows, width), jnp.bfloat16),
            jax.ShapeDtypeStruct((rows, 2 * width), jnp.float32),
        ],
        in_specs=[VMEM] * (len(xs) + 4),
        out_specs=[VMEM, VMEM],
        compiler_params=PARAMS,
        cost_estimate=COST,
        name="own_patch_attention",
    )(seen, *xs, gains, scales, w_in)


def call_patch(sizes, fast, step, micro, shape, seen, xs, weights):
    rows, width = shape
    return pl.pallas_call(
        functools.partial(patch_kernel, sizes, fast, step, micro),
        out_shape=blocks_of(sizes[0], rows, width),
        in_specs=[VMEM] * (1 + len(xs) + len(weights)),
        out_specs=[VMEM] * sizes[0],
        compiler_params=PARAMS,
        cost_estimate=COST,
        name="patch_attention_and_ffn",
    )(seen, *xs, *weights)


def call_write(kernel, sizes, shape, number, xs, out):
    given = [] if out is None else [out]
    return pl.pallas_call(
        kernel,
        out_shape=jax.ShapeDtypeStruct(shape, jnp.bfloat16),
        grid=(1,),
        in_specs=[VMEM] * len(xs) + [pl.BlockSpec(memory_space=pl.ANY)] * len(given),
        out_specs=pl.BlockSpec((None,) + shape[1:], lambda i: (number, 0, 0)),
        input_output_aliases={len(xs): 0} if given else {},
        compiler_params=PARAMS,
        name="final_order",
    )(*xs, *given)


def flipped(x, axis, k):
    return lax.ppermute(x, axis, [(s, s ^ k) for s in range(lax.axis_size(axis))])


def handed_on(x, k):
    pipes, shards = lax.axis_size("pipe"), lax.axis_size("patch")
    pairs = [
        (stage * shards + s, (stage + 1) % pipes * shards + (s ^ k))
        for stage in range(pipes)
        for s in range(shards)
    ]
    return lax.ppermute(x, ("pipe", "patch"), pairs)


def local(inputs, seen, gains, scales, w_in, w_out, w_up, w_down):
    shards = lax.axis_size("patch")
    peers = lax.axis_size("hour")
    pipes = lax.axis_size("pipe")
    micro, patches, hours, width = inputs.shape
    rows = patches * hours
    fast = FAST
    slow = shards // fast
    sizes = (slow, peers, patches, hours // slow)
    last = pipes - 1
    gains = gains.reshape(gains.shape[1], 1, width)
    far = far_first(slow)
    order = call_order(sizes, rows)

    def gathered(blocks, axis, count, sequence):
        own = [jnp.concatenate([blocks[k] for k in piece]) for piece in pieces_of(sequence)]
        out = list(own)
        for j in range(1, count):
            out += [flipped(piece, axis, j) for piece in own]
        return out

    def along_slow(blocks, send, first):
        got = {k: send(blocks[k], k * fast) for k in far if k >= first}
        return [got.get(k, blocks[k]) for k in range(slow)]

    def in_stage(x, k):
        return flipped(x, "patch", k)

    def onward(x):
        return lax.ppermute(x, "pipe", [(s, (s + 1) % pipes) for s in range(pipes)])

    x = inputs.reshape(micro, rows, width)
    given = [x] + [flipped(x, "hour", j) for j in range(1, peers)]
    came = []
    out = None
    back = []
    for step in range(micro + pipes - 1):
        now = given if step < micro else []
        mixed = call_time(
            sizes, step, micro, x.shape[1:], order, now, came, gains, scales, w_in, w_out
        )
        own = along_slow(mixed, in_stage, 1)
        spread = gathered(own, "patch", fast, [0] + [k for k in far if k])
        begun = call_own_patch(
            sizes, fast, step, micro, x.shape[1:], seen, own, gains, scales, w_in
        )
        if back:
            spread, back = lax.optimization_barrier((spread, back))
            write = functools.partial(early_kernel, sizes, pipes)
            out = call_write(write, sizes, x.shape, step - pipes, back, out)
        at_end = step == micro + pipes - 2
        weights = [*begun, gains, w_in, w_out, w_up, w_down]
        done = call_patch(sizes, fast, step, micro, x.shape[1:], seen, spread, weights)
        if not at_end:
            arrived = along_slow(done, handed_on, 0)
            came = gathered(arrived, "hour", peers, far)
            if step >= last:
                back = [jnp.concatenate(arrived)]
                for _ in range(1, pipes):
                    back.append(onward(back[-1]))
    stage = lax.axis_index("pipe")
    blocks = {}
    for count, k in enumerate(far):
        own = done[k]
        if count >= slow // 2:
            own, blocks[far[0]] = lax.optimization_barrier((own, blocks[far[0]]))
        chosen = block = own
        for hop in range(pipes - 1):
            block = onward(block)
            chosen = jnp.where(stage == hop, block, chosen)
        blocks[k] = chosen
    blocks = {k: in_stage(blocks[k], k * fast) if k else blocks[k] for k in far}
    blocks = [blocks[k] for k in range(slow)]
    write = functools.partial(final_kernel, sizes)
    out = call_write(write, sizes, x.shape, micro - 1, blocks, out)
    return out.reshape(inputs.shape)


def solution(mesh):
    placed = (
        P(None, "patch", "hour", None),
        P(),
        P("pipe", None, None),
        P("pipe", None, None),
        P("pipe", None, None, None),
        P("pipe", None, None, None),
        P("pipe", None, None),
        P("pipe", None, None),
    )
    return jax.shard_map(
        local, mesh=mesh, in_specs=placed, out_specs=P(None, "patch", "hour", None), check_vma=False
    )
```

```python
import functools

import jax
import jax.numpy as jnp
from jax import lax
from jax.experimental import pallas as pl
from jax.experimental.pallas import tpu as pltpu
from jax.sharding import PartitionSpec as P

HEADS = 8
HEAD_DIM = 64
PB = 64
FAST = 2
LOG2E = 1.4426950408889634


def row_norm(x, gain):
    factor = lax.rsqrt(jnp.mean(x * x, axis=-1, keepdims=True) + 1e-05)
    return (x * factor * gain).astype(jnp.bfloat16)


def matmul(a, b):
    return jnp.dot(a, b, preferred_element_type=jnp.float32)


def same_head():
    rows = lax.broadcasted_iota(jnp.int32, (256, 256), 0) // HEAD_DIM
    cols = lax.broadcasted_iota(jnp.int32, (256, 256), 1) // HEAD_DIM
    return jnp.where(rows == cols, 1.0, 0.0).astype(jnp.bfloat16)


def head_factor(values, group):
    squares = (values * values).astype(jnp.bfloat16)
    halves = [
        matmul(squares[:, start : start + 256], group) for start in range(0, values.shape[1], 256)
    ]
    sums = jnp.concatenate(halves, axis=1)
    return lax.rsqrt(sums * (1.0 / HEAD_DIM) + 1e-06)


def regrouped(x, groups, inner):
    outer = x.shape[0] // (groups * inner)
    starts = [(o * groups + g) * inner for g in range(groups) for o in range(outer)]
    return jnp.concatenate([x[start : start + inner] for start in starts], axis=0)


def queries(normed, scale_of, w_in):
    width = normed.shape[1]
    head = lax.broadcasted_iota(jnp.int32, (1, width), 1) // HEAD_DIM
    scale = jnp.zeros((1, width), jnp.float32)
    for n in range(HEADS):
        scale = jnp.where(head == n, scale_of(n) * (LOG2E / HEAD_DIM), scale)
    q = matmul(normed, w_in[:, :width])
    return (q * head_factor(q, same_head()) * scale).astype(jnp.bfloat16)


def keys_and_values(normed, w_in):
    width = normed.shape[1]
    k = matmul(normed, w_in[:, width : 2 * width])
    v = matmul(normed, w_in[:, 2 * width :]).astype(jnp.bfloat16)
    return (k * head_factor(k, same_head())).astype(jnp.bfloat16), v


def attention_sums(q, k, v, groups, mask):
    rows, width = q.shape
    pair = 2 * HEAD_DIM
    size = rows // groups
    sets = k.shape[0] // rows
    keys = size * sets
    first = lax.broadcasted_iota(jnp.int32, (1, pair), 1) < HEAD_DIM
    low = jnp.where(first, 1.0, 0.0).astype(jnp.bfloat16)
    high = jnp.where(first, 0.0, 1.0).astype(jnp.bfloat16)
    low_all = jnp.broadcast_to(low, (keys, pair))
    high_all = jnp.broadcast_to(high, (keys, pair))
    both = jnp.concatenate([mask, mask], axis=1)
    out = []
    for g in range(groups):
        q_g = q[g * size : (g + 1) * size]
        spans = [slice(i * rows + g * size, i * rows + (g + 1) * size) for i in range(sets)]
        k_g = jnp.concatenate([k[span] for span in spans], axis=0)
        v_g = jnp.concatenate([v[span] for span in spans], axis=0)
        parts = []
        for start in range(0, width, pair):
            q2, k2, v2 = (t[:, start : start + pair] for t in (q_g, k_g, v_g))
            scores = lax.dot_general(
                q2,
                jnp.concatenate([k2 * low, k2 * high], axis=0),
                (((1,), (1,)), ((), ())),
                preferred_element_type=jnp.float32,
            )
            powers = jnp.exp2(scores).astype(jnp.bfloat16) * both
            upper = jnp.concatenate([v2 * low, low_all], axis=1)
            lower = jnp.concatenate([v2 * high, high_all], axis=1)
            parts.append(matmul(powers, jnp.concatenate([upper, lower], axis=0)))
        out.append(parts)
    return out


def projected(sums, w_out):
    pair = 2 * HEAD_DIM
    rows = [
        jnp.concatenate([(t[:, :pair] / t[:, pair:]).astype(jnp.bfloat16) for t in parts], axis=1)
        for parts in sums
    ]
    return matmul(jnp.concatenate(rows, axis=0), w_out[...])


def rounded(x):
    return x.astype(jnp.bfloat16).astype(jnp.float32)


def digits(shape, dimension, *bases):
    index = lax.broadcasted_iota(jnp.int32, shape, dimension)
    out = []
    for base in bases:
        out.append(index % base)
        index = index // base
    return out + [index]


def far_first(slow):
    return sorted(range(slow), key=lambda k: (k < slow // 2, k))


def pieces_of(sequence):
    return [[k] for k in sequence]


def row_sets(refs, slow, pieces):
    sets = []
    for start in range(0, len(refs), len(pieces)):
        found = {}
        for ref, piece in zip(refs[start : start + len(pieces)], pieces):
            size = ref.shape[0] // len(piece)
            for place, k in enumerate(piece):
                found[k] = ref[place * size : (place + 1) * size, :]
        sets.append([found[k] for k in range(slow)])
    return sets


def here():
    shard = lax.axis_index("patch")
    return lax.axis_index("pipe"), lax.div(shard, FAST), lax.rem(shard, FAST)


def at_work(stage, step, micro):
    number = step - stage
    return jnp.logical_and(number >= 0, number < micro)


def order_kernel(sizes, order_ref):
    slow, _, patches, hl = sizes
    shape = order_ref.shape
    patch, late, offset = digits(shape, 0, patches, hl)
    source = lax.broadcasted_iota(jnp.int32, shape, 1)
    wanted = (patch * slow + (offset ^ here()[1])) * hl + late
    order_ref[...] = jnp.where(wanted == source, 1.0, 0.0).astype(jnp.bfloat16)


def time_kernel(sizes, step, micro, *refs):
    shards, peers, patches, hl = sizes
    given = peers if step < micro else 0
    order_refs, refs = refs[: min(given, 1)], refs[min(given, 1) :]
    pieces = pieces_of(far_first(shards))
    came = peers * len(pieces) if step > 0 else 0
    input_refs, refs = refs[:given], refs[given:]
    came_refs, refs = refs[:came], refs[came:]
    (gain_ref, scale_ref, w_in_ref, w_out_ref), refs = refs[:4], refs[4:]
    y_refs, refs = refs[:shards], refs[shards:]
    x_ref = refs[0]
    rows = x_ref.shape[0] // peers
    stage = here()[0]

    @pl.when(at_work(stage, step, micro))
    def _():
        if given:

            @pl.when(stage == 0)
            def _():
                order = order_refs[0][...]
                for j, ref in enumerate(input_refs):
                    moved = matmul(order, ref[step]).astype(jnp.bfloat16)
                    x_ref[j * rows : (j + 1) * rows, :] = moved

        if came:

            @pl.when(stage != 0)
            def _():
                for j, blocks in enumerate(row_sets(came_refs, shards, pieces)):
                    x_ref[j * rows : (j + 1) * rows, :] = jnp.concatenate(blocks, axis=0)

        inner = min(patches, 8)
        groups = patches // inner
        xs = [
            regrouped(x_ref[j * rows : (j + 1) * rows, :].astype(jnp.float32), groups, inner)
            for j in range(peers)
        ]
        shape = (rows // groups, rows // groups * peers)
        mine = digits(shape, 0, inner)[0]
        theirs = digits(shape, 1, inner)[0]
        mask = jnp.where(mine == theirs, 1.0, 0.0).astype(jnp.bfloat16)
        normed = [row_norm(x, gain_ref[0]) for x in xs]
        w_in = w_in_ref.at[0, 0]
        q = queries(normed[0], lambda n: scale_ref[0, 0:1, n : n + 1], w_in)
        k, v = keys_and_values(jnp.concatenate(normed, axis=0), w_in)
        update = projected(attention_sums(q, k, v, groups, mask), w_out_ref.at[0, 0])
        y = regrouped(xs[0] + update, rows // (groups * inner), inner).astype(jnp.bfloat16)
        size = rows // shards
        for k in range(shards):
            y_refs[k][...] = y[k * size : (k + 1) * size]


def hour_groups(sizes):
    _, _, patches, hl = sizes
    groups = 2 if hl % 2 == 0 else 1
    return groups, hl // groups * patches


def patch_mask(sizes, fast, others, seen_ref):
    slow, _, patches, hl = sizes
    groups, inner = hour_groups(sizes)
    size = slow * inner
    shape = (size, size * len(others))
    _, my_slow, my_fast = here()

    def block_and_hour(dimension, first):
        patch, late, offset, other = digits(shape, dimension, patches, hl // groups, slow)
        shard = (offset ^ my_slow) * fast + ((other + first) ^ my_fast)
        return (shard * patches + patch) // PB, late

    query_block, query_hour = block_and_hour(0, 0)
    key_block, key_hour = block_and_hour(1, others[0])
    seen = None
    for kv in range(seen_ref.shape[1]):
        chosen = jnp.broadcast_to(seen_ref[0:1, kv : kv + 1], shape)
        for b in range(1, seen_ref.shape[0]):
            chosen = jnp.where(query_block == b, seen_ref[b : b + 1, kv : kv + 1], chosen)
        hit = jnp.where(chosen == key_block, 1.0, 0.0)
        seen = hit if seen is None else jnp.maximum(seen, hit)
    return jnp.where(query_hour == key_hour, seen, 0.0).astype(jnp.bfloat16)


def own_patch_kernel(sizes, fast, step, micro, seen_ref, *refs):
    slow = sizes[0]
    x_refs, (gain_ref, scale_ref, w_in_ref), (q_ref, sums_ref) = (
        refs[:slow],
        refs[slow : slow + 3],
        refs[slow + 3 :],
    )

    @pl.when(at_work(here()[0], step, micro))
    def _():
        groups, inner = hour_groups(sizes)
        x = jnp.concatenate([ref[...] for ref in x_refs], axis=0).astype(jnp.float32)
        normed = row_norm(regrouped(x, groups, inner), gain_ref[1])
        w_in = w_in_ref.at[0, 1]
        q = queries(normed, lambda n: scale_ref[0, 1:2, n : n + 1], w_in)
        k, v = keys_and_values(normed, w_in)
        q_ref[...] = q
        mask = patch_mask(sizes, fast, [0], seen_ref)
        sums = attention_sums(q, k, v, groups, mask)
        sums_ref[...] = jnp.concatenate([jnp.concatenate(t, axis=1) for t in sums], axis=0)


def feed_forward(x, gain, up_ref, down_ref):
    normed = row_norm(x, gain)
    total = x
    chunk = 512
    for start in range(0, up_ref.shape[2], chunk):
        u = matmul(normed, up_ref[0, :, start : start + chunk])
        bent = jnp.tanh(u * (0.7978845608028654 + 0.035677408136300125 * (u * u)))
        hidden = (0.5 * u * (1.0 + bent)).astype(jnp.bfloat16)
        total = total + matmul(hidden, down_ref[0, start : start + chunk, :])
    return total


def write_blocks(y, inner, y_refs):
    y = regrouped(y, len(y_refs), inner).astype(jnp.bfloat16)
    size = y.shape[0] // len(y_refs)
    for k, y_ref in enumerate(y_refs):
        y_ref[...] = y[k * size : (k + 1) * size]


def patch_kernel(sizes, fast, near, step, micro, seen_ref, *refs):
    slow = sizes[0]
    count = fast * slow
    outs = slow - near + (1 if near else 0)
    x_refs, refs, y_refs = refs[:count], refs[count:-outs], refs[-outs:]
    q_ref, sums_ref, gain_ref, w_in_ref, w_out_ref, up_ref, down_ref = refs
    pieces = pieces_of([0] + [k for k in far_first(slow) if k])

    @pl.when(at_work(here()[0], step, micro))
    def _():
        groups, inner = hour_groups(sizes)
        xs = [
            regrouped(jnp.concatenate(blocks, axis=0).astype(jnp.float32), groups, inner)
            for blocks in row_sets(x_refs, slow, pieces)
        ]
        x = xs[0]
        rows, width = x.shape
        normed = jnp.concatenate([row_norm(t, gain_ref[1]) for t in xs[1:]], axis=0)
        k, v = keys_and_values(normed, w_in_ref.at[0, 1])
        mask = patch_mask(sizes, fast, range(1, fast), seen_ref)
        more = attention_sums(q_ref[...], k, v, groups, mask)
        size = rows // groups
        sums = [
            [
                t + sums_ref[g * size : (g + 1) * size, i * 256 : (i + 1) * 256]
                for i, t in enumerate(parts)
            ]
            for g, parts in enumerate(more)
        ]
        x = rounded(x + projected(sums, w_out_ref.at[0, 1]))
        first = near * inner
        if near:
            held = [x[g * size : g * size + first] for g in range(groups)]
            y_refs[0][...] = jnp.concatenate(held, axis=0).astype(jnp.bfloat16)
            x = jnp.concatenate([x[g * size + first : (g + 1) * size] for g in range(groups)], axis=0)
        y = feed_forward(x, gain_ref[2], up_ref, down_ref)
        write_blocks(y, inner, y_refs[1:] if near else y_refs)


def near_kernel(sizes, step, micro, x_ref, gain_ref, up_ref, down_ref, *y_refs):
    @pl.when(at_work(here()[0], step, micro))
    def _():
        x = x_ref[...].astype(jnp.float32)
        inner = hour_groups(sizes)[1]
        write_blocks(feed_forward(x, gain_ref[2], up_ref, down_ref), inner, y_refs)


def write_rows(sizes, x, y_ref):
    slow, _, patches, hl = sizes
    rows = slow * patches * hl
    late, shard, patch = digits((rows, rows), 0, hl, slow)
    source = lax.broadcasted_iota(jnp.int32, (rows, rows), 1)
    wanted = ((shard ^ here()[1]) * hl + late) * patches + patch
    order = jnp.where(wanted == source, 1.0, 0.0).astype(jnp.bfloat16)
    y_ref[...] = matmul(order, x).astype(jnp.bfloat16)


def early_kernel(sizes, pipes, *refs):
    x_refs, y_ref = refs[:pipes], refs[-1]
    for stage, x_ref in enumerate(x_refs):

        @pl.when(here()[0] == stage)
        def _():
            write_rows(sizes, x_ref[...], y_ref)


def final_kernel(sizes, *refs):
    x_refs, y_ref = refs[: sizes[0]], refs[-1]
    write_rows(sizes, jnp.concatenate([ref[...] for ref in x_refs], axis=0), y_ref)


VMEM = pl.BlockSpec(memory_space=pltpu.VMEM)
PARAMS = pltpu.CompilerParams(vmem_limit_bytes=32 << 20)
COST = pl.CostEstimate(flops=5 << 30, bytes_accessed=1 << 20, transcendentals=1 << 20)


def blocks_of(count, rows, width):
    return [jax.ShapeDtypeStruct((rows // count, width), jnp.bfloat16)] * count


def call_order(sizes, rows):
    return pl.pallas_call(
        functools.partial(order_kernel, sizes),
        out_shape=jax.ShapeDtypeStruct((rows, rows), jnp.bfloat16),
        in_specs=[],
        out_specs=VMEM,
        compiler_params=PARAMS,
        cost_estimate=COST,
        name="input_order",
    )()


def call_time(sizes, step, micro, shape, order, given, came, gains, scales, w_in, w_out):
    rows, width = shape
    xs = ([order] if given else []) + list(given) + list(came)
    return pl.pallas_call(
        functools.partial(time_kernel, sizes, step, micro),
        out_shape=blocks_of(sizes[0], rows, width),
        in_specs=[VMEM] * (len(xs) + 4),
        out_specs=[VMEM] * sizes[0],
        scratch_shapes=[pltpu.VMEM((rows * sizes[1], width), jnp.bfloat16)],
        compiler_params=PARAMS,
        cost_estimate=COST,
        name="time_attention",
    )(*xs, gains, scales, w_in, w_out)


def call_own_patch(sizes, fast, step, micro, shape, seen, xs, gains, scales, w_in):
    rows, width = shape
    return pl.pallas_call(
        functools.partial(own_patch_kernel, sizes, fast, step, micro),
        out_shape=[
            jax.ShapeDtypeStruct((rows, width), jnp.bfloat16),
            jax.ShapeDtypeStruct((rows, 2 * width), jnp.float32),
        ],
        in_specs=[VMEM] * (len(xs) + 4),
        out_specs=[VMEM, VMEM],
        compiler_params=PARAMS,
        cost_estimate=COST,
        name="own_patch_attention",
    )(seen, *xs, gains, scales, w_in)


def call_patch(sizes, fast, near, step, micro, shape, seen, xs, weights):
    rows, width = shape
    slow = sizes[0]
    blocks = blocks_of(slow, rows, width)
    outs = blocks[near:]
    if near:
        outs = [jax.ShapeDtypeStruct((rows // slow * near, width), jnp.bfloat16)] + outs
    outs = pl.pallas_call(
        functools.partial(patch_kernel, sizes, fast, near, step, micro),
        out_shape=outs,
        in_specs=[VMEM] * (1 + len(xs) + len(weights)),
        out_specs=[VMEM] * len(outs),
        compiler_params=PARAMS,
        cost_estimate=COST,
        name="patch_attention_and_ffn",
    )(seen, *xs, *weights)
    if not near:
        return list(outs)
    gains, _, _, w_up, w_down = weights[-5:]
    near_blocks = pl.pallas_call(
        functools.partial(near_kernel, sizes, step, micro),
        out_shape=blocks[:near],
        in_specs=[VMEM] * 4,
        out_specs=[VMEM] * near,
        compiler_params=PARAMS,
        cost_estimate=COST,
        name="near_ffn",
    )(outs[0], gains, w_up, w_down)
    return list(near_blocks) + list(outs[1:])


def call_write(kernel, sizes, shape, number, xs, out):
    given = [] if out is None else [out]
    return pl.pallas_call(
        kernel,
        out_shape=jax.ShapeDtypeStruct(shape, jnp.bfloat16),
        grid=(1,),
        in_specs=[VMEM] * len(xs) + [pl.BlockSpec(memory_space=pl.ANY)] * len(given),
        out_specs=pl.BlockSpec((None,) + shape[1:], lambda i: (number, 0, 0)),
        input_output_aliases={len(xs): 0} if given else {},
        compiler_params=PARAMS,
        name="final_order",
    )(*xs, *given)


def flipped(x, axis, k):
    return lax.ppermute(x, axis, [(s, s ^ k) for s in range(lax.axis_size(axis))])


def handed_on(x, k):
    pipes, shards = lax.axis_size("pipe"), lax.axis_size("patch")
    pairs = [
        (stage * shards + s, (stage + 1) % pipes * shards + (s ^ k))
        for stage in range(pipes)
        for s in range(shards)
    ]
    return lax.ppermute(x, ("pipe", "patch"), pairs)


def local(inputs, seen, gains, scales, w_in, w_out, w_up, w_down):
    shards = lax.axis_size("patch")
    peers = lax.axis_size("hour")
    pipes = lax.axis_size("pipe")
    micro, patches, hours, width = inputs.shape
    rows = patches * hours
    fast = FAST
    slow = shards // fast
    sizes = (slow, peers, patches, hours // slow)
    last = pipes - 1
    gains = gains.reshape(gains.shape[1], 1, width)
    far = far_first(slow)
    order = call_order(sizes, rows)

    def gathered(blocks, axis, count, sequence):
        own = [jnp.concatenate([blocks[k] for k in piece]) for piece in pieces_of(sequence)]
        out = list(own)
        for j in range(1, count):
            out += [flipped(piece, axis, j) for piece in own]
        return out

    def along_slow(blocks, send, first):
        got = {k: send(blocks[k], k * fast) for k in far if k >= first}
        return [got.get(k, blocks[k]) for k in range(slow)]

    def in_stage(x, k):
        return flipped(x, "patch", k)

    def onward(x):
        return lax.ppermute(x, "pipe", [(s, (s + 1) % pipes) for s in range(pipes)])

    x = inputs.reshape(micro, rows, width)
    given = [x] + [flipped(x, "hour", j) for j in range(1, peers)]
    came = []
    out = None
    back = []
    for step in range(micro + pipes - 1):
        now = given if step < micro else []
        mixed = call_time(
            sizes, step, micro, x.shape[1:], order, now, came, gains, scales, w_in, w_out
        )
        own = along_slow(mixed, in_stage, 1)
        spread = gathered(own, "patch", fast, [0] + [k for k in far if k])
        begun = call_own_patch(
            sizes, fast, step, micro, x.shape[1:], seen, own, gains, scales, w_in
        )
        if back:
            spread, back = lax.optimization_barrier((spread, back))
            write = functools.partial(early_kernel, sizes, pipes)
            out = call_write(write, sizes, x.shape, step - pipes, back, out)
        at_end = step == micro + pipes - 2
        weights = [*begun, gains, w_in, w_out, w_up, w_down]
        near = slow // 2 if at_end else 0
        done = call_patch(sizes, fast, near, step, micro, x.shape[1:], seen, spread, weights)
        if not at_end:
            arrived = along_slow(done, handed_on, 0)
            came = gathered(arrived, "hour", peers, far)
            if step >= last:
                back = [jnp.concatenate(arrived)]
                for _ in range(1, pipes):
                    back.append(onward(back[-1]))
    stage = lax.axis_index("pipe")
    blocks = {}
    for k in far:
        chosen = block = done[k]
        for hop in range(pipes - 1):
            block = onward(block)
            chosen = jnp.where(stage == hop, block, chosen)
        blocks[k] = chosen
    blocks = {k: in_stage(blocks[k], k * fast) if k else blocks[k] for k in far}
    blocks = [blocks[k] for k in range(slow)]
    write = functools.partial(final_kernel, sizes)
    out = call_write(write, sizes, x.shape, micro - 1, blocks, out)
    return out.reshape(inputs.shape)


def solution(mesh):
    placed = (
        P(None, "patch", "hour", None),
        P(),
        P("pipe", None, None),
        P("pipe", None, None),
        P("pipe", None, None, None),
        P("pipe", None, None, None),
        P("pipe", None, None),
        P("pipe", None, None),
    )
    return jax.shard_map(
        local, mesh=mesh, in_specs=placed, out_specs=P(None, "patch", "hour", None), check_vma=False
    )
```

```python
import functools

import jax
import jax.numpy as jnp
from jax import lax
from jax.experimental import pallas as pl
from jax.experimental.pallas import tpu as pltpu
from jax.sharding import PartitionSpec as P

HEADS = 8
HEAD_DIM = 64
PB = 64
FAST = 2
LOG2E = 1.4426950408889634


def row_norm(x, gain):
    factor = lax.rsqrt(jnp.mean(x * x, axis=-1, keepdims=True) + 1e-05)
    return (x * factor * gain).astype(jnp.bfloat16)


def matmul(a, b):
    return jnp.dot(a, b, preferred_element_type=jnp.float32)


def same_head():
    rows = lax.broadcasted_iota(jnp.int32, (256, 256), 0) // HEAD_DIM
    cols = lax.broadcasted_iota(jnp.int32, (256, 256), 1) // HEAD_DIM
    return jnp.where(rows == cols, 1.0, 0.0).astype(jnp.bfloat16)


def head_factor(values, group):
    squares = (values * values).astype(jnp.bfloat16)
    halves = [
        matmul(squares[:, start : start + 256], group) for start in range(0, values.shape[1], 256)
    ]
    sums = jnp.concatenate(halves, axis=1)
    return lax.rsqrt(sums * (1.0 / HEAD_DIM) + 1e-06)


def regrouped(x, groups, inner):
    outer = x.shape[0] // (groups * inner)
    starts = [(o * groups + g) * inner for g in range(groups) for o in range(outer)]
    return jnp.concatenate([x[start : start + inner] for start in starts], axis=0)


def queries(normed, scale_of, w_in):
    width = normed.shape[1]
    head = lax.broadcasted_iota(jnp.int32, (1, width), 1) // HEAD_DIM
    scale = jnp.zeros((1, width), jnp.float32)
    for n in range(HEADS):
        scale = jnp.where(head == n, scale_of(n) * (LOG2E / HEAD_DIM), scale)
    q = matmul(normed, w_in[:, :width])
    return (q * head_factor(q, same_head()) * scale).astype(jnp.bfloat16)


def keys_and_values(normed, w_in):
    width = normed.shape[1]
    k = matmul(normed, w_in[:, width : 2 * width])
    v = matmul(normed, w_in[:, 2 * width :]).astype(jnp.bfloat16)
    return (k * head_factor(k, same_head())).astype(jnp.bfloat16), v


def attention_sums(q, k, v, groups, mask):
    rows, width = q.shape
    pair = 2 * HEAD_DIM
    size = rows // groups
    sets = k.shape[0] // rows
    keys = size * sets
    first = lax.broadcasted_iota(jnp.int32, (1, pair), 1) < HEAD_DIM
    low = jnp.where(first, 1.0, 0.0).astype(jnp.bfloat16)
    high = jnp.where(first, 0.0, 1.0).astype(jnp.bfloat16)
    low_all = jnp.broadcast_to(low, (keys, pair))
    high_all = jnp.broadcast_to(high, (keys, pair))
    both = jnp.concatenate([mask, mask], axis=1)
    out = []
    for g in range(groups):
        q_g = q[g * size : (g + 1) * size]
        spans = [slice(i * rows + g * size, i * rows + (g + 1) * size) for i in range(sets)]
        k_g = jnp.concatenate([k[span] for span in spans], axis=0)
        v_g = jnp.concatenate([v[span] for span in spans], axis=0)
        parts = []
        for start in range(0, width, pair):
            q2, k2, v2 = (t[:, start : start + pair] for t in (q_g, k_g, v_g))
            scores = lax.dot_general(
                q2,
                jnp.concatenate([k2 * low, k2 * high], axis=0),
                (((1,), (1,)), ((), ())),
                preferred_element_type=jnp.float32,
            )
            powers = jnp.exp2(scores).astype(jnp.bfloat16) * both
            upper = jnp.concatenate([v2 * low, low_all], axis=1)
            lower = jnp.concatenate([v2 * high, high_all], axis=1)
            parts.append(matmul(powers, jnp.concatenate([upper, lower], axis=0)))
        out.append(parts)
    return out


def projected(sums, w_out):
    pair = 2 * HEAD_DIM
    rows = [
        jnp.concatenate([(t[:, :pair] / t[:, pair:]).astype(jnp.bfloat16) for t in parts], axis=1)
        for parts in sums
    ]
    return matmul(jnp.concatenate(rows, axis=0), w_out[...])


def rounded(x):
    return x.astype(jnp.bfloat16).astype(jnp.float32)


def digits(shape, dimension, *bases):
    index = lax.broadcasted_iota(jnp.int32, shape, dimension)
    out = []
    for base in bases:
        out.append(index % base)
        index = index // base
    return out + [index]


def far_first(slow):
    return sorted(range(slow), key=lambda k: (k < slow // 2, k))


def pieces_of(sequence):
    return [[k] for k in sequence]


def row_sets(refs, slow, pieces):
    sets = []
    for start in range(0, len(refs), len(pieces)):
        found = {}
        for ref, piece in zip(refs[start : start + len(pieces)], pieces):
            size = ref.shape[0] // len(piece)
            for place, k in enumerate(piece):
                found[k] = ref[place * size : (place + 1) * size, :]
        sets.append([found[k] for k in range(slow)])
    return sets


def here():
    shard = lax.axis_index("patch")
    return lax.axis_index("pipe"), lax.div(shard, FAST), lax.rem(shard, FAST)


def at_work(stage, step, micro):
    number = step - stage
    return jnp.logical_and(number >= 0, number < micro)


def order_kernel(sizes, order_ref):
    slow, _, patches, hl = sizes
    shape = order_ref.shape
    patch, late, offset = digits(shape, 0, patches, hl)
    source = lax.broadcasted_iota(jnp.int32, shape, 1)
    wanted = (patch * slow + (offset ^ here()[1])) * hl + late
    order_ref[...] = jnp.where(wanted == source, 1.0, 0.0).astype(jnp.bfloat16)


def time_kernel(sizes, step, micro, *refs):
    shards, peers, patches, hl = sizes
    given = peers if step < micro else 0
    order_refs, refs = refs[: min(given, 1)], refs[min(given, 1) :]
    pieces = pieces_of(far_first(shards))
    came = peers * len(pieces) if step > 0 else 0
    input_refs, refs = refs[:given], refs[given:]
    came_refs, refs = refs[:came], refs[came:]
    (gain_ref, scale_ref, w_in_ref, w_out_ref), refs = refs[:4], refs[4:]
    y_refs, refs = refs[:shards], refs[shards:]
    x_ref = refs[0]
    rows = x_ref.shape[0] // peers
    stage = here()[0]

    @pl.when(at_work(stage, step, micro))
    def _():
        if given:

            @pl.when(stage == 0)
            def _():
                order = order_refs[0][...]
                for j, ref in enumerate(input_refs):
                    moved = matmul(order, ref[step]).astype(jnp.bfloat16)
                    x_ref[j * rows : (j + 1) * rows, :] = moved

        if came:

            @pl.when(stage != 0)
            def _():
                for j, blocks in enumerate(row_sets(came_refs, shards, pieces)):
                    x_ref[j * rows : (j + 1) * rows, :] = jnp.concatenate(blocks, axis=0)

        inner = min(patches, 8)
        groups = patches // inner
        xs = [
            regrouped(x_ref[j * rows : (j + 1) * rows, :].astype(jnp.float32), groups, inner)
            for j in range(peers)
        ]
        shape = (rows // groups, rows // groups * peers)
        mine = digits(shape, 0, inner)[0]
        theirs = digits(shape, 1, inner)[0]
        mask = jnp.where(mine == theirs, 1.0, 0.0).astype(jnp.bfloat16)
        normed = [row_norm(x, gain_ref[0]) for x in xs]
        w_in = w_in_ref.at[0, 0]
        q = queries(normed[0], lambda n: scale_ref[0, 0:1, n : n + 1], w_in)
        k, v = keys_and_values(jnp.concatenate(normed, axis=0), w_in)
        update = projected(attention_sums(q, k, v, groups, mask), w_out_ref.at[0, 0])
        y = regrouped(xs[0] + update, rows // (groups * inner), inner).astype(jnp.bfloat16)
        size = rows // shards
        for k in range(shards):
            y_refs[k][...] = y[k * size : (k + 1) * size]


def hour_groups(sizes):
    _, _, patches, hl = sizes
    groups = 2 if hl % 2 == 0 else 1
    return groups, hl // groups * patches


def patch_mask(sizes, fast, others, seen_ref):
    slow, _, patches, hl = sizes
    groups, inner = hour_groups(sizes)
    size = slow * inner
    shape = (size, size * len(others))
    _, my_slow, my_fast = here()

    def block_and_hour(dimension, first):
        patch, late, offset, other = digits(shape, dimension, patches, hl // groups, slow)
        shard = (offset ^ my_slow) * fast + ((other + first) ^ my_fast)
        return (shard * patches + patch) // PB, late

    query_block, query_hour = block_and_hour(0, 0)
    key_block, key_hour = block_and_hour(1, others[0])
    seen = None
    for kv in range(seen_ref.shape[1]):
        chosen = jnp.broadcast_to(seen_ref[0:1, kv : kv + 1], shape)
        for b in range(1, seen_ref.shape[0]):
            chosen = jnp.where(query_block == b, seen_ref[b : b + 1, kv : kv + 1], chosen)
        hit = jnp.where(chosen == key_block, 1.0, 0.0)
        seen = hit if seen is None else jnp.maximum(seen, hit)
    return jnp.where(query_hour == key_hour, seen, 0.0).astype(jnp.bfloat16)


def own_patch_kernel(sizes, fast, step, micro, seen_ref, *refs):
    slow = sizes[0]
    x_refs, (gain_ref, scale_ref, w_in_ref), (q_ref, sums_ref) = (
        refs[:slow],
        refs[slow : slow + 3],
        refs[slow + 3 :],
    )

    @pl.when(at_work(here()[0], step, micro))
    def _():
        groups, inner = hour_groups(sizes)
        x = jnp.concatenate([ref[...] for ref in x_refs], axis=0).astype(jnp.float32)
        normed = row_norm(regrouped(x, groups, inner), gain_ref[1])
        w_in = w_in_ref.at[0, 1]
        q = queries(normed, lambda n: scale_ref[0, 1:2, n : n + 1], w_in)
        k, v = keys_and_values(normed, w_in)
        q_ref[...] = q
        mask = patch_mask(sizes, fast, [0], seen_ref)
        sums = attention_sums(q, k, v, groups, mask)
        sums_ref[...] = jnp.concatenate([jnp.concatenate(t, axis=1) for t in sums], axis=0)


def feed_forward(x, gain, up_ref, down_ref):
    normed = row_norm(x, gain)
    total = x
    chunk = 512
    for start in range(0, up_ref.shape[2], chunk):
        u = matmul(normed, up_ref[0, :, start : start + chunk])
        bent = jnp.tanh(u * (0.7978845608028654 + 0.035677408136300125 * (u * u)))
        hidden = (0.5 * u * (1.0 + bent)).astype(jnp.bfloat16)
        total = total + matmul(hidden, down_ref[0, start : start + chunk, :])
    return total


def write_blocks(y, inner, y_refs):
    y = regrouped(y, len(y_refs), inner).astype(jnp.bfloat16)
    size = y.shape[0] // len(y_refs)
    for k, y_ref in enumerate(y_refs):
        y_ref[...] = y[k * size : (k + 1) * size]


def patch_kernel(sizes, fast, near, step, micro, seen_ref, *refs):
    slow = sizes[0]
    count = fast * slow
    outs = slow - near + (1 if near else 0)
    x_refs, refs, y_refs = refs[:count], refs[count:-outs], refs[-outs:]
    q_ref, sums_ref, gain_ref, w_in_ref, w_out_ref, up_ref, down_ref = refs
    pieces = pieces_of([0] + [k for k in far_first(slow) if k])

    @pl.when(at_work(here()[0], step, micro))
    def _():
        groups, inner = hour_groups(sizes)
        xs = [
            regrouped(jnp.concatenate(blocks, axis=0).astype(jnp.float32), groups, inner)
            for blocks in row_sets(x_refs, slow, pieces)
        ]
        x = xs[0]
        rows, width = x.shape
        normed = jnp.concatenate([row_norm(t, gain_ref[1]) for t in xs[1:]], axis=0)
        k, v = keys_and_values(normed, w_in_ref.at[0, 1])
        mask = patch_mask(sizes, fast, range(1, fast), seen_ref)
        more = attention_sums(q_ref[...], k, v, groups, mask)
        size = rows // groups
        sums = [
            [
                t + sums_ref[g * size : (g + 1) * size, i * 256 : (i + 1) * 256]
                for i, t in enumerate(parts)
            ]
            for g, parts in enumerate(more)
        ]
        x = rounded(x + projected(sums, w_out_ref.at[0, 1]))
        first = near * inner
        if near:
            held = [x[g * size : g * size + first] for g in range(groups)]
            y_refs[0][...] = jnp.concatenate(held, axis=0).astype(jnp.bfloat16)
            x = jnp.concatenate([x[g * size + first : (g + 1) * size] for g in range(groups)], axis=0)
        y = feed_forward(x, gain_ref[2], up_ref, down_ref)
        write_blocks(y, inner, y_refs[1:] if near else y_refs)


def near_kernel(sizes, step, micro, x_ref, gain_ref, up_ref, down_ref, *y_refs):
    @pl.when(at_work(here()[0], step, micro))
    def _():
        x = x_ref[...].astype(jnp.float32)
        inner = hour_groups(sizes)[1]
        write_blocks(feed_forward(x, gain_ref[2], up_ref, down_ref), inner, y_refs)


def write_rows(sizes, x, y_ref):
    slow, _, patches, hl = sizes
    rows = slow * patches * hl
    late, shard, patch = digits((rows, rows), 0, hl, slow)
    source = lax.broadcasted_iota(jnp.int32, (rows, rows), 1)
    wanted = ((shard ^ here()[1]) * hl + late) * patches + patch
    order = jnp.where(wanted == source, 1.0, 0.0).astype(jnp.bfloat16)
    y_ref[...] = matmul(order, x).astype(jnp.bfloat16)


def early_kernel(sizes, pipes, *refs):
    x_refs, y_ref = refs[:pipes], refs[-1]
    for stage, x_ref in enumerate(x_refs):

        @pl.when(here()[0] == stage)
        def _():
            write_rows(sizes, x_ref[...], y_ref)


def final_kernel(sizes, *refs):
    x_refs, y_ref = refs[: sizes[0]], refs[-1]
    write_rows(sizes, jnp.concatenate([ref[...] for ref in x_refs], axis=0), y_ref)


VMEM = pl.BlockSpec(memory_space=pltpu.VMEM)
PARAMS = pltpu.CompilerParams(vmem_limit_bytes=20 << 20)
COST = pl.CostEstimate(flops=5 << 30, bytes_accessed=1 << 20, transcendentals=1 << 20)


def blocks_of(count, rows, width):
    return [jax.ShapeDtypeStruct((rows // count, width), jnp.bfloat16)] * count


def call_order(sizes, rows):
    return pl.pallas_call(
        functools.partial(order_kernel, sizes),
        out_shape=jax.ShapeDtypeStruct((rows, rows), jnp.bfloat16),
        in_specs=[],
        out_specs=VMEM,
        compiler_params=PARAMS,
        cost_estimate=COST,
        name="input_order",
    )()


def call_time(sizes, step, micro, shape, order, given, came, gains, scales, w_in, w_out):
    rows, width = shape
    xs = ([order] if given else []) + list(given) + list(came)
    return pl.pallas_call(
        functools.partial(time_kernel, sizes, step, micro),
        out_shape=blocks_of(sizes[0], rows, width),
        in_specs=[VMEM] * (len(xs) + 4),
        out_specs=[VMEM] * sizes[0],
        scratch_shapes=[pltpu.VMEM((rows * sizes[1], width), jnp.bfloat16)],
        compiler_params=PARAMS,
        cost_estimate=COST,
        name="time_attention",
    )(*xs, gains, scales, w_in, w_out)


def call_own_patch(sizes, fast, step, micro, shape, seen, xs, gains, scales, w_in):
    rows, width = shape
    return pl.pallas_call(
        functools.partial(own_patch_kernel, sizes, fast, step, micro),
        out_shape=[
            jax.ShapeDtypeStruct((rows, width), jnp.bfloat16),
            jax.ShapeDtypeStruct((rows, 2 * width), jnp.float32),
        ],
        in_specs=[VMEM] * (len(xs) + 4),
        out_specs=[VMEM, VMEM],
        compiler_params=PARAMS,
        cost_estimate=COST,
        name="own_patch_attention",
    )(seen, *xs, gains, scales, w_in)


def call_patch(sizes, fast, near, step, micro, shape, seen, xs, weights):
    rows, width = shape
    slow = sizes[0]
    blocks = blocks_of(slow, rows, width)
    outs = blocks[near:]
    if near:
        outs = [jax.ShapeDtypeStruct((rows // slow * near, width), jnp.bfloat16)] + outs
    outs = pl.pallas_call(
        functools.partial(patch_kernel, sizes, fast, near, step, micro),
        out_shape=outs,
        in_specs=[VMEM] * (1 + len(xs) + len(weights)),
        out_specs=[VMEM] * len(outs),
        compiler_params=PARAMS,
        cost_estimate=COST,
        name="patch_attention_and_ffn",
    )(seen, *xs, *weights)
    if not near:
        return list(outs)
    gains, _, _, w_up, w_down = weights[-5:]
    near_blocks = pl.pallas_call(
        functools.partial(near_kernel, sizes, step, micro),
        out_shape=blocks[:near],
        in_specs=[VMEM] * 4,
        out_specs=[VMEM] * near,
        compiler_params=PARAMS,
        cost_estimate=COST,
        name="near_ffn",
    )(outs[0], gains, w_up, w_down)
    return list(near_blocks) + list(outs[1:])


def call_write(kernel, sizes, shape, number, xs, out):
    given = [] if out is None else [out]
    return pl.pallas_call(
        kernel,
        out_shape=jax.ShapeDtypeStruct(shape, jnp.bfloat16),
        grid=(1,),
        in_specs=[VMEM] * len(xs) + [pl.BlockSpec(memory_space=pl.ANY)] * len(given),
        out_specs=pl.BlockSpec((None,) + shape[1:], lambda i: (number, 0, 0)),
        input_output_aliases={len(xs): 0} if given else {},
        compiler_params=PARAMS,
        name="final_order",
    )(*xs, *given)


def flipped(x, axis, k):
    return lax.ppermute(x, axis, [(s, s ^ k) for s in range(lax.axis_size(axis))])


def handed_on(x, k):
    pipes, shards = lax.axis_size("pipe"), lax.axis_size("patch")
    pairs = [
        (stage * shards + s, (stage + 1) % pipes * shards + (s ^ k))
        for stage in range(pipes)
        for s in range(shards)
    ]
    return lax.ppermute(x, ("pipe", "patch"), pairs)


def local(inputs, seen, gains, scales, w_in, w_out, w_up, w_down):
    shards = lax.axis_size("patch")
    peers = lax.axis_size("hour")
    pipes = lax.axis_size("pipe")
    micro, patches, hours, width = inputs.shape
    rows = patches * hours
    fast = FAST
    slow = shards // fast
    sizes = (slow, peers, patches, hours // slow)
    last = pipes - 1
    gains = gains.reshape(gains.shape[1], 1, width)
    far = far_first(slow)
    order = call_order(sizes, rows)

    def gathered(blocks, axis, count, sequence):
        own = [jnp.concatenate([blocks[k] for k in piece]) for piece in pieces_of(sequence)]
        out = list(own)
        for j in range(1, count):
            out += [flipped(piece, axis, j) for piece in own]
        return out

    def along_slow(blocks, send, first):
        got = {k: send(blocks[k], k * fast) for k in far if k >= first}
        return [got.get(k, blocks[k]) for k in range(slow)]

    def in_stage(x, k):
        return flipped(x, "patch", k)

    def onward(x):
        return lax.ppermute(x, "pipe", [(s, (s + 1) % pipes) for s in range(pipes)])

    x = inputs.reshape(micro, rows, width)
    given = [x] + [flipped(x, "hour", j) for j in range(1, peers)]
    came = []
    out = None
    back = []
    for step in range(micro + pipes - 1):
        now = given if step < micro else []
        mixed = call_time(
            sizes, step, micro, x.shape[1:], order, now, came, gains, scales, w_in, w_out
        )
        own = along_slow(mixed, in_stage, 1)
        spread = gathered(own, "patch", fast, [0] + [k for k in far if k])
        begun = call_own_patch(
            sizes, fast, step, micro, x.shape[1:], seen, own, gains, scales, w_in
        )
        if back:
            spread, back = lax.optimization_barrier((spread, back))
            write = functools.partial(early_kernel, sizes, pipes)
            out = call_write(write, sizes, x.shape, step - pipes, back, out)
        at_end = step == micro + pipes - 2
        weights = [*begun, gains, w_in, w_out, w_up, w_down]
        near = slow // 2 if at_end else 0
        done = call_patch(sizes, fast, near, step, micro, x.shape[1:], seen, spread, weights)
        if not at_end:
            arrived = along_slow(done, handed_on, 0)
            came = gathered(arrived, "hour", peers, far)
            if step >= last:
                back = [jnp.concatenate(arrived)]
                for _ in range(1, pipes):
                    back.append(onward(back[-1]))
    stage = lax.axis_index("pipe")
    blocks = {}
    for k in far:
        chosen = block = done[k]
        for hop in range(pipes - 1):
            block = onward(block)
            chosen = jnp.where(stage == hop, block, chosen)
        blocks[k] = chosen
    blocks = {k: in_stage(blocks[k], k * fast) if k else blocks[k] for k in far}
    blocks = [blocks[k] for k in range(slow)]
    write = functools.partial(final_kernel, sizes)
    out = call_write(write, sizes, x.shape, micro - 1, blocks, out)
    return out.reshape(inputs.shape)


def solution(mesh):
    placed = (
        P(None, "patch", "hour", None),
        P(),
        P("pipe", None, None),
        P("pipe", None, None),
        P("pipe", None, None, None),
        P("pipe", None, None, None),
        P("pipe", None, None),
        P("pipe", None, None),
    )
    return jax.shard_map(
        local, mesh=mesh, in_specs=placed, out_specs=P(None, "patch", "hour", None), check_vma=False
    )
```
